128 devices in a mesh: dp: 32 (over x, y, core), tensor: 4 (over z).
Axes of the slice: x: 4, y: 4, z: 4, core: 2. Of those that a mesh axis runs over, the one named last changes fastest.
Arguments:
- inputs: bfloat16 [16384, 1024], P(('dp', 'tensor')), may hold values from -6 to 6
- lengths: int32 [32], replicated, may hold values from 1 to 16, 128 in all
- w_qkv: bfloat16 [1, 1024, 3, 1024], P(None, 'dp', None, 'tensor'), may hold values from -0.1875 to 0.1875
- w_out: bfloat16 [1, 1024, 1024], P(None, 'tensor', 'dp'), may hold values from -0.75 to 0.75
- w_fc: bfloat16 [1, 1024, 4096], P(None, 'dp', 'tensor'), may hold values from -0.1875 to 0.1875
- w_proj: bfloat16 [1, 4096, 1024], P(None, 'tensor', 'dp'), may hold values from -0.09375 to 0.09375
- b_qv: bfloat16 [1, 2, 1024], P(None, None, ('tensor', 'dp')), may hold values from -3 to 3
- b_fc: bfloat16 [1, 4096], P(None, ('tensor', 'dp')), may hold values from -3 to 3
- gains: float32 [1, 2, 1024], P(None, None, ('dp', 'tensor')), may hold values from 0.5 to 1.5
- shifts: float32 [1, 4, 1024], P(None, None, ('dp', 'tensor')), may hold values from -2 to 2
- cotangent: bfloat16 [16384, 1024], P(('dp', 'tensor')), may hold values from -24 to 24
Outputs:
- outputs: float32 [16384, 1024], P(('dp', 'tensor'))
- grad_inputs: float32 [16384, 1024], P(('dp', 'tensor'))
- grad_w_qkv: float32 [1, 1024, 3, 1024], P(None, 'dp', None, 'tensor')
- grad_w_out: float32 [1, 1024, 1024], P(None, 'tensor', 'dp')
- grad_w_fc: float32 [1, 1024, 4096], P(None, 'dp', 'tensor')
- grad_w_proj: float32 [1, 4096, 1024], P(None, 'tensor', 'dp')
- grad_b_qv: float32 [1, 2, 1024], P(None, None, ('tensor', 'dp'))
- grad_b_fc: float32 [1, 4096], P(None, ('tensor', 'dp'))
- grad_gains: float32 [1, 2, 1024], P(None, None, ('dp', 'tensor'))
- grad_shifts: float32 [1, 4, 1024], P(None, None, ('dp', 'tensor'))
The draws below stay inside these ranges and needn't reach their ends.
Inputs may be any that keep to these rules, and one draw needn't show every extreme that they name: lengths counts blocks of 128 tokens; the lengths sum to 128 and the longest is exactly 16.
All inputs are finite; a program needn't handle non-finite values.
Results may differ from the reference program's by a relative error of at most 0.012.
Values may be sent and summed in bfloat16 or wider, within the bound.
A program may use at most 192 MiB of HBM per device.

```python
import math
import jax
import jax.numpy as jnp
import numpy as np
from jax import lax

D = 1024
HEADS = 16
HEAD_DIM = 64
FF = 4096
LAYERS = 1
BLOCK = 128
MAXB = 16
NBLK = 128
TOKENS = 16384
NSEQ = 32


def raised(result, rng, source, target, blocks, factor):
    owner, partner = [(jnp.arange(result.shape[axis_at]) // (result.shape[axis_at] // blocks)).reshape([-1 if axis == axis_at else 1 for axis in range(result.ndim)]) for axis_at in (source, target)]
    chosen = jax.random.permutation(rng, blocks)[partner]
    strong = (owner == chosen) | (owner == (partner + blocks // 2) % blocks)
    return jnp.where(strong, factor * result, result)


def shard_levels(own_key, dims, shards, least, high):
    def one(dim, shards_of):
        heights = jax.random.uniform(jax.random.fold_in(jax.random.fold_in(own_key, 6), dim), (shards_of,), jnp.float32, least / len(shards), high / len(shards))
        return jnp.repeat(jnp.exp(heights), dims[dim] // shards_of).reshape((-1,) + (1,) * (len(dims) - dim - 1))

    loudness = one(*shards[0])
    for cut in shards[1:]:
        loudness = loudness * one(*cut)
    return loudness


def split_up(count, total, bound, skew):
    weights = [(1 << 20) // math.isqrt(grade ** skew) + 1 for grade in range(2, count + 1)]
    spare, counts = total - bound - (count - 1), [1] * (count - 1)
    while spare > 0:
        candidates = [i for i in range(count - 1) if counts[i] < bound]
        mass, remaining = sum([weights[i] for i in candidates]), spare
        for i in candidates:
            more = min(bound - counts[i], max(1, remaining * weights[i] // mass), spare)
            counts[i] = counts[i] + more
            spare = spare - more
    return np.array([bound] + counts)


def uneven_parts(own_key, count, total, reach, lean):
    if count == 2:
        one = jax.random.randint(own_key, (), max(1, total - reach), min(reach, total - 1) + 1)
        return jnp.stack([one, total - one])
    tallies = jnp.asarray(split_up(count, total, reach, lean), jnp.int32)
    couples = (count - 1) // 2
    donor, receiver = tallies[1:1 + 2 * couples:2], tallies[2:2 + 2 * couples:2]
    room = jnp.minimum(donor - 1, reach - receiver)
    moved = jax.random.randint(jax.random.fold_in(own_key, 1), (couples,), 0, 1 << 20) % (room + 1)
    tallies = tallies.at[1:1 + 2 * couples:2].set(donor - moved).at[2:2 + 2 * couples:2].set(receiver + moved)
    return tallies[jax.random.permutation(jax.random.fold_in(own_key, 2), count)]


def normal_values(rng, dims, width, limit, shards=(), kind=jnp.bfloat16):
    values = width * jax.random.normal(rng, dims, jnp.float32)
    if shards:
        values = values * shard_levels(rng, dims, shards, -0.22, 0.18)
    return jnp.clip(values, -limit, limit).astype(kind)


def noise_with(own_key, dims, scale, most, split, heavy, held_as=jnp.bfloat16):
    array = scale * jax.random.normal(own_key, dims, jnp.float32)
    if split:
        array = array * shard_levels(own_key, dims, split, -0.22, 0.18)
    return jnp.clip(raised(array, jax.random.fold_in(own_key, 3), *heavy), -most, most).astype(held_as)


def setup_inputs(seed: int = 0) -> dict:
    key_of = jax.random.split(jax.random.key(seed), 12)
    inputs = normal_values(key_of[0], (TOKENS, D), 1.0, 6.0, ((0, 128),))
    lengths = uneven_parts(key_of[1], NSEQ, NBLK, MAXB, 2).astype(jnp.int32)
    w_qkv = normal_values(key_of[2], (LAYERS, D, 3, D), D ** -0.5, 0.1875, ((1, 32), (3, 4)))
    w_out = normal_values(key_of[3], (LAYERS, D, D), (D // 16) ** -0.5, 0.75, ((1, 4), (2, 32)))
    w_fc = normal_values(key_of[4], (LAYERS, D, FF), D ** -0.5, 0.1875, ((1, 32), (2, 4)))
    w_proj = normal_values(key_of[5], (LAYERS, FF, D), FF ** -0.5, 0.09375, ((1, 4), (2, 32)))
    b_qv = normal_values(key_of[6], (LAYERS, 2, D), 0.5, 3.0, ((2, 128),))
    b_fc = normal_values(key_of[7], (LAYERS, FF), 0.5, 3.0, ((1, 128),))
    gains = jnp.clip(1.0 + 0.1 * jax.random.normal(key_of[8], (LAYERS, 2, D), jnp.float32), 0.5, 1.5)
    shifts = normal_values(key_of[9], (LAYERS, 4, D), 0.3, 2.0, ((2, 128),), jnp.float32)
    cotangent = noise_with(key_of[10], (TOKENS, D), 1.0, 24.0, ((0, 128),), (0, 1, 128, 5.5))
    return dict(inputs=inputs, lengths=lengths, w_qkv=w_qkv, w_out=w_out, w_fc=w_fc, w_proj=w_proj, b_qv=b_qv, b_fc=b_fc, gains=gains, shifts=shifts, cotangent=cotangent)


@jax.custom_vjp
def low(v):
    return lax.optimization_barrier(v.astype(jnp.bfloat16)).astype(jnp.float32)

@jax.custom_vjp
def low_back(v):
    return v

def low_keep(v):
    return (low(v), None)

def low_pass(kept, grad):
    return (grad,)

def back_keep(v):
    return (v, None)

def back_low(kept, grad):
    return (low(grad),)
low.defvjp(low_keep, low_pass)
low_back.defvjp(back_keep, back_low)

def matmul(left_side, right_side):
    return jnp.dot(left_side, right_side, precision=lax.Precision.HIGHEST, preferred_element_type=jnp.float32)

def layer_norm(values, gain_row, shift_row):
    centre = values - lax.optimization_barrier(jnp.mean(values, axis=-1, keepdims=True))
    spread = lax.optimization_barrier(jnp.mean(centre * centre, axis=-1, keepdims=True))
    return centre * lax.rsqrt(spread + 1e-05) * gain_row + shift_row

def gelu_tanh(values):
    return 0.5 * values * (1.0 + jnp.tanh(0.7978845608028654 * (values + 0.044715 * values * values * values)))

def sequence_of(lengths, positions):
    bounds = jnp.cumsum(lengths) * BLOCK
    found_seq = lax.optimization_barrier(jnp.sum((positions[:, None] >= bounds[None, :]).astype(jnp.int32), axis=1))
    return jnp.where(positions >= 0, found_seq, -1).astype(jnp.int32)

def attention(mixed, seq_ids):
    window = MAXB * BLOCK
    query_rows = 4 * BLOCK
    score_scale = HEAD_DIM ** (-0.5)
    queries = mixed[:, 0].reshape(TOKENS, HEADS, HEAD_DIM)
    padding = ((window, 0), (0, 0), (0, 0))
    key_rows = jnp.pad(mixed[:, 1].reshape(TOKENS, HEADS, HEAD_DIM), padding)
    value_rows = jnp.pad(mixed[:, 2].reshape(TOKENS, HEADS, HEAD_DIM), padding)
    key_seq = jnp.concatenate([jnp.full((window,), -1, jnp.int32), seq_ids])

    def one_block(block_start):
        query_block = lax.dynamic_slice_in_dim(queries, block_start, query_rows, 0)
        key_block = lax.dynamic_slice_in_dim(key_rows, block_start, window + query_rows, 0)
        value_block = lax.dynamic_slice_in_dim(value_rows, block_start, window + query_rows, 0)
        query_seq = lax.dynamic_slice_in_dim(seq_ids, block_start, query_rows, 0)
        block_keys_seq = lax.dynamic_slice_in_dim(key_seq, block_start, window + query_rows, 0)
        query_pos = block_start + jnp.arange(query_rows, dtype=jnp.int32)
        key_pos = block_start - window + jnp.arange(window + query_rows, dtype=jnp.int32)
        allowed = (query_seq[:, None] == block_keys_seq[None, :]) & (key_pos[None, :] <= query_pos[:, None])
        scores = jnp.einsum('qhd,khd->hqk', query_block, key_block, precision=lax.Precision.HIGHEST)
        scores = low_back(scores * score_scale)
        scores = jnp.where(allowed[None], scores, -1e+30)
        row_peak = lax.optimization_barrier(jnp.max(scores, axis=-1, keepdims=True))
        exp_scores = jnp.exp(scores - row_peak)
        soft_weights = exp_scores / lax.optimization_barrier(jnp.sum(exp_scores, axis=-1, keepdims=True))
        return jnp.einsum('hqk,khd->qhd', low(soft_weights), value_block, precision=lax.Precision.HIGHEST)
    starts = jnp.arange(TOKENS // query_rows, dtype=jnp.int32) * query_rows
    blocks = lax.map(jax.checkpoint(one_block), starts)
    return blocks.reshape(TOKENS, D)

def block_forward(residual, weight_qkv, weight_out, weight_fc, weight_proj, bias_qv, bias_fc, gain_rows, shift_rows, seq_ids):
    normed_one = low(layer_norm(residual, gain_rows[0], shift_rows[0]))
    mixed = matmul(normed_one, weight_qkv.reshape(D, 3 * D)).reshape(TOKENS, 3, D)
    bias_full = jnp.stack([bias_qv[0], jnp.zeros_like(bias_qv[0]), bias_qv[1]])
    mixed = low_back(low(mixed + bias_full))
    context = low_back(low(attention(mixed, seq_ids)))
    after = residual + low_back(matmul(context, weight_out)) + shift_rows[2]
    normed_two = low(layer_norm(after, gain_rows[1], shift_rows[1]))
    pre_act = low_back(matmul(normed_two, weight_fc) + bias_fc)
    act_low = low(gelu_tanh(pre_act))
    return after + low_back(matmul(act_low, weight_proj)) + shift_rows[3]

def reference(inputs, lengths, w_qkv, w_out, w_fc, w_proj, b_qv, b_fc, gains, shifts, cotangent):
    seq_ids = sequence_of(lengths, jnp.arange(TOKENS, dtype=jnp.int32))

    def forward(residual, weight_qkv, weight_out, weight_fc, weight_proj, bias_qv, bias_fc, gain_all, shift_all):
        for layer_index in range(LAYERS):
            residual = block_forward(residual, weight_qkv[layer_index], weight_out[layer_index], weight_fc[layer_index], weight_proj[layer_index], bias_qv[layer_index], bias_fc[layer_index], gain_all[layer_index], shift_all[layer_index], seq_ids)
        return residual
    outputs, pullback = jax.vjp(forward, inputs.astype(jnp.float32), w_qkv.astype(jnp.float32), w_out.astype(jnp.float32), w_fc.astype(jnp.float32), w_proj.astype(jnp.float32), b_qv.astype(jnp.float32), b_fc.astype(jnp.float32), gains.astype(jnp.float32), shifts.astype(jnp.float32))
    grads = pullback(cotangent.astype(jnp.float32))
    return (outputs, grads[0], grads[1], grads[2], grads[3], grads[4], grads[5], grads[6], grads[7], grads[8])
```

```python
import functools

import jax
import jax.numpy as jnp
from jax import lax
from jax.experimental import pallas as pl
from jax.experimental.pallas import tpu as pltpu
from jax.sharding import PartitionSpec as P

HEAD_DIM = 64
BLOCK = 128
D = 1024
GROUP = 512
BF = jnp.bfloat16
F32 = jnp.float32
MESH = pl.DeviceIdType.MESH
VMEM_LIMIT = 58 * 1024 * 1024


def nn(a, b):
    return jnp.dot(a, b, preferred_element_type=F32)


def nt(a, b):
    return lax.dot_general(a, b, (((1,), (1,)), ((), ())), preferred_element_type=F32)


def tn(a, b):
    return lax.dot_general(a, b, (((0,), (0,)), ((), ())), preferred_element_type=F32)


def rows(start, size, step=None):
    return pl.ds(pl.multiple_of(start, step or size), size)


class Place:
    def __init__(self):
        self.dp = lax.axis_index("dp")
        self.z = lax.axis_index("tensor")
        self.c = lax.rem(self.dp, 2)
        self.chip = self.dp // 2
        self.y = lax.rem(self.chip, 4)
        self.x = self.chip // 4

    def at(self, dx=0, dy=0, dz=0, flip=False):
        x = lax.rem(self.x + dx + 4, 4)
        y = lax.rem(self.y + dy + 4, 4)
        c = 1 - self.c if flip else self.c
        return ((x * 4 + y) * 2 + c, lax.rem(self.z + dz + 4, 4))

    def linear(self, step):
        return (lax.rem(self.chip + step + 16, 16) * 2 + self.c, self.z)


class Copies:
    def __init__(self, send_sem, recv_sem):
        self.send_sem, self.recv_sem = send_sem, recv_sem
        self.started = []

    def put(self, src, dst, device):
        k = len(self.started)
        copy = pltpu.make_async_remote_copy(
            src_ref=src,
            dst_ref=dst,
            send_sem=self.send_sem.at[k],
            recv_sem=self.recv_sem.at[k],
            device_id=device,
            device_id_type=MESH,
        )
        copy.start()
        self.started.append(copy)
        return copy

    def finish(self):
        for copy in self.started:
            copy.wait_send()


def greet(devices):
    barrier = pltpu.get_barrier_semaphore()
    for device in devices:
        pl.semaphore_signal(barrier, inc=1, device_id=device, device_id_type=MESH)
    pl.semaphore_wait(barrier, len(devices))


class RingGather:
    def __init__(self, copies, place, buf, size=BLOCK):
        self.copies, self.place, self.buf, self.size = copies, place, buf, size

    def block(self, dz, part=None):
        start = lax.rem(self.place.z + dz + 4, 4) * self.size
        if part is None:
            return self.buf.at[rows(start, self.size)]
        half = self.size // 2
        return self.buf.at[rows(start + part * half, half)]

    def start(self):
        own = self.block(0)
        self.up = self.copies.put(own, own, self.place.at(dz=1))
        self.down = self.copies.put(own, own, self.place.at(dz=-1))

    def below(self):
        self.up.wait_recv()
        half = self.block(-1, 0)
        self.up2 = self.copies.put(half, half, self.place.at(dz=1))

    def above(self):
        self.down.wait_recv()
        half = self.block(1, 1)
        self.down2 = self.copies.put(half, half, self.place.at(dz=-1))

    def far(self):
        self.up2.wait_recv()
        self.down2.wait_recv()


class PlaneGather:
    def __init__(self, copies, place, w, first, width):
        self.copies, self.place, self.w = copies, place, w
        c = place.c
        self.first, self.width = first, width
        self.cols = pl.ds(pl.multiple_of(first + c * (width // 2), 128), width // 2)
        self.near = 1 - c, c

    def dev(self, axis, step):
        c = self.place.c
        if axis == 0:
            return self.place.at(dx=c * step, dy=(1 - c) * step)
        return self.place.at(dx=(1 - c) * step, dy=c * step)

    def block(self, first_off, second_off, part=None):
        p, c = self.place, self.place.c
        a = lax.rem(p.y * (1 - c) + p.x * c + first_off + 4, 4)
        b = lax.rem(p.x * (1 - c) + p.y * c + second_off + 4, 4)
        x = b * (1 - c) + a * c
        y = a * (1 - c) + b * c
        start = (x * 4 + y) * 64
        if part is None:
            return self.w.at[rows(start, 64), self.cols]
        return self.w.at[rows(start + 32 * part, 32), self.cols]

    def put(self, ref, device):
        return self.copies.put(ref, ref, device)

    def start(self):
        p = self.place
        mine = self.w.at[rows(p.dp * 32, 32), pl.ds(self.first, self.width)]
        self.swap = self.put(mine, p.at(flip=True))

    def spread(self, first_off):
        ref = self.block(first_off, 0)
        return (self.put(ref, self.dev(1, 1)), self.put(ref, self.dev(1, -1)))

    def share(self, first_off, second_off):
        self.shared.append(self.put(self.block(first_off, second_off), self.place.at(flip=True)))

    def step1(self):
        self.swap.wait_recv()
        ref = self.block(0, 0)
        self.shared = []
        self.up = self.put(ref, self.dev(0, 1))
        self.down = self.put(ref, self.dev(0, -1))
        self.out = {0: self.spread(0)}

    def step2(self):
        self.up.wait_recv()
        self.up2 = self.put(self.block(-1, 0, 0), self.dev(0, 1))
        self.down.wait_recv()
        self.down2 = self.put(self.block(1, 0, 1), self.dev(0, -1))
        self.out[-1] = self.spread(-1)
        self.out[1] = self.spread(1)
        self.share(-1, 0)
        self.share(1, 0)

    def step3(self):
        self.up2.wait_recv()
        self.down2.wait_recv()
        self.out[2] = self.spread(2)
        self.share(2, 0)

    def step4(self):
        self.far = []
        for first_off in (0, -1, 1, 2):
            up, down = self.out[first_off]
            up.wait_recv()
            self.far.append(self.put(self.block(first_off, -1, 0), self.dev(1, 1)))
            down.wait_recv()
            self.far.append(self.put(self.block(first_off, 1, 1), self.dev(1, -1)))
            self.share(first_off, -1)
            self.share(first_off, 1)

    def step5(self):
        for k, first_off in enumerate((0, -1, 1, 2)):
            self.far[2 * k].wait_recv()
            self.far[2 * k + 1].wait_recv()
            self.share(first_off, 2)

    def step6(self):
        for copy in self.shared:
            copy.wait_recv()


def normalised(values):
    centre = values - jnp.mean(values, axis=-1, keepdims=True)
    spread = jnp.mean(centre * centre, axis=-1, keepdims=True)
    scale = lax.rsqrt(spread + 1e-05)
    return centre * scale, scale


def first_kernel(
    x_ref, cot_ref, shard_ref, small_ref,
    n1_ref, q_ref, kv_ref, cotg_ref, w_ref, vec_ref, bqv_ref,
    xg, vz, vall, send_sem, recv_sem,
):
    p = Place()
    greet(
        [p.at(dz=1), p.at(dz=-1), p.at(dz=2), p.at(dx=1), p.at(dx=-1), p.at(dx=2),
         p.at(dy=1), p.at(dy=-1), p.at(dy=2), p.at(flip=True), p.linear(1), p.linear(-1)]
    )
    copies = Copies(send_sem, recv_sem)
    w_ref[rows(p.dp * 32, 32), :] = shard_ref[...]
    head = PlaneGather(copies, p, w_ref, 0, 768)
    head.start()
    small = []
    vz[p.z] = small_ref[0:8]
    for dz in (1, -1, 2):
        small.append(copies.put(vz.at[p.z], vz.at[p.z], p.at(dz=dz)))
    xg[rows(p.z * BLOCK, BLOCK), :] = x_ref[...]
    ring = RingGather(copies, p, xg)
    ring.start()
    head.step1()
    for copy in small:
        copy.wait_recv()
    vall[p.c, p.chip, 0:8] = vz[0] + vz[1] + vz[2] + vz[3]
    vall[p.c, p.chip, 8:16] = small_ref[8:16]
    mine = vall.at[p.c, p.chip]
    small = [copies.put(mine, mine, p.at(dy=dy)) for dy in (1, -1, 2)]
    ring.below()
    ring.above()
    head.step2()
    tail = PlaneGather(copies, p, w_ref, 768, 2304)
    tail.start()
    for copy in small:
        copy.wait_recv()
    mine = vall.at[p.c, rows(p.x * 4, 4)]
    small = [copies.put(mine, mine, p.at(dx=dx)) for dx in (1, -1, 2)]
    head.step3()
    cotg_ref[rows(p.z * BLOCK, BLOCK), :] = cot_ref[...]
    cot_ring = RingGather(copies, p, cotg_ref)
    cot_ring.start()
    for copy in small:
        copy.wait_recv()
    mine = vall.at[p.c]
    last = copies.put(mine, mine, p.at(flip=True))
    head.step4()
    tail.step1()
    ring.far()
    last.wait_recv()
    lanes = []
    for k in range(8):
        total = vall[0, 2 * k] + vall[0, 2 * k + 1] + vall[1, 2 * k] + vall[1, 2 * k + 1]
        vec_ref[:, k * 128:(k + 1) * 128] = total
        lanes.append(total)
    for h in range(2):
        bqv_ref[:, h * 128:(h + 1) * 128] = lanes[4 * h] + lanes[4 * h + 1] + lanes[4 * h + 2] + lanes[4 * h + 3]

    def norm_block(k, carry):
        block = rows(lax.rem(p.z + k, 4) * BLOCK, BLOCK)
        hat, _ = normalised(xg[block, :].astype(F32))
        n1_ref[block, :] = (hat * vec_ref[0:1, :] + vec_ref[2:3, :]).astype(BF)
        return carry

    lax.fori_loop(0, 4, norm_block, 0)
    head.step5()
    tail.step2()
    head.step6()
    tail.step3()
    tail.step4()
    halo = []
    for k in range(4):
        start = lax.rem(p.z + k, 4) * BLOCK
        block = rows(start, BLOCK)
        values = n1_ref[block, :]
        q_ref[block, :] = (nn(values, w_ref[:, 0:256]) + bqv_ref[9:10, :]).astype(BF)
        mine = rows(4 * GROUP + start, BLOCK)
        kv_ref[mine, 0:256] = nn(values, w_ref[:, 256:512]).astype(BF)
        kv_ref[mine, 256:512] = (nn(values, w_ref[:, 512:768]) + bqv_ref[10:11, :]).astype(BF)
        halo.append(
            copies.put(kv_ref.at[mine], kv_ref.at[rows(2 * GROUP + start, BLOCK)], p.linear(1))
        )
    tail.step5()
    cot_ring.below()
    cot_ring.above()
    relay, cross = [], []
    sibling = p.at(flip=True)
    for k in range(4):
        start = lax.rem(p.z + k, 4) * BLOCK
        halo[k].wait_recv()
        near = kv_ref.at[rows(2 * GROUP + start, BLOCK)]
        relay.append(copies.put(near, kv_ref.at[rows(start, BLOCK)], p.linear(1)))
        cross.append(
            copies.put(near, kv_ref.at[rows((1 + 2 * p.c) * GROUP + start, BLOCK)], sibling)
        )
    cot_ring.far()
    for k in range(4):
        start = lax.rem(p.z + k, 4) * BLOCK
        relay[k].wait_recv()
        cross.append(
            copies.put(
                kv_ref.at[rows((4 - 4 * p.c) * GROUP + start, BLOCK)],
                kv_ref.at[rows((3 - 2 * p.c) * GROUP + start, BLOCK)],
                sibling,
            )
        )
    for copy in cross:
        copy.wait_recv()
    tail.step6()
    copies.finish()


N1_COPIES = 2 * 36 + 4 + 4 + 3 + 3 + 3 + 1 + 16


def vm(count):
    return [pl.BlockSpec(memory_space=pltpu.VMEM)] * count


def call_first(x, cot, shard, small):
    return pl.pallas_call(
        first_kernel,
        out_shape=(
            jax.ShapeDtypeStruct((GROUP, D), BF),
            jax.ShapeDtypeStruct((GROUP, 256), BF),
            jax.ShapeDtypeStruct((5 * GROUP, 512), BF),
            jax.ShapeDtypeStruct((GROUP, D), BF),
            jax.ShapeDtypeStruct((D, 3072), BF),
            jax.ShapeDtypeStruct((16, D), F32),
            jax.ShapeDtypeStruct((16, 256), F32),
        ),
        in_specs=vm(4),
        out_specs=tuple(vm(7)),
        scratch_shapes=[
            pltpu.VMEM((GROUP, D), BF),
            pltpu.VMEM((4, 8, 128), F32),
            pltpu.VMEM((2, 16, 16, 128), F32),
            pltpu.SemaphoreType.DMA((N1_COPIES,)),
            pltpu.SemaphoreType.DMA((N1_COPIES,)),
        ],
        compiler_params=pltpu.CompilerParams(
            collective_id=1, has_side_effects=True, vmem_limit_bytes=VMEM_LIMIT
        ),
        name="gather_and_project",
    )(x, cot, shard, small)


def pack_small(gains, shifts, b_qv, b_fc):
    dp, z = lax.axis_index("dp"), lax.axis_index("tensor")
    lane = jnp.arange(128, dtype=jnp.int32)[None, :]
    eight = jnp.concatenate([gains, shifts, jnp.zeros((2, 8), F32)], axis=0)
    top = jnp.where(lane // 8 == lax.rem(dp * 4 + z, 16), jnp.tile(eight, (1, 16)), 0.0)
    fc = jnp.where(lane // 32 == lax.rem(dp, 4), jnp.tile(b_fc[None].astype(F32), (1, 4)), 0.0)
    qv = jnp.where(lane // 8 == lax.rem(dp, 16), jnp.tile(b_qv.astype(F32), (1, 16)), 0.0)
    return jnp.concatenate([top, fc, qv, jnp.zeros((5, 128), F32)], axis=0)


def pack_weights(w_qkv, w_out, w_fc, w_proj):
    return jnp.concatenate(
        [w_qkv[0].reshape(32, 768), w_out[0].T, w_fc[0], w_proj[0].T], axis=1
    )


SPAN = 4


def from_behind(value, axis, steps):
    count = lax.axis_size(axis)
    first, last = (max(0, -steps), min(count, count - steps))
    return lax.ppermute(value, axis, [(source, source + steps) for source in range(first, last)])


def layer_norm(values, gain_row, shift_row):
    centre = values - jnp.mean(values, axis=-1, keepdims=True)
    spread = jnp.mean(centre * centre, axis=-1, keepdims=True)
    return centre * lax.rsqrt(spread + 1e-05) * gain_row + shift_row


def gelu_tanh(values):
    return (
        0.5
        * values
        * (1.0 + jnp.tanh(0.7978845608028654 * (values + 0.044715 * values * values * values)))
    )


def sequence_of(lengths, positions):
    bounds = jnp.cumsum(lengths) * BLOCK
    found_seq = jnp.sum((positions[:, None] >= bounds[None, :]).astype(jnp.int32), axis=1)
    return jnp.where(positions >= 0, found_seq, -1)


def contract_rows(left_side, right_side):
    return lax.dot_general(
        left_side, right_side, (((0,), (0,)), ((), ())), preferred_element_type=jnp.float32
    )


def contract_cols(left_side, right_side):
    return lax.dot_general(
        left_side, right_side, (((1,), (1,)), ((), ())), preferred_element_type=jnp.float32
    )


def gather_rows(normed):
    return lax.all_gather(normed.astype(jnp.bfloat16), "tensor", axis=0, tiled=True)


def gather_grads(gradient):
    return lax.all_gather(gradient.astype(jnp.bfloat16), "tensor", axis=0, tiled=True)


def tensor_sum(left_side, right_side):
    row_count = left_side.shape[0] // lax.axis_size("tensor")

    def partial_value(start_row, row_num):
        return jnp.dot(left_side, right_side, preferred_element_type=jnp.float32)

    return lax.psum_scatter(
        partial_value(jnp.int32(0), row_count * lax.axis_size("tensor")),
        "tensor",
        scatter_dimension=0,
        tiled=True,
    )


def tensor_back(left_side, right_side):
    row_count = left_side.shape[0] // lax.axis_size("tensor")

    def partial_value(start_row, row_num):
        return contract_cols(left_side, right_side)

    return lax.psum_scatter(
        partial_value(jnp.int32(0), row_count * lax.axis_size("tensor")),
        "tensor",
        scatter_dimension=0,
        tiled=True,
    )


def split_heads(qkv_low, key_set):
    heads_local = qkv_low.shape[2] // HEAD_DIM
    queries = qkv_low[:, 0].reshape(qkv_low.shape[0], heads_local, HEAD_DIM)
    key_rows = key_set[:, 0].reshape(key_set.shape[0], heads_local, HEAD_DIM)
    value_rows = key_set[:, 1].reshape(key_set.shape[0], heads_local, HEAD_DIM)
    return (queries, key_rows, value_rows)


def attend_forward(qkv_low, key_set, allowed):
    queries, key_rows, value_rows = split_heads(qkv_low, key_set)
    scores = jnp.einsum(
        "qhd,khd->hqk", queries, key_rows, preferred_element_type=jnp.float32
    ) * HEAD_DIM ** (-0.5)
    masked = jnp.where(allowed[None], scores, -1e30)
    row_peak = jnp.max(masked, axis=-1, keepdims=True)
    exp_scores = jnp.exp(masked - row_peak)
    row_total = jnp.sum(exp_scores, axis=-1, keepdims=True)
    soft_weights = (exp_scores / row_total).astype(jnp.bfloat16)
    context = jnp.einsum(
        "hqk,khd->qhd", soft_weights, value_rows, preferred_element_type=jnp.float32
    )
    return (
        context.reshape(qkv_low.shape[0], -1).astype(jnp.bfloat16),
        row_peak + jnp.log(row_total),
    )


def attend_backward(qkv_low, key_set, allowed, log_total, grad_context):
    queries, key_rows, value_rows = split_heads(qkv_low, key_set)
    score_scale = HEAD_DIM ** (-0.5)
    scores = (
        jnp.einsum("qhd,khd->hqk", queries, key_rows, preferred_element_type=jnp.float32)
        * score_scale
    )
    masked = jnp.where(allowed[None], scores, -1e30)
    soft_weights = jnp.exp(masked - log_total)
    grad_heads = grad_context.reshape(queries.shape)
    grad_soft = jnp.einsum(
        "qhd,khd->hqk", grad_heads, value_rows, preferred_element_type=jnp.float32
    )
    row_inner = jnp.sum(soft_weights * grad_soft, axis=-1, keepdims=True)
    grad_scores = (soft_weights * (grad_soft - row_inner)).astype(jnp.bfloat16)
    grad_queries = (
        jnp.einsum("hqk,khd->qhd", grad_scores, key_rows, preferred_element_type=jnp.float32)
        * score_scale
    )
    grad_keys = (
        jnp.einsum("hqk,qhd->khd", grad_scores, queries, preferred_element_type=jnp.float32)
        * score_scale
    )
    grad_values = jnp.einsum(
        "hqk,qhd->khd",
        soft_weights.astype(jnp.bfloat16),
        grad_heads,
        preferred_element_type=jnp.float32,
    )
    key_count = key_set.shape[0]
    grad_pairs = jnp.stack(
        [grad_keys.reshape(key_count, -1), grad_values.reshape(key_count, -1)], axis=1
    )
    return (grad_queries.reshape(qkv_low.shape[0], -1), grad_pairs)


def on_device(inputs, lengths, w_qkv, w_out, w_fc, w_proj, b_qv, b_fc, gains, shifts, cotangent):
    n1, q, kv, cotg, wall, vec, bqv = call_first(
        inputs, cotangent, pack_weights(w_qkv, w_out, w_fc, w_proj),
        pack_small(gains[0], shifts[0], b_qv[0], b_fc[0])
    )
    all_gains, all_shifts = vec[None, 0:2], vec[None, 2:6]
    group_index = lax.axis_index("dp")
    tok_group = 512
    query_pos = group_index * tok_group + jnp.arange(tok_group, dtype=jnp.int32)
    key_pos = (group_index - SPAN) * tok_group + jnp.arange((SPAN + 1) * tok_group, dtype=jnp.int32)
    same_seq = sequence_of(lengths, query_pos)[:, None] == sequence_of(lengths, key_pos)[None, :]
    allowed = same_seq & (key_pos[None, :] <= query_pos[:, None])
    residual = inputs.astype(jnp.float32)
    levels = 1
    weight_qkv, weight_out, weight_fc, weight_proj = (
        wall[:, :768].reshape(1024, 3, 256), wall[:, 768:1024].T, wall[:, 1024:2048], wall[:, 2048:].T)
    bias_fc = vec[8]
    fetched = None
    layer_gains, layer_shifts = all_gains[0], all_shifts[0]
    gathered_one = n1
    key_set = kv.reshape(2560, 2, 256)
    qkv_low = jnp.concatenate([q[:, None], key_set[2048:]], axis=1)
    context_low, log_total = attend_forward(qkv_low, key_set, allowed)
    after = residual + tensor_sum(context_low, weight_out) + layer_shifts[2]
    gathered_two = gather_rows(layer_norm(after, layer_gains[1], layer_shifts[1]))
    pre_act = jnp.dot(gathered_two, weight_fc, preferred_element_type=jnp.float32) + bias_fc.astype(
        jnp.float32
    )
    act_low = gelu_tanh(pre_act).astype(jnp.bfloat16)
    output_rows = after + tensor_sum(act_low, weight_proj) + layer_shifts[3]
    grad_res = cotangent.astype(jnp.float32)
    reduced = [None] * levels
    gain_parts = [None] * levels
    shift_parts = [None] * levels
    layer_index = 0
    layer_index = 0
    layer_input = residual
    grad_mlp = cotg
    grad_weight_proj = contract_rows(act_low, grad_mlp)
    grad_act = contract_cols(grad_mlp, weight_proj)
    gelu_value, gelu_pull = jax.vjp(gelu_tanh, pre_act)
    grad_pre = gelu_pull(grad_act)[0].astype(jnp.bfloat16)
    grad_bias_fc = jnp.sum(grad_pre.astype(jnp.float32), axis=0)
    grad_weight_fc = contract_rows(gathered_two, grad_pre)
    grad_normed_two = tensor_back(grad_pre, weight_fc)
    norm_value, norm_pull = jax.vjp(layer_norm, after, layer_gains[1], layer_shifts[1])
    grad_after_norm, grad_gain_two, grad_shift_two = norm_pull(grad_normed_two)
    grad_after = grad_res + grad_after_norm
    grad_mlp_bias = jnp.sum(grad_res, axis=0)
    grad_attn = gather_grads(grad_after)
    grad_weight_out = contract_rows(context_low, grad_attn)
    grad_context = contract_cols(grad_attn, weight_out).astype(jnp.bfloat16)
    grad_queries, grad_pairs = attend_backward(qkv_low, key_set, allowed, log_total, grad_context)
    pair_pieces = grad_pairs.reshape(SPAN + 1, tok_group, 2, grad_pairs.shape[2])
    pair_total = pair_pieces[SPAN]
    carried = jnp.zeros_like(pair_total)
    for hop_index in range(SPAN, 0, -1):
        carried = from_behind(carried + pair_pieces[SPAN - hop_index], "dp", -1)
    pair_total = pair_total + carried
    grad_qkv = jnp.concatenate([grad_queries[:, None], pair_total], axis=1).astype(jnp.bfloat16)
    grad_qkv_wide = grad_qkv.astype(jnp.float32)
    grad_bias_qv = jnp.stack(
        [jnp.sum(grad_qkv_wide[:, 0], axis=0), jnp.sum(grad_qkv_wide[:, 2], axis=0)]
    )
    grad_flat = grad_qkv.reshape(tok_group, -1)
    grad_weight_qkv = contract_rows(gathered_one, grad_flat).reshape(weight_qkv.shape)
    grad_normed_one = tensor_back(grad_flat, weight_qkv.reshape(weight_qkv.shape[0], -1))
    norm_value, norm_pull = jax.vjp(layer_norm, layer_input, layer_gains[0], layer_shifts[0])
    grad_input_norm, grad_gain_one, grad_shift_one = norm_pull(grad_normed_one)
    grad_attn_bias = jnp.sum(grad_after, axis=0)
    grad_res = grad_after + grad_input_norm
    reduced[layer_index] = (
        lax.psum_scatter(grad_weight_qkv, "dp", scatter_dimension=0, tiled=True),
        lax.psum_scatter(grad_weight_out, "dp", scatter_dimension=1, tiled=True),
        lax.psum_scatter(grad_weight_fc, "dp", scatter_dimension=0, tiled=True),
        lax.psum_scatter(grad_weight_proj, "dp", scatter_dimension=1, tiled=True),
        lax.psum_scatter(grad_bias_qv, "dp", scatter_dimension=1, tiled=True),
        lax.psum_scatter(grad_bias_fc, "dp", scatter_dimension=0, tiled=True),
    )
    gain_parts[layer_index] = jnp.stack([grad_gain_one, grad_gain_two])
    shift_parts[layer_index] = jnp.stack(
        [grad_shift_one, grad_shift_two, grad_attn_bias, grad_mlp_bias]
    )
    grad_gains, grad_shifts = (
        lax.psum_scatter(jnp.stack(gain_parts), ("dp", "tensor"), scatter_dimension=2, tiled=True),
        lax.psum_scatter(jnp.stack(shift_parts), ("dp", "tensor"), scatter_dimension=2, tiled=True),
    )
    grad_w_qkv = jnp.stack([reduced[0][0]])
    grad_w_out = jnp.stack([reduced[0][1]])
    grad_w_fc = jnp.stack([reduced[0][2]])
    grad_w_proj = jnp.stack([reduced[0][3]])
    grad_b_qv = jnp.stack([reduced[0][4]])
    grad_b_fc = jnp.stack([reduced[0][5]])
    return (
        output_rows,
        grad_res,
        grad_w_qkv,
        grad_w_out,
        grad_w_fc,
        grad_w_proj,
        grad_b_qv,
        grad_b_fc,
        grad_gains,
        grad_shifts,
    )


def solution(mesh):
    return jax.shard_map(
        on_device,
        mesh=mesh,
        in_specs=(
            P(("dp", "tensor"), None),
            P(),
            P(None, "dp", None, "tensor"),
            P(None, "tensor", "dp"),
            P(None, "dp", "tensor"),
            P(None, "tensor", "dp"),
            P(None, None, ("tensor", "dp")),
            P(None, ("tensor", "dp")),
            P(None, None, ("dp", "tensor")),
            P(None, None, ("dp", "tensor")),
            P(("dp", "tensor"), None),
        ),
        out_specs=(
            P(("dp", "tensor"), None),
            P(("dp", "tensor"), None),
            P(None, "dp", None, "tensor"),
            P(None, "tensor", "dp"),
            P(None, "dp", "tensor"),
            P(None, "tensor", "dp"),
            P(None, None, ("tensor", "dp")),
            P(None, ("tensor", "dp")),
            P(None, None, ("dp", "tensor")),
            P(None, None, ("dp", "tensor")),
        ),
        check_vma=False,
    )
```

```python
import functools

import jax
import jax.numpy as jnp
from jax import lax
from jax.experimental import pallas as pl
from jax.experimental.pallas import tpu as pltpu
from jax.sharding import PartitionSpec as P

HEAD_DIM = 64
BLOCK = 128
D = 1024
GROUP = 512
BF = jnp.bfloat16
F32 = jnp.float32
MESH = pl.DeviceIdType.MESH
VMEM_LIMIT = 58 * 1024 * 1024


def nn(a, b):
    return jnp.dot(a, b, preferred_element_type=F32)


def nt(a, b):
    return lax.dot_general(a, b, (((1,), (1,)), ((), ())), preferred_element_type=F32)


def tn(a, b):
    return lax.dot_general(a, b, (((0,), (0,)), ((), ())), preferred_element_type=F32)


def rows(start, size, step=None):
    return pl.ds(pl.multiple_of(start, step or size), size)


class Place:
    def __init__(self):
        self.dp = lax.axis_index("dp")
        self.z = lax.axis_index("tensor")
        self.c = lax.rem(self.dp, 2)
        self.chip = self.dp // 2
        self.y = lax.rem(self.chip, 4)
        self.x = self.chip // 4

    def at(self, dx=0, dy=0, dz=0, flip=False):
        x = lax.rem(self.x + dx + 4, 4)
        y = lax.rem(self.y + dy + 4, 4)
        c = 1 - self.c if flip else self.c
        return ((x * 4 + y) * 2 + c, lax.rem(self.z + dz + 4, 4))

    def linear(self, step):
        return (lax.rem(self.chip + step + 16, 16) * 2 + self.c, self.z)


class Copies:
    def __init__(self, send_sem, recv_sem):
        self.send_sem, self.recv_sem = send_sem, recv_sem
        self.started, self.settled = [], []

    def put(self, src, dst, device):
        k = len(self.started)
        copy = pltpu.make_async_remote_copy(
            src_ref=src,
            dst_ref=dst,
            send_sem=self.send_sem.at[k],
            recv_sem=self.recv_sem.at[k],
            device_id=device,
            device_id_type=MESH,
        )
        copy.start()
        self.started.append(copy)
        return copy

    def settle(self, *copies):
        for copy in copies:
            copy.wait_send()
            self.settled.append(copy)

    def finish(self):
        for copy in self.started:
            if not any(copy is other for other in self.settled):
                copy.wait_send()


def greet(devices):
    barrier = pltpu.get_barrier_semaphore()
    for device in devices:
        pl.semaphore_signal(barrier, inc=1, device_id=device, device_id_type=MESH)
    pl.semaphore_wait(barrier, len(devices))


class RingGather:
    def __init__(self, copies, place, buf, size=BLOCK):
        self.copies, self.place, self.buf, self.size = copies, place, buf, size

    def block(self, dz, part=None):
        start = lax.rem(self.place.z + dz + 4, 4) * self.size
        if part is None:
            return self.buf.at[rows(start, self.size)]
        half = self.size // 2
        return self.buf.at[rows(start + part * half, half)]

    def start(self):
        own = self.block(0)
        self.up = self.copies.put(own, own, self.place.at(dz=1))
        self.down = self.copies.put(own, own, self.place.at(dz=-1))

    def below(self):
        self.up.wait_recv()
        half = self.block(-1, 0)
        self.up2 = self.copies.put(half, half, self.place.at(dz=1))

    def above(self):
        self.down.wait_recv()
        half = self.block(1, 1)
        self.down2 = self.copies.put(half, half, self.place.at(dz=-1))

    def far(self):
        self.up2.wait_recv()
        self.down2.wait_recv()


class PlaneGather:
    def __init__(self, copies, place, w, first, width):
        self.copies, self.place, self.w = copies, place, w
        c = place.c
        self.first, self.width = first, width
        self.cols = pl.ds(pl.multiple_of(first + c * (width // 2), 128), width // 2)
        self.near = 1 - c, c

    def dev(self, axis, step):
        c = self.place.c
        if axis == 0:
            return self.place.at(dx=c * step, dy=(1 - c) * step)
        return self.place.at(dx=(1 - c) * step, dy=c * step)

    def block(self, first_off, second_off, part=None):
        p, c = self.place, self.place.c
        a = lax.rem(p.y * (1 - c) + p.x * c + first_off + 4, 4)
        b = lax.rem(p.x * (1 - c) + p.y * c + second_off + 4, 4)
        x = b * (1 - c) + a * c
        y = a * (1 - c) + b * c
        start = (x * 4 + y) * 64
        if part is None:
            return self.w.at[rows(start, 64), self.cols]
        return self.w.at[rows(start + 32 * part, 32), self.cols]

    def put(self, ref, device):
        return self.copies.put(ref, ref, device)

    def start(self):
        p = self.place
        mine = self.w.at[rows(p.dp * 32, 32), pl.ds(self.first, self.width)]
        self.swap = self.put(mine, p.at(flip=True))

    def spread(self, first_off):
        ref = self.block(first_off, 0)
        return (self.put(ref, self.dev(1, 1)), self.put(ref, self.dev(1, -1)))

    def share(self, first_off, second_off):
        self.shared.append(self.put(self.block(first_off, second_off), self.place.at(flip=True)))

    def step1(self):
        self.swap.wait_recv()
        ref = self.block(0, 0)
        self.shared = []
        self.up = self.put(ref, self.dev(0, 1))
        self.down = self.put(ref, self.dev(0, -1))
        self.out = {0: self.spread(0)}

    def step2(self):
        self.up.wait_recv()
        self.up2 = self.put(self.block(-1, 0, 0), self.dev(0, 1))
        self.down.wait_recv()
        self.down2 = self.put(self.block(1, 0, 1), self.dev(0, -1))
        self.out[-1] = self.spread(-1)
        self.out[1] = self.spread(1)
        self.share(-1, 0)
        self.share(1, 0)

    def step3(self):
        self.up2.wait_recv()
        self.down2.wait_recv()
        self.out[2] = self.spread(2)
        self.share(2, 0)

    def step4(self):
        self.far = []
        for first_off in (0, -1, 1, 2):
            up, down = self.out[first_off]
            up.wait_recv()
            self.far.append(self.put(self.block(first_off, -1, 0), self.dev(1, 1)))
            down.wait_recv()
            self.far.append(self.put(self.block(first_off, 1, 1), self.dev(1, -1)))
            self.share(first_off, -1)
            self.share(first_off, 1)

    def step5(self):
        for k, first_off in enumerate((0, -1, 1, 2)):
            self.far[2 * k].wait_recv()
            self.far[2 * k + 1].wait_recv()
            self.share(first_off, 2)

    def step6(self):
        for copy in self.shared:
            copy.wait_recv()


def normalised(values):
    centre = values - jnp.mean(values, axis=-1, keepdims=True)
    spread = jnp.mean(centre * centre, axis=-1, keepdims=True)
    scale = lax.rsqrt(spread + 1e-05)
    return centre * scale, scale


def first_kernel(
    x_ref, cot_ref, shard_ref, small_ref,
    n1_ref, q_ref, kv_ref, cotg_ref, w_ref, vec_ref, bqv_ref,
    xg, vz, vall, send_sem, recv_sem,
):
    p = Place()
    greet(
        [p.at(dz=1), p.at(dz=-1), p.at(dz=2), p.at(dx=1), p.at(dx=-1), p.at(dx=2),
         p.at(dy=1), p.at(dy=-1), p.at(dy=2), p.at(flip=True), p.linear(1), p.linear(-1)]
    )
    copies = Copies(send_sem, recv_sem)
    w_ref[rows(p.dp * 32, 32), :] = shard_ref[...]
    head = PlaneGather(copies, p, w_ref, 0, 768)
    head.start()
    small = []
    vz[p.z] = small_ref[0:8]
    for dz in (1, -1, 2):
        small.append(copies.put(vz.at[p.z], vz.at[p.z], p.at(dz=dz)))
    xg[rows(p.z * BLOCK, BLOCK), :] = x_ref[...]
    ring = RingGather(copies, p, xg)
    ring.start()
    head.step1()
    for copy in small:
        copy.wait_recv()
    vall[p.c, p.chip, 0:8] = vz[0] + vz[1] + vz[2] + vz[3]
    vall[p.c, p.chip, 8:16] = small_ref[8:16]
    mine = vall.at[p.c, p.chip]
    small = [copies.put(mine, mine, p.at(dy=dy)) for dy in (1, -1, 2)]
    ring.below()
    ring.above()
    head.step2()
    tail = PlaneGather(copies, p, w_ref, 768, 2304)
    tail.start()
    for copy in small:
        copy.wait_recv()
    mine = vall.at[p.c, rows(p.x * 4, 4)]
    small = [copies.put(mine, mine, p.at(dx=dx)) for dx in (1, -1, 2)]
    head.step3()
    cotg_ref[rows(p.z * BLOCK, BLOCK), :] = cot_ref[...]
    cot_ring = RingGather(copies, p, cotg_ref)
    cot_ring.start()
    for copy in small:
        copy.wait_recv()
    mine = vall.at[p.c]
    last = copies.put(mine, mine, p.at(flip=True))
    head.step4()
    tail.step1()
    ring.far()
    last.wait_recv()
    lanes = []
    for k in range(8):
        total = vall[0, 2 * k] + vall[0, 2 * k + 1] + vall[1, 2 * k] + vall[1, 2 * k + 1]
        vec_ref[:, k * 128:(k + 1) * 128] = total
        lanes.append(total)
    for h in range(2):
        bqv_ref[:, h * 128:(h + 1) * 128] = lanes[4 * h] + lanes[4 * h + 1] + lanes[4 * h + 2] + lanes[4 * h + 3]

    def norm_block(k, carry):
        block = rows(lax.rem(p.z + k, 4) * BLOCK, BLOCK)
        hat, _ = normalised(xg[block, :].astype(F32))
        n1_ref[block, :] = (hat * vec_ref[0:1, :] + vec_ref[2:3, :]).astype(BF)
        return carry

    lax.fori_loop(0, 4, norm_block, 0)
    head.step5()
    tail.step2()
    head.step6()
    tail.step3()
    tail.step4()
    halo = []
    for k in range(4):
        start = lax.rem(p.z + k, 4) * BLOCK
        block = rows(start, BLOCK)
        values = n1_ref[block, :]
        q_ref[block, :] = (nn(values, w_ref[:, 0:256]) + bqv_ref[9:10, :]).astype(BF)
        mine = rows(4 * GROUP + start, BLOCK)
        kv_ref[mine, 0:256] = nn(values, w_ref[:, 256:512]).astype(BF)
        kv_ref[mine, 256:512] = (nn(values, w_ref[:, 512:768]) + bqv_ref[10:11, :]).astype(BF)
        halo.append(
            copies.put(kv_ref.at[mine], kv_ref.at[rows(2 * GROUP + start, BLOCK)], p.linear(1))
        )
    tail.step5()
    cot_ring.below()
    cot_ring.above()
    relay, cross = [], []
    sibling = p.at(flip=True)
    for k in range(4):
        start = lax.rem(p.z + k, 4) * BLOCK
        halo[k].wait_recv()
        near = kv_ref.at[rows(2 * GROUP + start, BLOCK)]
        relay.append(copies.put(near, kv_ref.at[rows(start, BLOCK)], p.linear(1)))
        cross.append(
            copies.put(near, kv_ref.at[rows((1 + 2 * p.c) * GROUP + start, BLOCK)], sibling)
        )
    cot_ring.far()
    for k in range(4):
        start = lax.rem(p.z + k, 4) * BLOCK
        relay[k].wait_recv()
        cross.append(
            copies.put(
                kv_ref.at[rows((4 - 4 * p.c) * GROUP + start, BLOCK)],
                kv_ref.at[rows((3 - 2 * p.c) * GROUP + start, BLOCK)],
                sibling,
            )
        )
    for copy in cross:
        copy.wait_recv()
    tail.step6()
    copies.finish()


N1_COPIES = 2 * 36 + 4 + 4 + 3 + 3 + 3 + 1 + 16


def vm(count):
    return [pl.BlockSpec(memory_space=pltpu.VMEM)] * count


def call_first(x, cot, shard, small):
    return pl.pallas_call(
        first_kernel,
        out_shape=(
            jax.ShapeDtypeStruct((GROUP, D), BF),
            jax.ShapeDtypeStruct((GROUP, 256), BF),
            jax.ShapeDtypeStruct((5 * GROUP, 512), BF),
            jax.ShapeDtypeStruct((GROUP, D), BF),
            jax.ShapeDtypeStruct((D, 3072), BF),
            jax.ShapeDtypeStruct((16, D), F32),
            jax.ShapeDtypeStruct((16, 256), F32),
        ),
        in_specs=vm(4),
        out_specs=tuple(vm(7)),
        scratch_shapes=[
            pltpu.VMEM((GROUP, D), BF),
            pltpu.VMEM((4, 8, 128), F32),
            pltpu.VMEM((2, 16, 16, 128), F32),
            pltpu.SemaphoreType.DMA((N1_COPIES,)),
            pltpu.SemaphoreType.DMA((N1_COPIES,)),
        ],
        compiler_params=pltpu.CompilerParams(
            collective_id=1, has_side_effects=True, vmem_limit_bytes=VMEM_LIMIT
        ),
        name="gather_and_project",
    )(x, cot, shard, small)


def pack_small(gains, shifts, b_qv, b_fc):
    dp, z = lax.axis_index("dp"), lax.axis_index("tensor")
    lane = jnp.arange(128, dtype=jnp.int32)[None, :]
    eight = jnp.concatenate([gains, shifts, jnp.zeros((2, 8), F32)], axis=0)
    top = jnp.where(lane // 8 == lax.rem(dp * 4 + z, 16), jnp.tile(eight, (1, 16)), 0.0)
    fc = jnp.where(lane // 32 == lax.rem(dp, 4), jnp.tile(b_fc[None].astype(F32), (1, 4)), 0.0)
    qv = jnp.where(lane // 8 == lax.rem(dp, 16), jnp.tile(b_qv.astype(F32), (1, 16)), 0.0)
    return jnp.concatenate([top, fc, qv, jnp.zeros((5, 128), F32)], axis=0)


def pack_weights(w_qkv, w_out, w_fc, w_proj):
    return jnp.concatenate(
        [w_qkv[0].reshape(32, 768), w_out[0].T, w_fc[0], w_proj[0].T], axis=1
    )


def heads_down(tile):
    head = lax.broadcasted_iota(jnp.int32, tile.shape, 0) // HEAD_DIM
    return jnp.concatenate([jnp.where(head == h, tile, 0.0) for h in range(4)], axis=1)


def heads_across(tile):
    head = lax.broadcasted_iota(jnp.int32, tile.shape, 1) // HEAD_DIM
    return jnp.concatenate([jnp.where(head == h, tile, 0.0) for h in range(4)], axis=0)


def causal(scores):
    key = lax.broadcasted_iota(jnp.int32, scores.shape, 0)
    query = lax.rem(lax.broadcasted_iota(jnp.int32, scores.shape, 1), BLOCK)
    return jnp.where(key <= query, scores, -1e30)


def attend_kernel(first_ref, q_ref, kv_ref, ctx_ref, lse_ref, vt, scores, acc):
    def turn(j, carry):
        block = rows(j * BLOCK, BLOCK)
        vt[j] = kv_ref[block, 256:512].astype(F32).T.astype(BF)
        return carry

    lax.fori_loop(first_ref[0], 20, turn, 0)

    def query_block(b, carry):
        first, last = first_ref[b], 16 + b
        queries = (q_ref[rows(b * BLOCK, BLOCK), :].astype(F32) * 0.125).T
        wide = heads_down(queries).astype(BF)

        def score(j, top):
            tile = nn(kv_ref[rows(j * BLOCK, BLOCK), 0:256], wide)
            scores[j - first] = tile
            return jnp.maximum(top, jnp.max(tile.reshape(16, 8, 512), axis=0))

        top = lax.fori_loop(first, last, score, jnp.full((8, 512), -1e30, F32))
        tile = causal(nn(kv_ref[rows(last * BLOCK, BLOCK), 0:256], wide))
        scores[last - first] = tile
        top = jnp.maximum(top, jnp.max(tile.reshape(16, 8, 512), axis=0))
        top = jnp.max(top, axis=0, keepdims=True)
        acc[...] = jnp.zeros_like(acc)

        def weigh(j, total):
            weights = jnp.exp(scores[j - first] - top)
            low = weights.astype(BF)
            for h in range(4):
                part = slice(h * HEAD_DIM, (h + 1) * HEAD_DIM)
                acc[part, :] += nn(vt[j, part, :], low[:, h * BLOCK:(h + 1) * BLOCK])
            return total + jnp.sum(weights.reshape(16, 8, 512), axis=0)

        total = lax.fori_loop(first, last + 1, weigh, jnp.zeros((8, 512), F32))
        total = jnp.sum(total, axis=0, keepdims=True)
        lse_ref[pl.ds(b, 1), :] = top + jnp.log(total)
        inverse = 1.0 / total
        context = jnp.concatenate(
            [acc[h * HEAD_DIM:(h + 1) * HEAD_DIM, :] * inverse[:, h * BLOCK:(h + 1) * BLOCK] for h in range(4)],
            axis=0,
        )
        ctx_ref[rows(b * BLOCK, BLOCK), :] = context.T.astype(BF)
        return carry

    lax.fori_loop(0, 4, query_block, 0)


def call_attend(first, q, kv):
    return pl.pallas_call(
        attend_kernel,
        out_shape=(
            jax.ShapeDtypeStruct((GROUP, 256), BF),
            jax.ShapeDtypeStruct((8, 512), F32),
        ),
        in_specs=[pl.BlockSpec(memory_space=pltpu.SMEM)] + vm(2),
        out_specs=tuple(vm(2)),
        scratch_shapes=[
            pltpu.VMEM((20, 256, BLOCK), BF),
            pltpu.VMEM((16, BLOCK, 512), F32),
            pltpu.VMEM((256, BLOCK), F32),
        ],
        compiler_params=pltpu.CompilerParams(vmem_limit_bytes=VMEM_LIMIT),
        name="attend",
    )(first, q, kv)


def attend_back_kernel(
    first_ref, q_ref, kv_ref, ctx_ref, lse_ref, dctx_ref, dq_ref, dkv_ref, kt, dkv, acc
):
    def turn(j, carry):
        block = rows(j * BLOCK, BLOCK)
        kt[j] = kv_ref[block, 0:256].astype(F32).T.astype(BF)
        return carry

    lax.fori_loop(first_ref[0], 20, turn, 0)

    def clear(j, carry):
        dkv[rows(j * BLOCK, BLOCK), :] = jnp.zeros((BLOCK, 512), F32)
        return carry

    lax.fori_loop(0, 20, clear, 0)

    def query_block(b, carry):
        first, last = first_ref[b], 16 + b
        block = rows(b * BLOCK, BLOCK)
        queries = q_ref[block, :].astype(F32) * 0.125
        grads = dctx_ref[block, :].astype(F32)
        turned = grads.T
        wide_q, tall_q = heads_down(queries.T).astype(BF), heads_across(queries).astype(BF)
        wide_g, tall_g = heads_down(turned).astype(BF), heads_across(grads).astype(BF)
        inner = turned * ctx_ref[block, :].astype(F32).T
        inner = jnp.concatenate(
            [jnp.sum(inner[h * HEAD_DIM:(h + 1) * HEAD_DIM], axis=0, keepdims=True) for h in range(4)],
            axis=1,
        )
        lse = lse_ref[pl.ds(b, 1), :]
        acc[...] = jnp.zeros_like(acc)

        def step(j, mask):
            keys = rows(j * BLOCK, BLOCK)
            tile = nn(kv_ref[keys, 0:256], wide_q)
            if mask:
                tile = causal(tile)
            weights = jnp.exp(tile - lse)
            grad = nn(kv_ref[keys, 256:512], wide_g)
            low = (weights * (grad - inner)).astype(BF)
            dkv[keys, 0:256] += nn(low, tall_q)
            dkv[keys, 256:512] += nn(weights.astype(BF), tall_g)
            for h in range(4):
                part = slice(h * HEAD_DIM, (h + 1) * HEAD_DIM)
                acc[part, :] += nn(kt[j, part, :], low[:, h * BLOCK:(h + 1) * BLOCK])

        def full(j, carry):
            step(j, False)
            return carry

        lax.fori_loop(first, last, full, 0)
        step(last, True)
        dq_ref[block, :] = (acc[...].T * 0.125).astype(BF)
        return carry

    lax.fori_loop(0, 4, query_block, 0)

    def store(j, carry):
        block = rows(j * BLOCK, BLOCK)
        dkv_ref[block, :] = dkv[block, :].astype(BF)
        return carry

    lax.fori_loop(0, 20, store, 0)


def call_attend_back(first, q, kv, ctx, lse, dctx):
    return pl.pallas_call(
        attend_back_kernel,
        out_shape=(
            jax.ShapeDtypeStruct((GROUP, 256), BF),
            jax.ShapeDtypeStruct((5 * GROUP, 512), BF),
        ),
        in_specs=[pl.BlockSpec(memory_space=pltpu.SMEM)] + vm(5),
        out_specs=tuple(vm(2)),
        scratch_shapes=[
            pltpu.VMEM((20, 256, BLOCK), BF),
            pltpu.VMEM((5 * GROUP, 512), F32),
            pltpu.VMEM((256, BLOCK), F32),
        ],
        compiler_params=pltpu.CompilerParams(vmem_limit_bytes=VMEM_LIMIT),
        name="attend_back",
    )(first, q, kv, ctx, lse, dctx)


def first_blocks(lengths):
    base = lax.axis_index("dp") * 4
    ends = jnp.cumsum(lengths)
    block = base + jnp.arange(4, dtype=jnp.int32)
    start = jnp.max(jnp.where(ends[None, :] <= block[:, None], ends[None, :], 0), axis=1)
    return start - base + 16


class PlaneScatter:
    copies_needed = 18

    def __init__(self, copies, place, g, scratch):
        self.copies, self.place, self.g = copies, place, g
        self.land, self.far, self.near, self.t, self.far2, self.near2, self.last, self.rest = scratch
        self.half = g.shape[1] // 2

    @staticmethod
    def scratch(width):
        half = width // 2
        return [
            pltpu.VMEM((1024, half), BF),
            pltpu.VMEM((2, 2, 64, half), BF),
            pltpu.VMEM((2, 4, 64, half), BF),
            pltpu.VMEM((4, 64, half), BF),
            pltpu.VMEM((2, 32, half), BF),
            pltpu.VMEM((2, 64, half), BF),
            pltpu.VMEM((32, half), F32),
            pltpu.VMEM((32, half), F32),
        ]

    def dev(self, axis, step):
        c = self.place.c
        if axis == 0:
            return self.place.at(dx=(1 - c) * step, dy=c * step)
        return self.place.at(dx=c * step, dy=(1 - c) * step)

    def first(self, step):
        p = self.place
        return lax.rem(p.x * (1 - p.c) + p.y * p.c + step + 4, 4)

    def second(self, step):
        p = self.place
        return lax.rem(p.y * (1 - p.c) + p.x * p.c + step + 4, 4)

    def block(self, f, s):
        c = self.place.c
        x, y = f * (1 - c) + s * c, s * (1 - c) + f * c
        return rows((x * 4 + y) * 64, 64)

    def start(self):
        c = self.place.c
        other = pl.ds(pl.multiple_of((1 - c) * self.half, 128), self.half)
        self.swap = self.copies.put(self.g.at[:, other], self.land, self.place.at(flip=True))

    def step1(self):
        self.swap.wait_recv()
        mine = pl.ds(pl.multiple_of(self.place.c * self.half, 128), self.half)
        self.mine = mine

        def join(k, carry):
            f = self.first(2 + k // 4)
            block = self.block(f, lax.rem(k, 4))
            self.land[block, :] = (self.land[block, :].astype(F32) + self.g[block, mine].astype(F32)).astype(BF)
            return carry

        lax.fori_loop(0, 4, join, 0)
        self.out = []
        for s in range(4):
            to = self.dev(0, 1 if s < 2 else -1)
            self.out.append(
                self.copies.put(self.land.at[self.block(self.first(2), s)], self.far.at[s // 2, s % 2], to)
            )
        lax.fori_loop(4, 16, join, 0)

    def step2(self):
        self.out2 = []
        for side, step in ((0, 1), (1, -1)):
            f = self.first(step)
            for s in range(4):
                block = self.block(f, s)
                if s // 2 == side:
                    self.out[s].wait_recv()
                    self.land[block, :] = (
                        self.land[block, :].astype(F32) + self.far[side, s % 2].astype(F32)
                    ).astype(BF)
                self.out2.append(
                    self.copies.put(self.land.at[block], self.near.at[side, s], self.dev(0, step))
                )

    def step3(self):
        f = self.first(0)
        for copy in self.out2:
            copy.wait_recv()

        def total(k, carry):
            s = self.second(2 + k)
            self.t[s] = (
                self.land[self.block(f, s), :].astype(F32)
                + self.near[0, s].astype(F32)
                + self.near[1, s].astype(F32)
            ).astype(BF)
            return carry

        lax.fori_loop(0, 1, total, 0)
        s = self.second(2)
        self.up = self.copies.put(self.t.at[s, 0:32], self.far2.at[0], self.dev(1, 1))
        self.down = self.copies.put(self.t.at[s, 32:64], self.far2.at[1], self.dev(1, -1))
        lax.fori_loop(1, 4, total, 0)

    def step4(self):
        s = self.second(1)
        self.up.wait_recv()
        self.t[s, 0:32] = (self.t[s, 0:32].astype(F32) + self.far2[0].astype(F32)).astype(BF)
        self.up2 = self.copies.put(self.t.at[s], self.near2.at[0], self.dev(1, 1))
        s = self.second(-1)
        self.down.wait_recv()
        self.t[s, 32:64] = (self.t[s, 32:64].astype(F32) + self.far2[1].astype(F32)).astype(BF)
        self.down2 = self.copies.put(self.t.at[s], self.near2.at[1], self.dev(1, -1))

    def part(self, c):
        half = rows(c * 32, 32)
        return (
            self.t[self.second(0), half].astype(F32)
            + self.near2[0, half].astype(F32)
            + self.near2[1, half].astype(F32)
        )

    def step5(self):
        self.up2.wait_recv()
        self.down2.wait_recv()
        c = self.place.c
        self.last[...] = self.part(1 - c)
        self.back = self.copies.put(self.last, self.rest, self.place.at(flip=True))

    def step6(self, out):
        out[:, self.mine] = self.part(self.place.c)
        self.back.wait_recv()
        other = pl.ds(pl.multiple_of((1 - self.place.c) * self.half, 128), self.half)
        out[:, other] = self.rest[...]


class RingScatter:
    copies_needed = 4

    def __init__(self, copies, place, scratch):
        self.copies, self.place = copies, place
        self.part, self.far, self.near = scratch

    @staticmethod
    def scratch():
        return [
            pltpu.VMEM((3, BLOCK, D), BF),
            pltpu.VMEM((2, 64, D), BF),
            pltpu.VMEM((2, BLOCK, D), BF),
        ]

    def send_far(self):
        p, c = self.place, self.copies
        self.up = c.put(self.part.at[2, 0:64], self.far.at[0], p.at(dz=1))
        self.down = c.put(self.part.at[2, 64:128], self.far.at[1], p.at(dz=-1))

    def send_above(self):
        self.up.wait_recv()
        self.part[0, 0:64] = (self.part[0, 0:64].astype(F32) + self.far[0].astype(F32)).astype(BF)
        self.up2 = self.copies.put(self.part.at[0], self.near.at[0], self.place.at(dz=1))

    def send_below(self):
        self.down.wait_recv()
        self.part[1, 64:128] = (self.part[1, 64:128].astype(F32) + self.far[1].astype(F32)).astype(BF)
        self.down2 = self.copies.put(self.part.at[1], self.near.at[1], self.place.at(dz=-1))

    def received(self):
        self.up2.wait_recv()
        self.down2.wait_recv()
        return self.near[0].astype(F32) + self.near[1].astype(F32)


class RingReturn:
    copies_needed = 6

    def __init__(self, copies, place, scratch):
        self.copies, self.place = copies, place
        self.part, self.near, self.mid, self.far = scratch

    @staticmethod
    def scratch():
        return [
            pltpu.VMEM((3, BLOCK, D), BF),
            pltpu.VMEM((2, BLOCK, D), BF),
            pltpu.VMEM((2, 64, D), BF),
            pltpu.VMEM((BLOCK, D), BF),
        ]

    def send_above(self):
        self.up = self.copies.put(self.part.at[0], self.near.at[0], self.place.at(dz=1))

    def send_below(self):
        self.down = self.copies.put(self.part.at[1], self.near.at[1], self.place.at(dz=-1))

    def send_far(self):
        p, c = self.place, self.copies
        self.up1 = c.put(self.part.at[2, 0:64], self.mid.at[0], p.at(dz=1))
        self.down1 = c.put(self.part.at[2, 64:128], self.mid.at[1], p.at(dz=-1))

    def pass_on(self):
        p, c = self.place, self.copies
        self.up1.wait_recv()
        self.up2 = c.put(self.mid.at[0], self.far.at[0:64], p.at(dz=1))
        self.down1.wait_recv()
        self.down2 = c.put(self.mid.at[1], self.far.at[64:128], p.at(dz=-1))

    def received(self):
        for copy in (self.up, self.down, self.up2, self.down2):
            copy.wait_recv()
        return self.near[0].astype(F32) + self.near[1].astype(F32) + self.far[...].astype(F32)


def norm_back(hat, scale, grad, gain):
    inner = grad * gain
    mean = jnp.mean(inner, axis=-1, keepdims=True)
    along = jnp.mean(inner * hat, axis=-1, keepdims=True)
    return (
        scale * (inner - mean - hat * along),
        jnp.sum(grad * hat, axis=0, keepdims=True),
        jnp.sum(grad, axis=0, keepdims=True),
    )


def weight_grad(left, right, out, first):
    width = right.shape[1]

    def tile(k, carry):
        turned = left[:, pl.ds(pl.multiple_of(k * 256, 256), 256)].astype(F32).T.astype(BF)
        out[rows(k * 256, 256), first:first + width] = nn(turned, right[...]).astype(BF)
        return carry

    lax.fori_loop(0, 4, tile, 0)


def middle_kernel(
    x_ref, ctx_ref, w_ref, vec_ref, cotg_ref,
    out_ref, gafter_ref, gaf_ref, dctx_ref, dw_ref, sums_ref,
    n2g, act, dpre, dact, own, after, g, send_sem, recv_sem, *scratch,
):
    p = Place()
    greet(
        [p.at(dz=1), p.at(dz=-1), p.at(dx=1), p.at(dx=-1), p.at(dy=1), p.at(dy=-1), p.at(flip=True)]
    )
    copies = Copies(send_sem, recv_sem)
    scatter1 = RingScatter(copies, p, scratch[0:3])
    outs = RingReturn(copies, p, scratch[3:7])
    backs = RingReturn(copies, p, scratch[7:11])
    plane = PlaneScatter(copies, p, g, scratch[11:19])

    def block(dz):
        return rows(lax.rem(p.z + dz + 4, 4) * BLOCK, BLOCK)

    def out_part(dz):
        return nt(ctx_ref[block(dz), :], w_ref[:, 768:1024])

    scatter1.part[2] = out_part(2).astype(BF)
    scatter1.send_far()
    scatter1.part[0] = out_part(1).astype(BF)
    scatter1.send_above()
    scatter1.part[1] = out_part(-1).astype(BF)
    scatter1.send_below()
    after[...] = x_ref[...].astype(F32) + out_part(0) + vec_ref[4:5, :]

    def act_grad(t, carry):
        cols = pl.ds(pl.multiple_of(2048 + t * 256, 256), 256)
        dact[:, pl.ds(pl.multiple_of(t * 256, 256), 256)] = nn(cotg_ref[...], w_ref[:, cols])
        return carry

    lax.fori_loop(0, 4, act_grad, 0)
    after[...] += scatter1.received()
    hat, scale = normalised(after[...])
    n2g[block(0), :] = (hat * vec_ref[1:2, :] + vec_ref[3:4, :]).astype(BF)
    ring = RingGather(copies, p, n2g)
    ring.start()

    def mlp(dz, put_out, put_back):
        here = block(dz)

        def hidden(t, carry):
            cols = pl.ds(pl.multiple_of(t * 256, 256), 256)
            pre = nn(n2g[here, :], w_ref[:, pl.ds(pl.multiple_of(1024 + t * 256, 256), 256)])
            pre = pre + vec_ref[8:9, cols]
            square = pre * pre
            bend = jnp.tanh(0.7978845608028654 * pre * (1.0 + 0.044715 * square))
            act[here, cols] = (0.5 * pre * (1.0 + bend)).astype(BF)
            slope = 0.5 * (1.0 + bend) + 0.5 * pre * (1.0 - bend * bend) * (
                0.7978845608028654 * (1.0 + 0.134145 * square)
            )
            dpre[here, cols] = (dact[here, cols] * slope).astype(BF)
            return carry

        lax.fori_loop(0, 4, hidden, 0)

        def project(t, carry):
            cols = pl.ds(pl.multiple_of(t * 256, 256), 256)
            put_back(cols, nt(dpre[here, :], w_ref[cols, 1024:2048]))
            put_out(cols, nt(act[here, :], w_ref[cols, 2048:3072]))
            return carry

        lax.fori_loop(0, 4, project, 0)

    def into(ref, k):
        def put(cols, value):
            ref[k, :, cols] = value.astype(ref.dtype)

        return put

    mlp(0, into(own, 0), into(own, 1))
    ring.below()
    ring.above()
    mlp(-1, into(outs.part, 1), into(backs.part, 1))
    backs.send_below()
    outs.send_below()
    mlp(1, into(outs.part, 0), into(backs.part, 0))
    backs.send_above()
    outs.send_above()
    ring.far()
    mlp(2, into(outs.part, 2), into(backs.part, 2))
    backs.send_far()
    outs.send_far()
    weight_grad(n2g, dpre, g, 0)
    backs.pass_on()
    outs.pass_on()
    weight_grad(cotg_ref, act, g, 1024)
    plane.start()
    sums_ref[...] = jnp.zeros_like(sums_ref)
    sums_ref[4:5, :] = jnp.sum(dpre[...].astype(F32), axis=0, keepdims=True)
    grad = own[1] + backs.received()
    hat, scale = normalised(after[...])
    back, gain, shift = norm_back(hat, scale, grad, vec_ref[1:2, :])
    residual = cotg_ref[block(0), :].astype(F32)
    back = back + residual
    gaf_ref[block(0), :] = back.astype(BF)
    ring2 = RingGather(copies, p, gaf_ref)
    ring2.start()
    gafter_ref[...] = back
    sums_ref[0:1, :] = gain
    sums_ref[1:2, :] = shift
    sums_ref[2:3, :] = jnp.sum(back, axis=0, keepdims=True)
    sums_ref[3:4, :] = jnp.sum(residual, axis=0, keepdims=True)
    plane.step1()

    def context_grad(dz):
        here = block(dz)
        dctx_ref[here, :] = nn(gaf_ref[here, :], w_ref[:, 768:1024]).astype(BF)

    context_grad(0)
    ring2.below()
    ring2.above()
    plane.step2()
    out_ref[...] = after[...] + own[0] + outs.received() + vec_ref[5:6, :]
    context_grad(-1)
    context_grad(1)
    ring2.far()
    context_grad(2)
    plane.step3()
    plane.step4()
    plane.step5()
    plane.step6(dw_ref)
    copies.finish()


N3_COPIES = 4 + 12 + 8 + 18


def call_middle(x, ctx, w, vec, cotg):
    return pl.pallas_call(
        middle_kernel,
        out_shape=(
            jax.ShapeDtypeStruct((BLOCK, D), F32),
            jax.ShapeDtypeStruct((BLOCK, D), F32),
            jax.ShapeDtypeStruct((GROUP, D), BF),
            jax.ShapeDtypeStruct((GROUP, 256), BF),
            jax.ShapeDtypeStruct((32, 2048), F32),
            jax.ShapeDtypeStruct((8, D), F32),
        ),
        in_specs=vm(5),
        out_specs=tuple(vm(6)),
        scratch_shapes=[
            pltpu.VMEM((GROUP, D), BF),
            pltpu.VMEM((GROUP, D), BF),
            pltpu.VMEM((GROUP, D), BF),
            pltpu.VMEM((GROUP, D), F32),
            pltpu.VMEM((2, BLOCK, D), F32),
            pltpu.VMEM((BLOCK, D), F32),
            pltpu.VMEM((D, 2048), BF),
            pltpu.SemaphoreType.DMA((N3_COPIES,)),
            pltpu.SemaphoreType.DMA((N3_COPIES,)),
            *RingScatter.scratch(),
            *RingReturn.scratch(),
            *RingReturn.scratch(),
            *PlaneScatter.scratch(2048),
        ],
        compiler_params=pltpu.CompilerParams(
            collective_id=2, has_side_effects=True, vmem_limit_bytes=VMEM_LIMIT
        ),
        name="mlp_both_ways",
    )(x, ctx, w, vec, cotg)


def last_kernel(
    x_ref, dq_ref, dkv_ref, n1_ref, w_ref, vec_ref, gafter_ref, gaf_ref, ctx_ref, sums_ref,
    gin_ref, dw_ref, small_ref,
    part, cross, hand, land, dqkv, g, zsum, ysum, csum, send_sem, recv_sem, *scratch,
):
    p = Place()
    greet(
        [p.at(dz=1), p.at(dz=-1), p.at(dz=2), p.at(dx=1), p.at(dx=-1), p.at(dx=2),
         p.at(dy=1), p.at(dy=-1), p.at(dy=2), p.at(flip=True), p.linear(1), p.linear(-1)]
    )
    copies = Copies(send_sem, recv_sem)
    scatter = RingScatter(copies, p, scratch[0:3])
    plane = PlaneScatter(copies, p, g, scratch[3:11])
    sibling = p.at(flip=True)
    even = p.c == 0

    def block(k):
        return rows(lax.rem(p.z + k, 4) * BLOCK, BLOCK)

    order = (2, 1, 3, 0)
    crossing = []
    for k in order:
        start = lax.rem(p.z + k, 4) * BLOCK
        for side in range(2):
            source = dkv_ref.at[rows((1 + 2 * side) * GROUP + start, BLOCK)]
            crossing.append(copies.put(source, cross.at[side, block(k)], sibling))
    far = []
    for i, k in enumerate(order):
        start = lax.rem(p.z + k, 4) * BLOCK
        crossing[2 * i].wait_recv()
        crossing[2 * i + 1].wait_recv()
        low = cross[0, block(k)].astype(F32)
        high = cross[1, block(k)].astype(F32)
        hand[0, block(k)] = (dkv_ref[rows(start, BLOCK), :].astype(F32) + jnp.where(even, 0.0, low)).astype(BF)
        far.append(copies.put(hand.at[0, block(k)], land.at[0, block(k)], p.linear(-1)))
        part[0, block(k)] = dkv_ref[rows(2 * GROUP + start, BLOCK), :].astype(F32) + jnp.where(even, low, high)
        part[1, block(k)] = dkv_ref[rows(4 * GROUP + start, BLOCK), :].astype(F32) + jnp.where(even, high, 0.0)
    dqkv[:, 0:256] = dq_ref[...]
    near = []
    for i, k in enumerate(order):
        far[i].wait_recv()
        hand[1, block(k)] = (part[0, block(k)] + land[0, block(k)].astype(F32)).astype(BF)
        near.append(copies.put(hand.at[1, block(k)], land.at[1, block(k)], p.linear(-1)))
    weight_grad(gaf_ref, ctx_ref, g, 768)
    small_ref[...] = jnp.zeros_like(small_ref)
    small_ref[8:9, :] = sums_ref[4:5, :]
    small_ref[9:10, 0:256] = jnp.sum(dq_ref[...].astype(F32), axis=0, keepdims=True)

    def grad_part(i, k):
        near[i].wait_recv()
        dqkv[block(k), 256:768] = (part[1, block(k)] + land[1, block(k)].astype(F32)).astype(BF)
        return nt(dqkv[block(k), :], w_ref[:, 0:768])

    scatter.part[2] = grad_part(0, 2).astype(BF)
    scatter.send_far()
    scatter.part[0] = grad_part(1, 1).astype(BF)
    scatter.send_above()
    scatter.part[1] = grad_part(2, 3).astype(BF)
    scatter.send_below()
    grad = grad_part(3, 0)
    weight_grad(n1_ref, dqkv, g, 0)
    plane.start()
    small_ref[10:11, 0:256] = jnp.sum(dqkv[:, 512:768].astype(F32), axis=0, keepdims=True)
    grad = grad + scatter.received()
    hat, scale = normalised(x_ref[...].astype(F32))
    back, gain, shift = norm_back(hat, scale, grad, vec_ref[0:1, :])
    small_ref[0:1, :] = gain
    small_ref[1:2, :] = sums_ref[0:1, :]
    small_ref[2:3, :] = shift
    small_ref[3:6, :] = sums_ref[1:4, :]
    top = small_ref.at[0:8]
    sends = [copies.put(top, zsum.at[i], p.at(dz=dz)) for i, dz in enumerate((1, -1, 2))]
    plane.step1()
    gin_ref[...] = gafter_ref[...] + back
    for copy in sends:
        copy.wait_recv()
    copies.settle(*sends)
    small_ref[0:8, :] = small_ref[0:8, :] + zsum[0] + zsum[1] + zsum[2]
    send = copies.put(small_ref, csum.at[0], sibling)
    plane.step2()
    send.wait_recv()
    csum[1] = small_ref[...] + csum[0]
    sends = [copies.put(csum.at[1], ysum.at[i], p.at(dy=dy)) for i, dy in enumerate((1, -1, 2))]
    plane.step3()
    for copy in sends:
        copy.wait_recv()
    csum[2] = csum[1] + ysum[0] + ysum[1] + ysum[2]
    sends = [copies.put(csum.at[2], ysum.at[3 + i], p.at(dx=dx)) for i, dx in enumerate((1, -1, 2))]
    plane.step4()
    plane.step5()
    for copy in sends:
        copy.wait_recv()
    copies.settle(send)
    small_ref[...] = csum[2] + ysum[3] + ysum[4] + ysum[5]
    plane.step6(dw_ref)
    copies.finish()


N5_COPIES = 8 + 4 + 4 + 4 + 18 + 3 + 1 + 3 + 3


def call_last(x, dq, dkv, n1, w, vec, gafter, gaf, ctx, sums):
    return pl.pallas_call(
        last_kernel,
        out_shape=(
            jax.ShapeDtypeStruct((BLOCK, D), F32),
            jax.ShapeDtypeStruct((32, 1024), F32),
            jax.ShapeDtypeStruct((16, D), F32),
        ),
        in_specs=vm(10),
        out_specs=tuple(vm(3)),
        scratch_shapes=[
            pltpu.VMEM((2, GROUP, 512), F32),
            pltpu.VMEM((2, GROUP, 512), BF),
            pltpu.VMEM((2, GROUP, 512), BF),
            pltpu.VMEM((2, GROUP, 512), BF),
            pltpu.VMEM((GROUP, 768), BF),
            pltpu.VMEM((D, 1024), BF),
            pltpu.VMEM((3, 8, D), F32),
            pltpu.VMEM((6, 16, D), F32),
            pltpu.VMEM((3, 16, D), F32),
            pltpu.SemaphoreType.DMA((N5_COPIES,)),
            pltpu.SemaphoreType.DMA((N5_COPIES,)),
            *RingScatter.scratch(),
            *PlaneScatter.scratch(1024),
        ],
        compiler_params=pltpu.CompilerParams(
            collective_id=3, has_side_effects=True, vmem_limit_bytes=VMEM_LIMIT
        ),
        name="project_back",
    )(x, dq, dkv, n1, w, vec, gafter, gaf, ctx, sums)


def on_device(inputs, lengths, w_qkv, w_out, w_fc, w_proj, b_qv, b_fc, gains, shifts, cotangent):
    dp, z = lax.axis_index("dp"), lax.axis_index("tensor")
    first = first_blocks(lengths)
    n1, q, kv, cotg, w, vec, _ = call_first(
        inputs,
        cotangent,
        pack_weights(w_qkv, w_out, w_fc, w_proj),
        pack_small(gains[0], shifts[0], b_qv[0], b_fc[0]),
    )
    ctx, lse = call_attend(first, q, kv)
    out, gafter, gaf, dctx, dw_mlp, sums = call_middle(inputs, ctx, w, vec, cotg)
    dq, dkv = call_attend_back(first, q, kv, ctx, lse, dctx)
    gin, dw_attn, small = call_last(inputs, dq, dkv, n1, w, vec, gafter, gaf, ctx, sums)
    own = lax.dynamic_slice(small, (0, (dp * 4 + z) * 8), (6, 8))
    return (
        out,
        gin,
        dw_attn[:, :768].reshape(1, 32, 3, 256),
        dw_attn[:, 768:].T[None],
        dw_mlp[None, :, :1024],
        dw_mlp[:, 1024:].T[None],
        lax.dynamic_slice(small, (9, dp * 8), (2, 8))[None],
        lax.dynamic_slice(small, (8, dp * 32), (1, 32)),
        own[None, 0:2],
        own[None, 2:6],
    )


def solution(mesh):
    return jax.shard_map(
        on_device,
        mesh=mesh,
        in_specs=(
            P(("dp", "tensor"), None),
            P(),
            P(None, "dp", None, "tensor"),
            P(None, "tensor", "dp"),
            P(None, "dp", "tensor"),
            P(None, "tensor", "dp"),
            P(None, None, ("tensor", "dp")),
            P(None, ("tensor", "dp")),
            P(None, None, ("dp", "tensor")),
            P(None, None, ("dp", "tensor")),
            P(("dp", "tensor"), None),
        ),
        out_specs=(
            P(("dp", "tensor"), None),
            P(("dp", "tensor"), None),
            P(None, "dp", None, "tensor"),
            P(None, "tensor", "dp"),
            P(None, "dp", "tensor"),
            P(None, "tensor", "dp"),
            P(None, None, ("tensor", "dp")),
            P(None, ("tensor", "dp")),
            P(None, None, ("dp", "tensor")),
            P(None, None, ("dp", "tensor")),
        ),
        check_vma=False,
    )
```

```python
import functools

import jax
import jax.numpy as jnp
from jax import lax
from jax.experimental import pallas as pl
from jax.experimental.pallas import tpu as pltpu
from jax.sharding import PartitionSpec as P

HEAD_DIM = 64
BLOCK = 128
D = 1024
GROUP = 512
BF = jnp.bfloat16
F32 = jnp.float32
MESH = pl.DeviceIdType.MESH
VMEM_LIMIT = 58 * 1024 * 1024


def nn(a, b):
    return jnp.dot(a, b, preferred_element_type=F32)


def nt(a, b):
    return lax.dot_general(a, b, (((1,), (1,)), ((), ())), preferred_element_type=F32)


def tn(a, b):
    return lax.dot_general(a, b, (((0,), (0,)), ((), ())), preferred_element_type=F32)


def rows(start, size, step=None):
    return pl.ds(pl.multiple_of(start, step or size), size)


class Place:
    def __init__(self):
        self.dp = lax.axis_index("dp")
        self.z = lax.axis_index("tensor")
        self.c = lax.rem(self.dp, 2)
        self.chip = self.dp // 2
        self.y = lax.rem(self.chip, 4)
        self.x = self.chip // 4

    def at(self, dx=0, dy=0, dz=0, flip=False):
        x = lax.rem(self.x + dx + 4, 4)
        y = lax.rem(self.y + dy + 4, 4)
        c = 1 - self.c if flip else self.c
        return ((x * 4 + y) * 2 + c, lax.rem(self.z + dz + 4, 4))

    def linear(self, step):
        return (lax.rem(self.chip + step + 16, 16) * 2 + self.c, self.z)

    def beside(self, dy, step):
        chip = self.x * 4 + lax.rem(self.y + dy + 4, 4)
        return (lax.rem(chip + step + 16, 16) * 2 + self.c, self.z)

    def beside_source(self, step=2, dy=-1):
        chip = lax.rem(self.chip - step + 16, 16)
        y = lax.rem(lax.rem(chip, 4) + dy + 4, 4)
        return ((chip // 4 * 4 + y) * 2 + self.c, self.z)


class Copies:
    def __init__(self, send_sem, recv_sem):
        self.send_sem, self.recv_sem = send_sem, recv_sem
        self.started, self.settled = [], []

    def put(self, src, dst, device):
        k = len(self.started)
        copy = pltpu.make_async_remote_copy(
            src_ref=src,
            dst_ref=dst,
            send_sem=self.send_sem.at[k],
            recv_sem=self.recv_sem.at[k],
            device_id=device,
            device_id_type=MESH,
        )
        copy.start()
        self.started.append(copy)
        return copy

    def settle(self, *copies):
        for copy in copies:
            copy.wait_send()
            self.settled.append(copy)

    def finish(self):
        for copy in self.started:
            if not any(copy is other for other in self.settled):
                copy.wait_send()


def greet(devices):
    barrier = pltpu.get_barrier_semaphore()
    for device in devices:
        pl.semaphore_signal(barrier, inc=1, device_id=device, device_id_type=MESH)
    pl.semaphore_wait(barrier, len(devices))


class RingGather:
    def __init__(self, copies, place, buf, size=BLOCK):
        self.copies, self.place, self.buf, self.size = copies, place, buf, size

    def block(self, dz, part=None):
        start = lax.rem(self.place.z + dz + 4, 4) * self.size
        if part is None:
            return self.buf.at[rows(start, self.size)]
        half = self.size // 2
        return self.buf.at[rows(start + part * half, half)]

    def start(self):
        own = self.block(0)
        self.up = self.copies.put(own, own, self.place.at(dz=1))
        self.down = self.copies.put(own, own, self.place.at(dz=-1))

    def below(self):
        self.up.wait_recv()
        half = self.block(-1, 0)
        self.up2 = self.copies.put(half, half, self.place.at(dz=1))

    def above(self):
        self.down.wait_recv()
        half = self.block(1, 1)
        self.down2 = self.copies.put(half, half, self.place.at(dz=-1))

    def far(self):
        self.up2.wait_recv()
        self.down2.wait_recv()


class DirectGather:
    copies_needed = 31

    def __init__(self, copies, place, w):
        self.copies, self.place, self.w = copies, place, w
        self.shared = []

    def dev(self, axis, step):
        c = self.place.c
        if axis == 0:
            return self.place.at(dx=c * step, dy=(1 - c) * step)
        return self.place.at(dx=(1 - c) * step, dy=c * step)

    def block(self, a, b):
        p, c = self.place, self.place.c
        x = lax.rem(p.x + b * (1 - c) + a * c + 4, 4)
        y = lax.rem(p.y + a * (1 - c) + b * c + 4, 4)
        return self.w.at[rows(((x * 4 + y) * 2 + c) * 32, 32)]

    def put(self, ref, device):
        return self.copies.put(ref, ref, device)

    def spread(self, a):
        ref = self.block(a, 0)
        self.second[a] = [self.put(ref, self.dev(1, step)) for step in (1, -1, 2)]
        self.shared.append(self.put(ref, self.place.at(flip=True)))

    def start(self):
        ref = self.block(0, 0)
        self.first = [self.put(ref, self.dev(0, step)) for step in (1, -1, 2)]
        self.second = {}
        self.spread(0)

    def step1(self):
        for copy, a in zip(self.first, (-1, 1, 2)):
            copy.wait_recv()
            self.spread(a)

    def step2(self):
        for a in (0, -1, 1, 2):
            for copy, b in zip(self.second[a], (-1, 1, 2)):
                copy.wait_recv()
                self.shared.append(self.put(self.block(a, b), self.place.at(flip=True)))

    def step3(self):
        for copy in self.shared:
            copy.wait_recv()


class PlaneGather:
    def __init__(self, copies, place, w, first, width):
        self.copies, self.place, self.w = copies, place, w
        c = place.c
        self.first, self.width = first, width
        self.cols = pl.ds(pl.multiple_of(first + c * (width // 2), 128), width // 2)

    def dev(self, axis, step):
        if axis == 0:
            return self.place.at(dy=step)
        return self.place.at(dx=step)

    def block(self, first_off, second_off, part=None):
        p = self.place
        start = (lax.rem(p.x + second_off + 4, 4) * 4 + lax.rem(p.y + first_off + 4, 4)) * 64
        if part is None:
            return self.w.at[rows(start, 64), self.cols]
        return self.w.at[rows(start + 32 * part, 32), self.cols]

    def put(self, ref, device):
        return self.copies.put(ref, ref, device)

    def start(self):
        p = self.place
        mine = self.w.at[rows(p.dp * 32, 32), pl.ds(self.first, self.width)]
        self.swap = self.put(mine, p.at(flip=True))

    def spread(self, first_off):
        ref = self.block(first_off, 0)
        return (self.put(ref, self.dev(1, 1)), self.put(ref, self.dev(1, -1)))

    def share(self, first_off, second_off):
        self.shared.append(self.put(self.block(first_off, second_off), self.place.at(flip=True)))

    def step1(self):
        self.swap.wait_recv()
        ref = self.block(0, 0)
        self.shared = []
        self.up = self.put(ref, self.dev(0, 1))
        self.down = self.put(ref, self.dev(0, -1))
        self.out = {0: self.spread(0)}

    def step2(self):
        self.up.wait_recv()
        self.up2 = self.put(self.block(-1, 0, 0), self.dev(0, 1))
        self.down.wait_recv()
        self.down2 = self.put(self.block(1, 0, 1), self.dev(0, -1))
        self.out[-1] = self.spread(-1)
        self.out[1] = self.spread(1)
        self.share(-1, 0)
        self.share(1, 0)

    def step3(self):
        self.up2.wait_recv()
        self.down2.wait_recv()
        self.out[2] = self.spread(2)
        self.share(2, 0)

    def step4(self):
        self.far = []
        for first_off in (0, -1, 1, 2):
            up, down = self.out[first_off]
            up.wait_recv()
            self.far.append(self.put(self.block(first_off, -1, 0), self.dev(1, 1)))
            down.wait_recv()
            self.far.append(self.put(self.block(first_off, 1, 1), self.dev(1, -1)))
            self.share(first_off, -1)
            self.share(first_off, 1)

    def step5(self):
        for k, first_off in enumerate((0, -1, 1, 2)):
            self.far[2 * k].wait_recv()
            self.far[2 * k + 1].wait_recv()
            self.share(first_off, 2)

    def step6(self):
        for copy in self.shared:
            copy.wait_recv()


def normalised(values):
    centre = values - jnp.mean(values, axis=-1, keepdims=True)
    spread = jnp.mean(centre * centre, axis=-1, keepdims=True)
    scale = lax.rsqrt(spread + 1e-05)
    return centre * scale, scale


def one_hot(shape, offset):
    row = lax.broadcasted_iota(jnp.int32, shape, 0)
    lane = lax.broadcasted_iota(jnp.int32, shape, 1)
    return jnp.where(lane == row + offset, 1.0, 0.0).astype(F32)


def exact(a, b):
    return jnp.dot(a, b, precision=lax.Precision.HIGHEST, preferred_element_type=F32)


def first_kernel(
    x_ref, cot_ref, wqkv_ref, wout_ref, wfc_ref, wproj_ref, gains_ref, shifts_ref, bqv_ref, bfc_ref,
    q_ref, kv_ref, vec_ref, n1_out, xg_out, cotg_out, wqkv_out, wo_out, wmlp_out,
    n1, xg, cotg, wq, wo, wmlp, vz, vall, bias, mid, out_sem, send_sem, recv_sem,
):
    p = Place()
    mine = rows(p.dp * 32, 32)
    for j in range(3):
        wq[mine, j * 256:(j + 1) * 256] = wqkv_ref[j]
    wq[mine, 768:1024] = wout_ref[...]
    wmlp[mine, 0:1024] = wfc_ref[...]
    wmlp[mine, 1024:2048] = wproj_ref[...]
    xg[rows(p.z * BLOCK, BLOCK), :] = x_ref[...]
    cotg[rows(p.z * BLOCK, BLOCK), :] = cot_ref[...]
    place8 = one_hot((8, 128), lax.rem(p.dp * 4 + p.z, 16) * 8)
    own = vz.at[p.z]
    own[...] = jnp.zeros((8, 128), F32)
    own[0:2] = exact(gains_ref[...], place8)
    own[2:6] = exact(shifts_ref[...], place8)
    tile = vall.at[p.c, p.chip]
    tile[8:16] = jnp.zeros((8, 128), F32)
    tile[8:9] = exact(bfc_ref[...].astype(F32), one_hot((32, 128), lax.rem(p.dp, 4) * 32))
    tile[9:11] = exact(bqv_ref[...].astype(F32), one_hot((8, 128), lax.rem(p.dp, 16) * 8))
    greet(
        [p.at(dz=1), p.at(dz=-1), p.at(dz=2), p.at(dx=1), p.at(dx=-1), p.at(dx=2),
         p.at(dy=1), p.at(dy=-1), p.at(dy=2), p.at(flip=True), p.linear(1), p.linear(-1),
         p.beside(1, 2), p.beside_source()]
    )
    copies = Copies(send_sem, recv_sem)
    head = DirectGather(copies, p, wq)
    head.start()
    small = [copies.put(own, own, p.at(dz=dz)) for dz in (1, -1, 2)]
    ring = RingGather(copies, p, xg)
    ring.start()
    tail = PlaneGather(copies, p, wmlp, 0, 2048)
    for copy in small:
        copy.wait_recv()
    tile[0:8] = vz[0] + vz[1] + vz[2] + vz[3]
    small = [copies.put(tile, tile, p.at(dy=dy)) for dy in (1, -1, 2)]
    head.step1()
    tail.start()
    for copy in small:
        copy.wait_recv()
    line = vall.at[p.c, rows(p.x * 4, 4)]
    small = [copies.put(line, line, p.at(dx=dx)) for dx in (1, -1, 2)]
    ring.below()
    ring.above()
    cot_ring = RingGather(copies, p, cotg)
    cot_ring.start()
    for copy in small:
        copy.wait_recv()
    plane = vall.at[p.c]
    last = copies.put(plane, plane, p.at(flip=True))
    head.step2()
    tail.step1()
    ring.far()
    last.wait_recv()
    lanes = []
    for k in range(8):
        total = vall[0, 2 * k] + vall[0, 2 * k + 1] + vall[1, 2 * k] + vall[1, 2 * k + 1]
        vec_ref[:, k * 128:(k + 1) * 128] = total
        lanes.append(total)
    for h in range(2):
        bias[:, h * 128:(h + 1) * 128] = lanes[4 * h] + lanes[4 * h + 1] + lanes[4 * h + 2] + lanes[4 * h + 3]

    def norm_block(k, carry):
        block = rows(lax.rem(p.z + k, 4) * BLOCK, BLOCK)
        hat, _ = normalised(xg[block, :].astype(F32))
        n1[block, :] = (hat * vec_ref[0:1, :] + vec_ref[2:3, :]).astype(BF)
        return carry

    lax.fori_loop(0, 4, norm_block, 0)
    cot_ring.below()
    cot_ring.above()
    head.step3()

    def start_of(k):
        return lax.rem(p.z + k, 4) * BLOCK

    sibling = p.at(flip=True)
    near, there, cross = {}, {}, []
    for k in (2, 0, 3, 1):
        start = start_of(k)
        block = rows(start, BLOCK)
        values = n1[block, :]
        ours = rows(4 * GROUP + start, BLOCK)
        kv_ref[ours, 0:256] = nn(values, wq[:, 256:512]).astype(BF)
        kv_ref[ours, 256:512] = (nn(values, wq[:, 512:768]) + bias[10:11, :]).astype(BF)
        if k < 2:
            there[k] = copies.put(kv_ref.at[ours], mid.at[k], p.at(dy=-1))
        else:
            near[k] = copies.put(kv_ref.at[ours], kv_ref.at[rows(2 * GROUP + start, BLOCK)], p.linear(1))
    for k in (0, 1):
        ours = kv_ref.at[rows(4 * GROUP + start_of(k), BLOCK)]
        near[k] = copies.put(ours, kv_ref.at[rows(2 * GROUP + start_of(k), BLOCK)], p.linear(1))
    wo[rows(p.z * D, D), :] = wq[:, 768:1024]
    wo_ring = RingGather(copies, p, wo, D)
    wo_ring.start()
    tail.step2()
    q_ref[...] = (nn(n1[...], wq[:, 0:256]) + bias[9:10, :]).astype(BF)
    saves = [
        pltpu.make_async_copy(source, target, out_sem.at[i])
        for i, (source, target) in enumerate(
            (
                (n1, n1_out), (xg, xg_out), (wq.at[:, 0:768], wqkv_out), (cotg, cotg_out),
                (wo, wo_out), (wmlp, wmlp_out),
            )
        )
    ]
    for i in range(3):
        saves[i].start()
    far = {}
    for k in (0, 1):
        there[k].wait_recv()
        far[k] = copies.put(mid.at[k], kv_ref.at[rows(start_of(k), BLOCK)], p.beside(1, 2))

    def pass_near(k, onward):
        near[k].wait_recv()
        ref = kv_ref.at[rows(2 * GROUP + start_of(k), BLOCK)]
        if onward:
            far[k] = copies.put(ref, kv_ref.at[rows(start_of(k), BLOCK)], p.linear(1))
        cross.append(
            copies.put(ref, kv_ref.at[rows((1 + 2 * p.c) * GROUP + start_of(k), BLOCK)], sibling)
        )

    pass_near(2, True)
    pass_near(3, True)
    tail.step3()
    cot_ring.far()
    saves[3].start()
    tail.step4()
    pass_near(0, False)
    pass_near(1, False)
    wo_ring.below()
    wo_ring.above()

    def pass_far(k):
        far[k].wait_recv()
        cross.append(
            copies.put(
                kv_ref.at[rows((4 - 4 * p.c) * GROUP + start_of(k), BLOCK)],
                kv_ref.at[rows((3 - 2 * p.c) * GROUP + start_of(k), BLOCK)],
                sibling,
            )
        )

    pass_far(0)
    pass_far(1)
    tail.step5()
    pass_far(2)
    pass_far(3)
    tail.step6()
    saves[5].start()
    wo_ring.far()
    saves[4].start()
    for copy in cross:
        copy.wait_recv()
    for save in saves:
        save.wait()
    copies.finish()


N1_COPIES = 31 + 36 + 10 + 12 + 18


def vm(count):
    return [pl.BlockSpec(memory_space=pltpu.VMEM)] * count


def far_memory(count):
    return [pl.BlockSpec(memory_space=pl.ANY)] * count


def call_first(*operands):
    shape = jax.ShapeDtypeStruct
    return pl.pallas_call(
        first_kernel,
        out_shape=(
            shape((GROUP, 256), BF),
            shape((5 * GROUP, 512), BF),
            shape((16, D), F32),
            shape((GROUP, D), BF),
            shape((GROUP, D), BF),
            shape((GROUP, D), BF),
            shape((D, 768), BF),
            shape((4 * D, 256), BF),
            shape((D, 2048), BF),
        ),
        in_specs=vm(10),
        out_specs=tuple(vm(3) + far_memory(6)),
        scratch_shapes=[
            pltpu.VMEM((GROUP, D), BF),
            pltpu.VMEM((GROUP, D), BF),
            pltpu.VMEM((GROUP, D), BF),
            pltpu.VMEM((D, 1024), BF),
            pltpu.VMEM((4 * D, 256), BF),
            pltpu.VMEM((D, 2048), BF),
            pltpu.VMEM((4, 8, 128), F32),
            pltpu.VMEM((2, 16, 16, 128), F32),
            pltpu.VMEM((16, 256), F32),
            pltpu.VMEM((2, BLOCK, 512), BF),
            pltpu.SemaphoreType.DMA((6,)),
            pltpu.SemaphoreType.DMA((N1_COPIES,)),
            pltpu.SemaphoreType.DMA((N1_COPIES,)),
        ],
        compiler_params=pltpu.CompilerParams(
            collective_id=1, has_side_effects=True, vmem_limit_bytes=VMEM_LIMIT
        ),
        name="gather_and_project",
    )(*operands)

SPAN = 512
TOGETHER = 4


def first_blocks(lengths_ref, first_ref):
    base = lax.axis_index("dp") * 4
    end = jnp.int32(0)
    first = [jnp.int32(0)] * 4
    for i in range(32):
        end = end + lengths_ref[i]
        first = [jnp.where(end <= base + b, end, first[b]) for b in range(4)]
    for b in range(4):
        first_ref[b] = first[b] - base + 16


def heads_across(tile):
    head = lax.broadcasted_iota(jnp.int32, tile.shape, 1) // HEAD_DIM
    return jnp.concatenate([jnp.where(head == h, tile, 0.0) for h in range(4)], axis=0)


def heads_together(tile):
    head = lax.broadcasted_iota(jnp.int32, (BLOCK, 256), 1) // HEAD_DIM
    return sum(jnp.where(head == h, tile[h * BLOCK:(h + 1) * BLOCK], 0.0) for h in range(4))


def causal(scores):
    query = lax.rem(lax.broadcasted_iota(jnp.int32, scores.shape, 0), BLOCK)
    key = lax.broadcasted_iota(jnp.int32, scores.shape, 1)
    return jnp.where(key <= query + (SPAN - BLOCK), scores, -1e30)


def outside(block, first):
    lane = lax.broadcasted_iota(jnp.int32, (1, SPAN), 1)
    return jnp.where(lane < (first - block) * BLOCK, -1e30, 0.0)


def parts(tile):
    return [tile[:, i * 128:(i + 1) * 128] for i in range(SPAN // 128)]


def attend_kernel(lengths_ref, q_ref, kv_ref, ctx_ref, lse_ref, scores, top, total, acc, tall, first_ref):
    first_blocks(lengths_ref, first_ref)
    tops, totals, accs, talls = (
        [ref.at[i] for i in range(TOGETHER)] for ref in (top, total, acc, tall)
    )

    def query_blocks(group, carry):
        blocks = [group * TOGETHER + i for i in range(TOGETHER)]
        firsts = [first_ref[b] for b in blocks]
        for i, b in enumerate(blocks):
            talls[i][...] = heads_across(q_ref[rows(b * BLOCK, BLOCK), :].astype(F32) * 0.125).astype(BF)

        def left_of(i, pair):
            return 17 + blocks[i] - (pair + 1) * (SPAN // BLOCK)

        def score(i, pair):
            left = left_of(i, pair)
            tile = nt(talls[i][...], kv_ref[rows(left * BLOCK, SPAN, BLOCK), 0:256])
            return tile + outside(left, firsts[i])

        for i in range(TOGETHER):
            tile = causal(score(i, 0))
            scores[i, 0] = tile
            tops[i][...] = functools.reduce(jnp.maximum, parts(tile))

        def more(pair, carry):
            for i in range(TOGETHER):
                tile = score(i, pair)
                scores[i, pair] = tile
                tops[i][...] = functools.reduce(jnp.maximum, parts(tile), tops[i][...])
            return carry

        counts = [(16 + b - first) // (SPAN // BLOCK) + 1 for b, first in zip(blocks, firsts)]
        pairs = functools.reduce(jnp.maximum, counts)
        lax.fori_loop(1, pairs, more, 0)
        for i in range(TOGETHER):
            tops[i][...] = jnp.broadcast_to(jnp.max(tops[i][...], axis=1, keepdims=True), (512, 128))
            totals[i][...] = jnp.zeros((512, 128), F32)
            accs[i][...] = jnp.zeros((512, 256), F32)

        def weigh(pair, carry):
            for i in range(TOGETHER):
                weights = [jnp.exp(part - tops[i][...]) for part in parts(scores[i, pair])]
                totals[i][...] += sum(weights)
                weights = jnp.concatenate([part.astype(BF) for part in weights], axis=1)
                accs[i][...] += nn(weights, kv_ref[rows(left_of(i, pair) * BLOCK, SPAN, BLOCK), 256:512])
            return carry

        lax.fori_loop(0, pairs, weigh, 0)
        for i, b in enumerate(blocks):
            sums = jnp.sum(totals[i][...], axis=1, keepdims=True)
            lse_ref[b] = tops[i][...] + jnp.log(sums)
            ctx_ref[rows(b * BLOCK, BLOCK), :] = heads_together(accs[i][...] * (1.0 / sums)).astype(BF)
        return carry

    lax.fori_loop(0, 4 // TOGETHER, query_blocks, 0)


def call_attend(lengths, q, kv):
    return pl.pallas_call(
        attend_kernel,
        out_shape=(
            jax.ShapeDtypeStruct((GROUP, 256), BF),
            jax.ShapeDtypeStruct((4, 512, 128), F32),
        ),
        in_specs=[pl.BlockSpec(memory_space=pltpu.SMEM)] + vm(2),
        out_specs=tuple(vm(2)),
        scratch_shapes=[
            pltpu.VMEM((TOGETHER, 2048 // SPAN, 512, SPAN), F32),
            pltpu.VMEM((TOGETHER, 512, 128), F32),
            pltpu.VMEM((TOGETHER, 512, 128), F32),
            pltpu.VMEM((TOGETHER, 512, 256), F32),
            pltpu.VMEM((TOGETHER, 512, 256), BF),
            pltpu.SMEM((4,), jnp.int32),
        ],
        compiler_params=pltpu.CompilerParams(vmem_limit_bytes=VMEM_LIMIT),
        name="attend",
    )(lengths, q, kv)


def attend_back_kernel(
    lengths_ref, q_ref, kv_ref, ctx_ref, lse_ref, dctx_ref, dq_ref, dkv_ref,
    dkv, acc, tall_q, tall_g, inner, first_ref,
):
    first_blocks(lengths_ref, first_ref)
    accs, talls_q, talls_g, inners = (
        [ref.at[i] for i in range(TOGETHER)] for ref in (acc, tall_q, tall_g, inner)
    )

    def clear(j, carry):
        dkv[rows(j * BLOCK, BLOCK), :] = jnp.zeros((BLOCK, 512), F32)
        return carry

    lax.fori_loop(0, 20, clear, 0)

    def query_blocks(group, carry):
        blocks = [group * TOGETHER + i for i in range(TOGETHER)]
        firsts = [first_ref[b] for b in blocks]
        for i, b in enumerate(blocks):
            block = rows(b * BLOCK, BLOCK)
            grads = dctx_ref[block, :].astype(F32)
            talls_q[i][...] = heads_across(q_ref[block, :].astype(F32) * 0.125).astype(BF)
            talls_g[i][...] = heads_across(grads).astype(BF)
            product = heads_across(grads * ctx_ref[block, :].astype(F32))
            inners[i][...] = jnp.broadcast_to(jnp.sum(product, axis=1, keepdims=True), (512, 128))
            accs[i][...] = jnp.zeros((512, 256), F32)

        def step(pair, mask):
            low, weights, keys = [], [], []
            for i, b in enumerate(blocks):
                left = 17 + b - (pair + 1) * (SPAN // BLOCK)
                keys.append(rows(left * BLOCK, SPAN, BLOCK))
                tile = nt(talls_q[i][...], kv_ref[keys[i], 0:256]) + outside(left, firsts[i])
                if mask:
                    tile = causal(tile)
                weight = jnp.exp(tile - jnp.concatenate([lse_ref[b]] * (SPAN // 128), axis=1))
                grad = nt(talls_g[i][...], kv_ref[keys[i], 256:512])
                inner_row = jnp.concatenate([inners[i][...]] * (SPAN // 128), axis=1)
                low.append((weight * (grad - inner_row)).astype(BF))
                weights.append(weight.astype(BF))
                accs[i][...] += nn(low[i], kv_ref[keys[i], 0:256])
            for i in range(TOGETHER):
                dkv[keys[i], 0:256] += tn(low[i], talls_q[i][...])
                dkv[keys[i], 256:512] += tn(weights[i], talls_g[i][...])

        step(0, True)

        def full(pair, carry):
            step(pair, False)
            return carry

        counts = [(16 + b - first) // (SPAN // BLOCK) + 1 for b, first in zip(blocks, firsts)]
        lax.fori_loop(1, functools.reduce(jnp.maximum, counts), full, 0)
        for i, b in enumerate(blocks):
            dq_ref[rows(b * BLOCK, BLOCK), :] = heads_together(accs[i][...] * 0.125).astype(BF)
        return carry

    lax.fori_loop(0, 4 // TOGETHER, query_blocks, 0)

    def store(j, carry):
        block = rows(j * BLOCK, BLOCK)
        dkv_ref[block, :] = dkv[block, :].astype(BF)
        return carry

    lax.fori_loop(0, 20, store, 0)


def call_attend_back(lengths, q, kv, ctx, lse, dctx):
    return pl.pallas_call(
        attend_back_kernel,
        out_shape=(
            jax.ShapeDtypeStruct((GROUP, 256), BF),
            jax.ShapeDtypeStruct((5 * GROUP, 512), BF),
        ),
        in_specs=[pl.BlockSpec(memory_space=pltpu.SMEM)] + vm(5),
        out_specs=tuple(vm(2)),
        scratch_shapes=[
            pltpu.VMEM((5 * GROUP, 512), F32),
            pltpu.VMEM((TOGETHER, 512, 256), F32),
            pltpu.VMEM((TOGETHER, 512, 256), BF),
            pltpu.VMEM((TOGETHER, 512, 256), BF),
            pltpu.VMEM((TOGETHER, 512, 128), F32),
            pltpu.SMEM((4,), jnp.int32),
        ],
        compiler_params=pltpu.CompilerParams(vmem_limit_bytes=VMEM_LIMIT),
        name="attend_back",
    )(lengths, q, kv, ctx, lse, dctx)


class PlaneScatter:
    copies_needed = 18

    def __init__(self, copies, place, g, scratch):
        self.copies, self.place, self.g = copies, place, g
        self.land, self.far, self.near, self.t, self.far2, self.near2, self.last, self.rest = scratch
        self.half = g.shape[1] // 2

    @staticmethod
    def scratch(width):
        half = width // 2
        return [
            pltpu.VMEM((1024, half), BF),
            pltpu.VMEM((2, 2, 64, half), BF),
            pltpu.VMEM((2, 4, 64, half), BF),
            pltpu.VMEM((4, 64, half), BF),
            pltpu.VMEM((2, 32, half), BF),
            pltpu.VMEM((2, 64, half), BF),
            pltpu.VMEM((32, half), F32),
            pltpu.VMEM((32, half), F32),
        ]

    def dev(self, axis, step):
        c = self.place.c
        if axis == 0:
            return self.place.at(dx=(1 - c) * step, dy=c * step)
        return self.place.at(dx=c * step, dy=(1 - c) * step)

    def first(self, step):
        p = self.place
        return lax.rem(p.x * (1 - p.c) + p.y * p.c + step + 4, 4)

    def second(self, step):
        p = self.place
        return lax.rem(p.y * (1 - p.c) + p.x * p.c + step + 4, 4)

    def block(self, f, s):
        c = self.place.c
        x, y = f * (1 - c) + s * c, s * (1 - c) + f * c
        return rows((x * 4 + y) * 64, 64)

    def start(self):
        c = self.place.c
        other = pl.ds(pl.multiple_of((1 - c) * self.half, 128), self.half)
        self.swap = self.copies.put(self.g.at[:, other], self.land, self.place.at(flip=True))

    def step1(self):
        self.swap.wait_recv()
        mine = pl.ds(pl.multiple_of(self.place.c * self.half, 128), self.half)
        self.mine = mine

        def join(k, carry):
            f = self.first(2 + k // 4)
            block = self.block(f, lax.rem(k, 4))
            self.land[block, :] = (self.land[block, :].astype(F32) + self.g[block, mine].astype(F32)).astype(BF)
            return carry

        lax.fori_loop(0, 4, join, 0)
        self.out = []
        for s in range(4):
            to = self.dev(0, 1 if s < 2 else -1)
            self.out.append(
                self.copies.put(self.land.at[self.block(self.first(2), s)], self.far.at[s // 2, s % 2], to)
            )
        lax.fori_loop(4, 16, join, 0)

    def step2(self):
        self.out2 = []
        for side, step in ((0, 1), (1, -1)):
            f = self.first(step)
            for s in range(4):
                block = self.block(f, s)
                if s // 2 == side:
                    self.out[s].wait_recv()
                    self.land[block, :] = (
                        self.land[block, :].astype(F32) + self.far[side, s % 2].astype(F32)
                    ).astype(BF)
                self.out2.append(
                    self.copies.put(self.land.at[block], self.near.at[side, s], self.dev(0, step))
                )

    def step3(self):
        f = self.first(0)
        for copy in self.out2:
            copy.wait_recv()

        def total(k, carry):
            s = self.second(2 + k)
            self.t[s] = (
                self.land[self.block(f, s), :].astype(F32)
                + self.near[0, s].astype(F32)
                + self.near[1, s].astype(F32)
            ).astype(BF)
            return carry

        lax.fori_loop(0, 1, total, 0)
        s = self.second(2)
        self.up = self.copies.put(self.t.at[s, 0:32], self.far2.at[0], self.dev(1, 1))
        self.down = self.copies.put(self.t.at[s, 32:64], self.far2.at[1], self.dev(1, -1))
        lax.fori_loop(1, 4, total, 0)

    def step4(self):
        s = self.second(1)
        self.up.wait_recv()
        self.t[s, 0:32] = (self.t[s, 0:32].astype(F32) + self.far2[0].astype(F32)).astype(BF)
        self.up2 = self.copies.put(self.t.at[s], self.near2.at[0], self.dev(1, 1))
        s = self.second(-1)
        self.down.wait_recv()
        self.t[s, 32:64] = (self.t[s, 32:64].astype(F32) + self.far2[1].astype(F32)).astype(BF)
        self.down2 = self.copies.put(self.t.at[s], self.near2.at[1], self.dev(1, -1))

    def part(self, c):
        half = rows(c * 32, 32)
        return (
            self.t[self.second(0), half].astype(F32)
            + self.near2[0, half].astype(F32)
            + self.near2[1, half].astype(F32)
        )

    def step5(self):
        self.up2.wait_recv()
        self.down2.wait_recv()
        c = self.place.c
        self.last[...] = self.part(1 - c)
        self.back = self.copies.put(self.last, self.rest, self.place.at(flip=True))

    def step6(self, out):
        out[:, self.mine] = self.part(self.place.c)
        self.back.wait_recv()
        other = pl.ds(pl.multiple_of((1 - self.place.c) * self.half, 128), self.half)
        out[:, other] = self.rest[...]


class QuickScatter:
    copies_needed = 17

    def __init__(self, copies, place, g, scratch):
        self.copies, self.place, self.g = copies, place, g
        self.land, self.near, self.t, self.near2, self.last, self.rest = scratch
        self.half = g.shape[1] // 2

    @staticmethod
    def scratch(width):
        half = width // 2
        return [
            pltpu.VMEM((1024, half), BF),
            pltpu.VMEM((3, 4, 64, half), BF),
            pltpu.VMEM((4, 64, half), BF),
            pltpu.VMEM((3, 64, half), BF),
            pltpu.VMEM((32, half), F32),
            pltpu.VMEM((32, half), F32),
        ]

    dev, first, second, block, start = (
        PlaneScatter.dev, PlaneScatter.first, PlaneScatter.second, PlaneScatter.block, PlaneScatter.start
    )

    def step1(self):
        self.swap.wait_recv()
        self.mine = pl.ds(pl.multiple_of(self.place.c * self.half, 128), self.half)
        self.out = []
        for i, step in enumerate((2, 1, -1, 0)):
            f = self.first(step)

            def join(s, carry):
                block = self.block(f, s)
                self.land[block, :] = (
                    self.land[block, :].astype(F32) + self.g[block, self.mine].astype(F32)
                ).astype(BF)
                return carry

            lax.fori_loop(0, 4, join, 0)
            if step:
                for s in range(4):
                    self.out.append(
                        self.copies.put(self.land.at[self.block(f, s)], self.near.at[i, s], self.dev(0, step))
                    )

    def step2(self):
        for copy in self.out:
            copy.wait_recv()
        f = self.first(0)

        def total(s, carry):
            value = self.land[self.block(f, s), :].astype(F32)
            for i in range(3):
                value = value + self.near[i, s].astype(F32)
            self.t[s] = value.astype(BF)
            return carry

        lax.fori_loop(0, 4, total, 0)
        self.out2 = [
            self.copies.put(self.t.at[self.second(step)], self.near2.at[i], self.dev(1, step))
            for i, step in enumerate((2, 1, -1))
        ]

    def part(self, c):
        half = rows(c * 32, 32)
        value = self.t[self.second(0), half].astype(F32)
        for i in range(3):
            value = value + self.near2[i, half].astype(F32)
        return value

    def step3(self):
        for copy in self.out2:
            copy.wait_recv()
        self.last[...] = self.part(1 - self.place.c)
        self.back = self.copies.put(self.last, self.rest, self.place.at(flip=True))

    step4 = PlaneScatter.step6


class RingScatter:
    copies_needed = 4

    def __init__(self, copies, place, scratch):
        self.copies, self.place = copies, place
        self.part, self.far, self.near = scratch

    @staticmethod
    def scratch():
        return [
            pltpu.VMEM((3, BLOCK, D), BF),
            pltpu.VMEM((2, 64, D), BF),
            pltpu.VMEM((2, BLOCK, D), BF),
        ]

    def send_far(self):
        p, c = self.place, self.copies
        self.up = c.put(self.part.at[2, 0:64], self.far.at[0], p.at(dz=1))
        self.down = c.put(self.part.at[2, 64:128], self.far.at[1], p.at(dz=-1))

    def send_above(self):
        self.up.wait_recv()
        self.part[0, 0:64] = (self.part[0, 0:64].astype(F32) + self.far[0].astype(F32)).astype(BF)
        self.up2 = self.copies.put(self.part.at[0], self.near.at[0], self.place.at(dz=1))

    def send_below(self):
        self.down.wait_recv()
        self.part[1, 64:128] = (self.part[1, 64:128].astype(F32) + self.far[1].astype(F32)).astype(BF)
        self.down2 = self.copies.put(self.part.at[1], self.near.at[1], self.place.at(dz=-1))

    def received(self):
        self.up2.wait_recv()
        self.down2.wait_recv()
        return self.near[0].astype(F32) + self.near[1].astype(F32)


class RingReturn:
    copies_needed = 6

    def __init__(self, copies, place, scratch):
        self.copies, self.place = copies, place
        self.part, self.near, self.mid, self.far = scratch

    @staticmethod
    def scratch():
        return [
            pltpu.VMEM((3, BLOCK, D), BF),
            pltpu.VMEM((2, BLOCK, D), BF),
            pltpu.VMEM((2, 64, D), BF),
            pltpu.VMEM((BLOCK, D), BF),
        ]

    def send_above(self):
        self.up = self.copies.put(self.part.at[0], self.near.at[0], self.place.at(dz=1))

    def send_below(self):
        self.down = self.copies.put(self.part.at[1], self.near.at[1], self.place.at(dz=-1))

    def send_far(self):
        p, c = self.place, self.copies
        self.up1 = c.put(self.part.at[2, 0:64], self.mid.at[0], p.at(dz=1))
        self.down1 = c.put(self.part.at[2, 64:128], self.mid.at[1], p.at(dz=-1))

    def pass_on(self):
        p, c = self.place, self.copies
        self.up1.wait_recv()
        self.up2 = c.put(self.mid.at[0], self.far.at[0:64], p.at(dz=1))
        self.down1.wait_recv()
        self.down2 = c.put(self.mid.at[1], self.far.at[64:128], p.at(dz=-1))

    def received(self):
        for copy in (self.up, self.down, self.up2, self.down2):
            copy.wait_recv()
        return self.near[0].astype(F32) + self.near[1].astype(F32) + self.far[...].astype(F32)


def norm_back(hat, scale, grad, gain):
    inner = grad * gain
    mean = jnp.mean(inner, axis=-1, keepdims=True)
    along = jnp.mean(inner * hat, axis=-1, keepdims=True)
    return (
        scale * (inner - mean - hat * along),
        jnp.sum(grad * hat, axis=0, keepdims=True),
        jnp.sum(grad, axis=0, keepdims=True),
    )


def weight_grad(left, right, out, first):
    width = right.shape[1]

    def tile(k, carry):
        turned = left[:, pl.ds(pl.multiple_of(k * 256, 256), 256)].astype(F32).T.astype(BF)
        out[rows(k * 256, 256), first:first + width] = nn(turned, right[...]).astype(BF)
        return carry

    lax.fori_loop(0, 4, tile, 0)


def middle_kernel(
    x_ref, ctx_ref, vec_ref, wo_any, wmlp_any, cotg_any,
    gafter_ref, gaf_ref, dctx_ref, sums_ref, res_ref, outs_ref, dw_any,
    wo, wmlp, cotg, ctxf, n2g, act, dpre, dact, back, own, after, dw, dctx, io_sem, send_sem, recv_sem,
    *scratch,
):
    p = Place()
    loads = [
        pltpu.make_async_copy(source, target, io_sem.at[i])
        for i, (source, target) in enumerate(((wo_any, wo), (cotg_any, cotg), (wmlp_any, wmlp)))
    ]
    for load in loads:
        load.start()
    greet([p.at(dz=1), p.at(dz=-1), p.at(dz=2)])
    copies = Copies(send_sem, recv_sem)
    backs = RingReturn(copies, p, scratch[0:4])

    def block(dz):
        return rows(lax.rem(p.z + dz + 4, 4) * BLOCK, BLOCK)

    swaps = [
        copies.put(ctx_ref.at[block(dz)], ctxf.at[p.z], p.at(dz=dz)) for dz in (2, 1, -1)
    ]
    ctxf[p.z] = ctx_ref[block(0), :]
    for load in loads:
        load.wait()

    def act_grad(t, carry):
        cols = pl.ds(pl.multiple_of(1024 + t * 256, 256), 256)
        dact[:, pl.ds(pl.multiple_of(t * 256, 256), 256)] = nn(cotg[...], wmlp[:, cols])
        return carry

    lax.fori_loop(0, 4, act_grad, 0)
    for copy in swaps:
        copy.wait_recv()
    total = x_ref[...].astype(F32) + vec_ref[4:5, :]
    for k in range(4):
        total = total + nt(ctxf[k], wo[k * D:(k + 1) * D, :])
    after[...] = total
    hat, scale = normalised(after[...])
    n2g[block(0), :] = (hat * vec_ref[1:2, :] + vec_ref[3:4, :]).astype(BF)
    ring = RingGather(copies, p, n2g)
    ring.start()

    def mlp(dz, put_back):
        here = block(dz)

        def hidden(t, carry):
            cols = pl.ds(pl.multiple_of(t * 256, 256), 256)
            pre = nn(n2g[here, :], wmlp[:, cols]) + vec_ref[8:9, cols]
            square = pre * pre
            bend = jnp.tanh(0.7978845608028654 * pre * (1.0 + 0.044715 * square))
            act[here, cols] = (0.5 * pre * (1.0 + bend)).astype(BF)
            slope = 0.5 * (1.0 + bend) + 0.5 * pre * (1.0 - bend * bend) * (
                0.7978845608028654 * (1.0 + 0.134145 * square)
            )
            dpre[here, cols] = (dact[here, cols] * slope).astype(BF)
            return carry

        lax.fori_loop(0, 4, hidden, 0)

        def project(t, carry):
            cols = pl.ds(pl.multiple_of(t * 256, 256), 256)
            put_back(cols, nt(dpre[here, :], wmlp[cols, 0:1024]))
            return carry

        lax.fori_loop(0, 4, project, 0)

    def into(k):
        def put(cols, value):
            backs.part[k, :, cols] = value.astype(BF)

        return put

    def keep(cols, value):
        own[:, cols] = value

    mlp(0, keep)
    ring.below()
    ring.above()
    mlp(-1, into(1))
    backs.send_below()
    mlp(1, into(0))
    backs.send_above()
    ring.far()
    mlp(2, into(2))
    backs.send_far()
    weight_grad(n2g, dpre, dw, 0)
    backs.pass_on()
    weight_grad(cotg, act, dw, 1024)
    save = pltpu.make_async_copy(dw, dw_any, io_sem.at[3])
    save.start()
    grad = own[...] + backs.received()
    hat, scale = normalised(after[...])
    grad_in, gain, shift = norm_back(hat, scale, grad, vec_ref[1:2, :])
    residual = cotg[block(0), :].astype(F32)
    back[...] = grad_in + residual
    gaf_ref[...] = back[...].astype(BF)
    for k in (2, 1, 3, 0):
        owner = lax.rem(p.z + k, 4)
        part = nn(gaf_ref[...], wo[rows(owner * D, D), :]).astype(BF)
        if k:
            dctx[k] = part
            swaps.append(copies.put(dctx.at[k], dctx_ref.at[block(0)], p.at(dz=k)))
        else:
            dctx_ref[block(0), :] = part
    sums_ref[...] = jnp.zeros_like(sums_ref)
    sums_ref[0:1, :] = gain
    sums_ref[1:2, :] = shift
    sums_ref[2:3, :] = jnp.sum(back[...], axis=0, keepdims=True)
    sums_ref[3:4, :] = jnp.sum(residual, axis=0, keepdims=True)
    sums_ref[4:5, :] = jnp.sum(dpre[...].astype(F32), axis=0, keepdims=True)
    gafter_ref[...] = back[...]

    def output_part(t, carry):
        cols = pl.ds(pl.multiple_of(t * 256, 256), 256)
        for k, dz in enumerate((1, -1, 2)):
            outs_ref[k, :, cols] = nt(act[block(dz), :], wmlp[cols, 1024:2048]).astype(BF)
        res_ref[:, cols] = (
            after[:, cols] + vec_ref[5:6, cols] + nt(act[block(0), :], wmlp[cols, 1024:2048])
        )
        return carry

    lax.fori_loop(0, 4, output_part, 0)
    for copy in swaps[3:]:
        copy.wait_recv()
    save.wait()
    copies.finish()


N3_COPIES = 6 + 4 + 6


def call_middle(*operands):
    shape = jax.ShapeDtypeStruct
    return pl.pallas_call(
        middle_kernel,
        out_shape=(
            shape((BLOCK, D), F32),
            shape((BLOCK, D), BF),
            shape((GROUP, 256), BF),
            shape((8, D), F32),
            shape((BLOCK, D), F32),
            shape((3, BLOCK, D), BF),
            shape((D, 2048), BF),
        ),
        in_specs=vm(3) + far_memory(3),
        out_specs=tuple(vm(6) + far_memory(1)),
        scratch_shapes=[
            pltpu.VMEM((4 * D, 256), BF),
            pltpu.VMEM((D, 2048), BF),
            pltpu.VMEM((GROUP, D), BF),
            pltpu.VMEM((4, BLOCK, 256), BF),
            pltpu.VMEM((GROUP, D), BF),
            pltpu.VMEM((GROUP, D), BF),
            pltpu.VMEM((GROUP, D), BF),
            pltpu.VMEM((GROUP, D), F32),
            pltpu.VMEM((BLOCK, D), F32),
            pltpu.VMEM((BLOCK, D), F32),
            pltpu.VMEM((BLOCK, D), F32),
            pltpu.VMEM((D, 2048), BF),
            pltpu.VMEM((4, BLOCK, 256), BF),
            pltpu.SemaphoreType.DMA((4,)),
            pltpu.SemaphoreType.DMA((N3_COPIES,)),
            pltpu.SemaphoreType.DMA((N3_COPIES,)),
            *RingReturn.scratch(),
        ],
        compiler_params=pltpu.CompilerParams(
            collective_id=2, has_side_effects=True, vmem_limit_bytes=VMEM_LIMIT
        ),
        name="mlp_both_ways",
    )(*operands)


def last_kernel(
    dq_ref, dkv_ref, x_ref, vec_ref, gafter_ref, gaf_ref, ctx_ref, sums_ref, res_ref, outs_ref,
    n1_any, xg_any, wqkv_any, dw_any,
    gin_ref, out_ref, early_ref, late_ref, small_ref,
    n1, xg, wqkv, gafg, part, cross, hand, land, mid, fin, dqkv, early, late, own, zsum, ysum, csum,
    io_sem, send_sem, recv_sem, *scratch,
):
    p = Place()
    loads = [
        pltpu.make_async_copy(source, target, io_sem.at[i])
        for i, (source, target) in enumerate(
            ((dw_any, early.at[:, 0:2048]), (n1_any, n1), (wqkv_any, wqkv), (xg_any, xg))
        )
    ]
    for load in loads:
        load.start()
    gafg[rows(p.z * BLOCK, BLOCK), :] = gaf_ref[...]
    greet(
        [p.at(dz=1), p.at(dz=-1), p.at(dz=2), p.at(dx=1), p.at(dx=-1), p.at(dx=2),
         p.at(dy=1), p.at(dy=-1), p.at(dy=2), p.at(flip=True), p.linear(1), p.linear(-1),
         p.beside(-1, -2), p.beside_source(-2, 1)]
    )
    copies = Copies(send_sem, recv_sem)
    scatter = RingScatter(copies, p, scratch[0:3])
    outs = RingReturn(copies, p, (outs_ref,) + scratch[3:6])
    plane = PlaneScatter(copies, p, early, scratch[6:14])
    quick = QuickScatter(copies, p, late, scratch[14:20])
    sibling = p.at(flip=True)
    even = p.c == 0

    def start_of(k):
        return lax.rem(p.z + k, 4) * BLOCK

    def block(k):
        return rows(start_of(k), BLOCK)

    order = (2, 1, 3, 0)
    crossing = []
    for k in order:
        for side in range(2):
            source = dkv_ref.at[rows((1 + 2 * side) * GROUP + start_of(k), BLOCK)]
            crossing.append(copies.put(source, cross.at[side, block(k)], sibling))
    ring = RingGather(copies, p, gafg)
    ring.start()
    outs.send_above()
    outs.send_below()
    outs.send_far()
    for load in loads:
        load.wait()
    weight_grad(n1, dq_ref, early, 2048)
    plane.start()
    dqkv[:, 0:256] = dq_ref[...]
    far, near = {}, {}
    for k in (3, 2, 0, 1):
        i = order.index(k)
        crossing[2 * i].wait_recv()
        crossing[2 * i + 1].wait_recv()
        low = cross[0, block(k)].astype(F32)
        high = cross[1, block(k)].astype(F32)
        hand[0, block(k)] = (
            dkv_ref[rows(start_of(k), BLOCK), :].astype(F32) + jnp.where(even, 0.0, low)
        ).astype(BF)
        if i < 2:
            far[k] = copies.put(hand.at[0, block(k)], mid.at[i], p.at(dy=1))
        else:
            far[k] = copies.put(hand.at[0, block(k)], land.at[0, block(k)], p.linear(-1))
        part[0, block(k)] = dkv_ref[rows(2 * GROUP + start_of(k), BLOCK), :].astype(F32) + jnp.where(even, low, high)
        part[1, block(k)] = dkv_ref[rows(4 * GROUP + start_of(k), BLOCK), :].astype(F32) + jnp.where(even, high, 0.0)
    for k in order[:2]:
        hand[1, block(k)] = part[0, block(k)].astype(BF)
        near[k] = copies.put(hand.at[1, block(k)], land.at[1, block(k)], p.linear(-1))
    for i, k in enumerate(order[:2]):
        far[k].wait_recv()
        far[k] = copies.put(mid.at[i], fin.at[i], p.beside(-1, -2))
    for k in order[2:]:
        far[k].wait_recv()
        hand[1, block(k)] = (part[0, block(k)] + land[0, block(k)].astype(F32)).astype(BF)
        near[k] = copies.put(hand.at[1, block(k)], land.at[1, block(k)], p.linear(-1))
    ring.below()
    ring.above()
    outs.pass_on()
    plane.step1()
    ring.far()
    weight_grad(gafg, ctx_ref, late, 512)
    small_ref[...] = jnp.zeros_like(small_ref)
    small_ref[8:9, :] = sums_ref[4:5, :]
    small_ref[9:10, 0:256] = jnp.sum(dq_ref[...].astype(F32), axis=0, keepdims=True)
    small_ref[1:2, :] = sums_ref[0:1, :]
    small_ref[3:6, :] = sums_ref[1:4, :]
    out_ref[...] = res_ref[...] + outs.received()
    plane.step2()

    for k in order:
        near[k].wait_recv()
        value = part[1, block(k)] + land[1, block(k)].astype(F32)
        if k in order[:2]:
            far[k].wait_recv()
            value = value + fin[order.index(k)].astype(F32)
        dqkv[block(k), 256:768] = value.astype(BF)
    weight_grad(n1, dqkv.at[:, 256:768], late, 0)
    quick.start()

    def grad_part(k):
        return nt(dqkv[block(k), :], wqkv[...])

    def tally(k, grad):
        hat, _ = normalised(xg[block(k), :].astype(F32))
        small_ref[0:1, :] += jnp.sum(grad * hat, axis=0, keepdims=True)
        small_ref[2:3, :] += jnp.sum(grad, axis=0, keepdims=True)

    grad = grad_part(2)
    scatter.part[2] = grad.astype(BF)
    scatter.send_far()
    tally(2, grad)
    above = grad_part(1)
    scatter.part[0] = above.astype(BF)
    below = grad_part(3)
    scatter.part[1] = below.astype(BF)
    scatter.send_above()
    scatter.send_below()
    plane.step3()
    quick.step1()
    tally(1, above)
    tally(3, below)
    own[...] = grad_part(0)
    tally(0, own[...])
    top = small_ref.at[0:8]
    sends = [copies.put(top, zsum.at[i], p.at(dz=dz)) for i, dz in enumerate((1, -1, 2))]
    small_ref[10:11, 0:256] = jnp.sum(dqkv[:, 512:768].astype(F32), axis=0, keepdims=True)
    plane.step4()
    for copy in sends:
        copy.wait_recv()
    copies.settle(*sends)
    small_ref[0:8, :] = small_ref[0:8, :] + zsum[0] + zsum[1] + zsum[2]
    send = copies.put(small_ref, csum.at[0], sibling)
    quick.step2()
    hat, scale = normalised(x_ref[...].astype(F32))
    back, _, _ = norm_back(hat, scale, own[...] + scatter.received(), vec_ref[0:1, :])
    gin_ref[...] = gafter_ref[...] + back
    send.wait_recv()
    csum[1] = small_ref[...] + csum[0]
    sends = [copies.put(csum.at[1], ysum.at[i], p.at(dy=dy)) for i, dy in enumerate((1, -1, 2))]
    plane.step5()
    quick.step3()
    for copy in sends:
        copy.wait_recv()
    csum[2] = csum[1] + ysum[0] + ysum[1] + ysum[2]
    sends = [copies.put(csum.at[2], ysum.at[3 + i], p.at(dx=dx)) for i, dx in enumerate((1, -1, 2))]
    plane.step6(early_ref)
    quick.step4(late_ref)
    for copy in sends:
        copy.wait_recv()
    copies.settle(send)
    small_ref[...] = csum[2] + ysum[3] + ysum[4] + ysum[5]
    copies.finish()


N5_COPIES = 8 + 4 + 6 + 4 + 4 + 2 + 4 + 18 + 17 + 3 + 1 + 3 + 3


def call_last(*operands):
    shape = jax.ShapeDtypeStruct
    return pl.pallas_call(
        last_kernel,
        out_shape=(
            shape((BLOCK, D), F32),
            shape((BLOCK, D), F32),
            shape((32, 2304), F32),
            shape((32, 768), F32),
            shape((16, D), F32),
        ),
        in_specs=vm(10) + far_memory(4),
        out_specs=tuple(vm(5)),
        scratch_shapes=[
            pltpu.VMEM((GROUP, D), BF),
            pltpu.VMEM((GROUP, D), BF),
            pltpu.VMEM((D, 768), BF),
            pltpu.VMEM((GROUP, D), BF),
            pltpu.VMEM((2, GROUP, 512), F32),
            pltpu.VMEM((2, GROUP, 512), BF),
            pltpu.VMEM((2, GROUP, 512), BF),
            pltpu.VMEM((2, GROUP, 512), BF),
            pltpu.VMEM((2, BLOCK, 512), BF),
            pltpu.VMEM((2, BLOCK, 512), BF),
            pltpu.VMEM((GROUP, 768), BF),
            pltpu.VMEM((D, 2304), BF),
            pltpu.VMEM((D, 768), BF),
            pltpu.VMEM((BLOCK, D), F32),
            pltpu.VMEM((3, 8, D), F32),
            pltpu.VMEM((6, 16, D), F32),
            pltpu.VMEM((3, 16, D), F32),
            pltpu.SemaphoreType.DMA((4,)),
            pltpu.SemaphoreType.DMA((N5_COPIES,)),
            pltpu.SemaphoreType.DMA((N5_COPIES,)),
            *RingScatter.scratch(),
            *RingReturn.scratch()[1:],
            *PlaneScatter.scratch(2304),
            *QuickScatter.scratch(768),
        ],
        compiler_params=pltpu.CompilerParams(
            collective_id=3, has_side_effects=True, vmem_limit_bytes=VMEM_LIMIT
        ),
        name="project_back",
    )(*operands)


def finish_kernel(
    out_ref, gin_ref, early_ref, late_ref, small_ref,
    out, gin, wqkv, wout, wfc, wproj, bqv, bfc, gains, shifts,
):
    dp, z = lax.axis_index("dp"), lax.axis_index("tensor")
    out[...] = out_ref[...]
    gin[...] = gin_ref[...]
    wqkv[0] = early_ref[:, 2048:2304]
    wqkv[1] = late_ref[:, 0:256]
    wqkv[2] = late_ref[:, 256:512]
    wout[...] = late_ref[:, 512:768]
    wfc[...] = early_ref[:, 0:1024]
    wproj[...] = early_ref[:, 1024:2048]

    def pick(first, offset, width):
        lanes = pl.ds(pl.multiple_of(offset // 128 * 128, 128), 128)
        row = lax.broadcasted_iota(jnp.int32, (128, 128), 0)
        lane = lax.broadcasted_iota(jnp.int32, (128, 128), 1)
        chosen = jnp.where(row == lane + lax.rem(offset, 128), 1.0, 0.0).astype(F32)
        return exact(small_ref[first:first + 8, lanes], chosen)[:, 0:width]

    eight = pick(0, (dp * 4 + z) * 8, 8)
    gains[...] = eight[0:2]
    shifts[...] = eight[2:6]
    bqv[...] = pick(8, dp * 8, 8)[1:3]
    bfc[...] = pick(8, dp * 32, 32)[0:1]


def call_finish(*operands):
    shape = jax.ShapeDtypeStruct
    return pl.pallas_call(
        finish_kernel,
        out_shape=(
            shape((BLOCK, D), F32),
            shape((BLOCK, D), F32),
            shape((3, 32, 256), F32),
            shape((32, 256), F32),
            shape((32, 1024), F32),
            shape((32, 1024), F32),
            shape((2, 8), F32),
            shape((1, 32), F32),
            shape((2, 8), F32),
            shape((4, 8), F32),
        ),
        in_specs=vm(5),
        out_specs=tuple(vm(10)),
        compiler_params=pltpu.CompilerParams(vmem_limit_bytes=VMEM_LIMIT),
        name="lay_out",
    )(*operands)


def on_device(inputs, lengths, w_qkv, w_out, w_fc, w_proj, b_qv, b_fc, gains, shifts, cotangent):
    q, kv, vec, n1, xg, cotg, wqkv, wo, wmlp = call_first(
        inputs, cotangent, w_qkv[0].transpose(1, 0, 2), w_out[0].T, w_fc[0], w_proj[0].T,
        gains[0], shifts[0], b_qv[0], b_fc,
    )
    ctx, lse = call_attend(lengths, q, kv)
    gafter, gaf, dctx, sums, res, outs, dw_mlp = call_middle(inputs, ctx, vec, wo, wmlp, cotg)
    dq, dkv = call_attend_back(lengths, q, kv, ctx, lse, dctx)
    gin, out, early, late, small = call_last(
        dq, dkv, inputs, vec, gafter, gaf, ctx, sums, res, outs, n1, xg, wqkv, dw_mlp
    )
    out, gin, g_qkv, g_out, g_fc, g_proj, g_bqv, g_bfc, g_gains, g_shifts = call_finish(
        out, gin, early, late, small
    )
    return (
        out, gin, g_qkv.transpose(1, 0, 2)[None], g_out.T[None], g_fc[None], g_proj.T[None],
        g_bqv[None], g_bfc, g_gains[None], g_shifts[None],
    )


def solution(mesh):
    return jax.shard_map(
        on_device,
        mesh=mesh,
        in_specs=(
            P(("dp", "tensor"), None),
            P(),
            P(None, "dp", None, "tensor"),
            P(None, "tensor", "dp"),
            P(None, "dp", "tensor"),
            P(None, "tensor", "dp"),
            P(None, None, ("tensor", "dp")),
            P(None, ("tensor", "dp")),
            P(None, None, ("dp", "tensor")),
            P(None, None, ("dp", "tensor")),
            P(("dp", "tensor"), None),
        ),
        out_specs=(
            P(("dp", "tensor"), None),
            P(("dp", "tensor"), None),
            P(None, "dp", None, "tensor"),
            P(None, "tensor", "dp"),
            P(None, "dp", "tensor"),
            P(None, "tensor", "dp"),
            P(None, None, ("tensor", "dp")),
            P(None, ("tensor", "dp")),
            P(None, None, ("dp", "tensor")),
            P(None, None, ("dp", "tensor")),
        ),
        check_vma=False,
    )
```

```python
import functools

import jax
import jax.numpy as jnp
from jax import lax
from jax.experimental import pallas as pl
from jax.experimental.pallas import tpu as pltpu
from jax.sharding import PartitionSpec as P

HEAD_DIM = 64
BLOCK = 128
D = 1024
GROUP = 512
SPAN = 512
BF = jnp.bfloat16
F32 = jnp.float32
MESH = pl.DeviceIdType.MESH
VMEM_LIMIT = 58 * 1024 * 1024


def nn(a, b):
    return jnp.dot(a, b, preferred_element_type=F32)


def nt(a, b):
    return lax.dot_general(a, b, (((1,), (1,)), ((), ())), preferred_element_type=F32)


def tn(a, b):
    return lax.dot_general(a, b, (((0,), (0,)), ((), ())), preferred_element_type=F32)


def rows(start, size, step=None):
    return pl.ds(pl.multiple_of(start, step or size), size)


class Place:
    def __init__(self):
        self.dp = lax.axis_index("dp")
        self.z = lax.axis_index("tensor")
        self.c = lax.rem(self.dp, 2)
        self.chip = self.dp // 2
        self.y = lax.rem(self.chip, 4)
        self.x = self.chip // 4

    def at(self, dx=0, dy=0, dz=0, flip=False):
        x = lax.rem(self.x + dx + 4, 4)
        y = lax.rem(self.y + dy + 4, 4)
        c = 1 - self.c if flip else self.c
        return ((x * 4 + y) * 2 + c, lax.rem(self.z + dz + 4, 4))

    def linear(self, step):
        return (lax.rem(self.chip + step + 16, 16) * 2 + self.c, self.z)

    def beside(self, dy, step):
        chip = self.x * 4 + lax.rem(self.y + dy + 4, 4)
        return (lax.rem(chip + step + 16, 16) * 2 + self.c, self.z)

    def beside_source(self, step=2, dy=-1):
        chip = lax.rem(self.chip - step + 16, 16)
        y = lax.rem(lax.rem(chip, 4) + dy + 4, 4)
        return ((chip // 4 * 4 + y) * 2 + self.c, self.z)


class Copies:
    def __init__(self, send_sem, recv_sem):
        self.send_sem, self.recv_sem = send_sem, recv_sem
        self.started, self.settled = [], []

    def put(self, src, dst, device):
        k = len(self.started)
        copy = pltpu.make_async_remote_copy(
            src_ref=src,
            dst_ref=dst,
            send_sem=self.send_sem.at[k],
            recv_sem=self.recv_sem.at[k],
            device_id=device,
            device_id_type=MESH,
        )
        copy.start()
        self.started.append(copy)
        return copy

    def settle(self, *copies):
        for copy in copies:
            copy.wait_send()
            self.settled.append(copy)

    def finish(self):
        for copy in self.started:
            if not any(copy is other for other in self.settled):
                copy.wait_send()


def greet(devices):
    barrier = pltpu.get_barrier_semaphore()
    for device in devices:
        pl.semaphore_signal(barrier, inc=1, device_id=device, device_id_type=MESH)
    pl.semaphore_wait(barrier, len(devices))


class RingGather:
    def __init__(self, copies, place, buf, size=BLOCK):
        self.copies, self.place, self.buf, self.size = copies, place, buf, size

    def block(self, dz, part=None):
        start = lax.rem(self.place.z + dz + 4, 4) * self.size
        if part is None:
            return self.buf.at[rows(start, self.size)]
        half = self.size // 2
        return self.buf.at[rows(start + part * half, half)]

    def start(self):
        own = self.block(0)
        self.up = self.copies.put(own, own, self.place.at(dz=1))
        self.down = self.copies.put(own, own, self.place.at(dz=-1))

    def below(self):
        self.up.wait_recv()
        half = self.block(-1, 0)
        self.up2 = self.copies.put(half, half, self.place.at(dz=1))

    def above(self):
        self.down.wait_recv()
        half = self.block(1, 1)
        self.down2 = self.copies.put(half, half, self.place.at(dz=-1))

    def far(self):
        self.up2.wait_recv()
        self.down2.wait_recv()


class DirectGather:
    copies_needed = 31

    def __init__(self, copies, place, w):
        self.copies, self.place, self.w = copies, place, w
        self.shared = []

    def dev(self, axis, step):
        c = self.place.c
        if axis == 0:
            return self.place.at(dx=c * step, dy=(1 - c) * step)
        return self.place.at(dx=(1 - c) * step, dy=c * step)

    def block(self, a, b):
        p, c = self.place, self.place.c
        x = lax.rem(p.x + b * (1 - c) + a * c + 4, 4)
        y = lax.rem(p.y + a * (1 - c) + b * c + 4, 4)
        return self.w.at[rows(((x * 4 + y) * 2 + c) * 32, 32)]

    def put(self, ref, device):
        return self.copies.put(ref, ref, device)

    def spread(self, a):
        ref = self.block(a, 0)
        self.second[a] = [self.put(ref, self.dev(1, step)) for step in (1, -1, 2)]
        self.shared.append(self.put(ref, self.place.at(flip=True)))

    def start(self):
        ref = self.block(0, 0)
        self.first = [self.put(ref, self.dev(0, step)) for step in (1, -1, 2)]
        self.second = {}
        self.spread(0)

    def step1(self):
        for copy, a in zip(self.first, (-1, 1, 2)):
            copy.wait_recv()
            self.spread(a)

    def step2(self):
        for a in (0, -1, 1, 2):
            for copy, b in zip(self.second[a], (-1, 1, 2)):
                copy.wait_recv()
                self.shared.append(self.put(self.block(a, b), self.place.at(flip=True)))

    def step3(self):
        for copy in self.shared:
            copy.wait_recv()


class PlaneGather:
    def __init__(self, copies, place, w, first, width):
        self.copies, self.place, self.w = copies, place, w
        c = place.c
        self.first, self.width = first, width
        self.cols = pl.ds(pl.multiple_of(first + c * (width // 2), 128), width // 2)

    def dev(self, axis, step):
        if axis == 0:
            return self.place.at(dy=step)
        return self.place.at(dx=step)

    def block(self, first_off, second_off, part=None):
        p = self.place
        start = (lax.rem(p.x + second_off + 4, 4) * 4 + lax.rem(p.y + first_off + 4, 4)) * 64
        if part is None:
            return self.w.at[rows(start, 64), self.cols]
        return self.w.at[rows(start + 32 * part, 32), self.cols]

    def put(self, ref, device):
        return self.copies.put(ref, ref, device)

    def start(self):
        p = self.place
        mine = self.w.at[rows(p.dp * 32, 32), pl.ds(self.first, self.width)]
        self.swap = self.put(mine, p.at(flip=True))

    def spread(self, first_off):
        ref = self.block(first_off, 0)
        return (self.put(ref, self.dev(1, 1)), self.put(ref, self.dev(1, -1)))

    def share(self, first_off, second_off):
        self.shared.append(self.put(self.block(first_off, second_off), self.place.at(flip=True)))

    def step1(self):
        self.swap.wait_recv()
        ref = self.block(0, 0)
        self.shared = []
        self.up = self.put(ref, self.dev(0, 1))
        self.down = self.put(ref, self.dev(0, -1))
        self.out = {0: self.spread(0)}

    def step2(self):
        self.up.wait_recv()
        self.up2 = self.put(self.block(-1, 0, 0), self.dev(0, 1))
        self.down.wait_recv()
        self.down2 = self.put(self.block(1, 0, 1), self.dev(0, -1))
        self.out[-1] = self.spread(-1)
        self.out[1] = self.spread(1)
        self.share(-1, 0)
        self.share(1, 0)

    def step3(self):
        self.up2.wait_recv()
        self.down2.wait_recv()
        self.out[2] = self.spread(2)
        self.share(2, 0)

    def step4(self):
        self.far = []
        for first_off in (0, -1, 1, 2):
            up, down = self.out[first_off]
            up.wait_recv()
            self.far.append(self.put(self.block(first_off, -1, 0), self.dev(1, 1)))
            down.wait_recv()
            self.far.append(self.put(self.block(first_off, 1, 1), self.dev(1, -1)))
            self.share(first_off, -1)
            self.share(first_off, 1)

    def step5(self):
        for k, first_off in enumerate((0, -1, 1, 2)):
            self.far[2 * k].wait_recv()
            self.far[2 * k + 1].wait_recv()
            self.share(first_off, 2)

    def step6(self):
        for copy in self.shared:
            copy.wait_recv()


def normalised(values):
    centre = values - jnp.mean(values, axis=-1, keepdims=True)
    spread = jnp.mean(centre * centre, axis=-1, keepdims=True)
    scale = lax.rsqrt(spread + 1e-05)
    return centre * scale, scale


def first_blocks(lengths_ref):
    base = lax.axis_index("dp") * 4
    end = jnp.int32(0)
    first = [jnp.int32(0)] * 4
    for i in range(32):
        end = end + lengths_ref[i]
        first = [jnp.where(end <= base + b, end, first[b]) for b in range(4)]
    return [first[b] - base + 16 for b in range(4)]


def heads_across(tile):
    head = lax.broadcasted_iota(jnp.int32, tile.shape, 1) // HEAD_DIM
    return jnp.concatenate([jnp.where(head == h, tile, 0.0) for h in range(4)], axis=0)


def heads_together(tile):
    head = lax.broadcasted_iota(jnp.int32, (BLOCK, 256), 1) // HEAD_DIM
    return sum(jnp.where(head == h, tile[h * BLOCK:(h + 1) * BLOCK], 0.0) for h in range(4))


def causal(scores, b):
    query = lax.rem(lax.broadcasted_iota(jnp.int32, scores.shape, 0), BLOCK)
    key = lax.broadcasted_iota(jnp.int32, scores.shape, 1)
    return jnp.where(key <= query + b * BLOCK, scores, -1e30)


def outside(block, first):
    lane = lax.broadcasted_iota(jnp.int32, (1, SPAN), 1)
    return jnp.where(lane < (first - block) * BLOCK, -1e30, 0.0)


def parts(tile):
    return [tile[:, i * 128:(i + 1) * 128] for i in range(SPAN // 128)]


class Attention:
    def __init__(self, lengths_ref, q_ref, kv_ref, scratch):
        self.first = first_blocks(lengths_ref)
        self.q_ref, self.kv_ref = q_ref, kv_ref
        self.tall, self.top, self.total, self.acc = scratch

    @staticmethod
    def scratch():
        return [
            pltpu.VMEM((4, 512, 256), BF),
            pltpu.VMEM((4, 512, 128), F32),
            pltpu.VMEM((4, 512, 128), F32),
            pltpu.VMEM((4, 512, 256), F32),
        ]

    def start(self):
        for b in range(4):
            queries = self.q_ref[b * BLOCK:(b + 1) * BLOCK, :].astype(F32) * 0.125
            self.tall[b] = heads_across(queries).astype(BF)

    def add(self, slot, own=False):
        keys = rows(slot * GROUP, GROUP)
        for b in range(4):
            tile = nt(self.tall[b], self.kv_ref[keys, 0:256]) + outside(slot * 4, self.first[b])
            if own:
                tile = causal(tile, b)
            pieces = parts(tile)
            peak = jnp.max(functools.reduce(jnp.maximum, pieces), axis=1, keepdims=True)
            top = jnp.broadcast_to(peak, (512, 128))
            if not own:
                top = jnp.maximum(top, self.top[b])
            weights = [jnp.exp(piece - top) for piece in pieces]
            low = jnp.concatenate([piece.astype(BF) for piece in weights], axis=1)
            product = nn(low, self.kv_ref[keys, 256:512])
            if own:
                self.total[b] = sum(weights)
                self.acc[b] = product
            else:
                shrink = jnp.exp(self.top[b] - top)
                self.total[b] = self.total[b] * shrink + sum(weights)
                self.acc[b] = self.acc[b] * jnp.concatenate([shrink, shrink], axis=1) + product
            self.top[b] = top

    def finish(self, ctx_ref, lse_ref):
        for b in range(4):
            sums = jnp.sum(self.total[b], axis=1, keepdims=True)
            lse_ref[b] = self.top[b] + jnp.log(sums)
            ctx_ref[b * BLOCK:(b + 1) * BLOCK, :] = heads_together(self.acc[b] * (1.0 / sums)).astype(BF)


class AttentionBack:
    def __init__(self, lengths_ref, q_ref, kv_ref, ctx_ref, lse_ref, dctx_ref, scratch):
        self.first = first_blocks(lengths_ref)
        self.q_ref, self.kv_ref, self.ctx_ref = q_ref, kv_ref, ctx_ref
        self.lse_ref, self.dctx_ref = lse_ref, dctx_ref
        self.tall_q, self.tall_g, self.inner, self.acc = scratch

    @staticmethod
    def scratch():
        return [
            pltpu.VMEM((2048, 256), BF),
            pltpu.VMEM((2048, 256), BF),
            pltpu.VMEM((4, 512, 128), F32),
            pltpu.VMEM((4, 512, 256), F32),
        ]

    def start(self):
        for b in range(4):
            block, tall = slice(b * BLOCK, (b + 1) * BLOCK), slice(b * 512, (b + 1) * 512)
            grads = self.dctx_ref[block, :].astype(F32)
            self.tall_q[tall, :] = heads_across(self.q_ref[block, :].astype(F32) * 0.125).astype(BF)
            self.tall_g[tall, :] = heads_across(grads).astype(BF)
            product = heads_across(grads * self.ctx_ref[block, :].astype(F32))
            self.inner[b] = jnp.broadcast_to(jnp.sum(product, axis=1, keepdims=True), (512, 128))
            self.acc[b] = jnp.zeros((512, 256), F32)

    def add(self, slot, dkv, own=False):
        keys = rows(slot * GROUP, GROUP)
        low, weights = [], []
        for b in range(4):
            tall = slice(b * 512, (b + 1) * 512)
            tile = nt(self.tall_q[tall, :], self.kv_ref[keys, 0:256]) + outside(slot * 4, self.first[b])
            if own:
                tile = causal(tile, b)
            weight = jnp.exp(tile - jnp.concatenate([self.lse_ref[b]] * 4, axis=1))
            grad = nt(self.tall_g[tall, :], self.kv_ref[keys, 256:512])
            low.append((weight * (grad - jnp.concatenate([self.inner[b]] * 4, axis=1))).astype(BF))
            weights.append(weight.astype(BF))
            self.acc[b] += nn(low[b], self.kv_ref[keys, 0:256])
        dkv[keys, 0:256] = tn(jnp.concatenate(low, axis=0), self.tall_q[...]).astype(BF)
        dkv[keys, 256:512] = tn(jnp.concatenate(weights, axis=0), self.tall_g[...]).astype(BF)

    def finish(self, dq):
        for b in range(4):
            dq[b * BLOCK:(b + 1) * BLOCK, :] = heads_together(self.acc[b] * 0.125).astype(BF)


def one_hot(shape, offset):
    row = lax.broadcasted_iota(jnp.int32, shape, 0)
    lane = lax.broadcasted_iota(jnp.int32, shape, 1)
    return jnp.where(lane == row + offset, 1.0, 0.0).astype(F32)


def exact(a, b):
    return jnp.dot(a, b, precision=lax.Precision.HIGHEST, preferred_element_type=F32)


def first_kernel(
    lengths_ref, x_ref, cot_ref, wqkv_ref, wout_ref, wfc_ref, gains_ref, shifts_ref, bqv_ref, bfc_ref,
    q_ref, kv_ref, vec_ref, ctx_ref, lse_ref, n1_out, xg_out, cotg_out, wqkv_out, wo_out, wfc_out,
    n1, xg, cotg, wq, wo, wfc, vz, vall, bias, mid, out_sem, send_sem, recv_sem, *scratch,
):
    p = Place()
    mine = rows(p.dp * 32, 32)
    for j in range(3):
        wq[mine, j * 256:(j + 1) * 256] = wqkv_ref[j]
    wq[mine, 768:1024] = wout_ref[...]
    wfc[mine, :] = wfc_ref[...]
    xg[rows(p.z * BLOCK, BLOCK), :] = x_ref[...]
    cotg[rows(p.z * BLOCK, BLOCK), :] = cot_ref[...]
    place8 = one_hot((8, 128), lax.rem(p.dp * 4 + p.z, 16) * 8)
    own = vz.at[p.z]
    own[...] = jnp.zeros((8, 128), F32)
    own[0:2] = exact(gains_ref[...], place8)
    own[2:6] = exact(shifts_ref[...], place8)
    tile = vall.at[p.c, p.chip]
    tile[8:16] = jnp.zeros((8, 128), F32)
    tile[8:9] = exact(bfc_ref[...].astype(F32), one_hot((32, 128), lax.rem(p.dp, 4) * 32))
    tile[9:11] = exact(bqv_ref[...].astype(F32), one_hot((8, 128), lax.rem(p.dp, 16) * 8))
    greet(
        [p.at(dz=1), p.at(dz=-1), p.at(dz=2), p.at(dx=1), p.at(dx=-1), p.at(dx=2),
         p.at(dy=1), p.at(dy=-1), p.at(dy=2), p.at(flip=True), p.linear(1), p.linear(-1),
         p.beside(1, 2), p.beside_source()]
    )
    copies = Copies(send_sem, recv_sem)
    head = DirectGather(copies, p, wq)
    head.start()
    small = [copies.put(own, own, p.at(dz=dz)) for dz in (1, -1, 2)]
    ring = RingGather(copies, p, xg)
    ring.start()
    tail = PlaneGather(copies, p, wfc, 0, 1024)
    for copy in small:
        copy.wait_recv()
    tile[0:8] = vz[0] + vz[1] + vz[2] + vz[3]
    small = [copies.put(tile, tile, p.at(dy=dy)) for dy in (1, -1, 2)]
    head.step1()
    tail.start()
    for copy in small:
        copy.wait_recv()
    line = vall.at[p.c, rows(p.x * 4, 4)]
    small = [copies.put(line, line, p.at(dx=dx)) for dx in (1, -1, 2)]
    ring.below()
    ring.above()
    cot_ring = RingGather(copies, p, cotg)
    cot_ring.start()
    for copy in small:
        copy.wait_recv()
    plane = vall.at[p.c]
    last = copies.put(plane, plane, p.at(flip=True))
    head.step2()
    tail.step1()
    ring.far()
    last.wait_recv()
    lanes = []
    for k in range(8):
        total = vall[0, 2 * k] + vall[0, 2 * k + 1] + vall[1, 2 * k] + vall[1, 2 * k + 1]
        vec_ref[:, k * 128:(k + 1) * 128] = total
        lanes.append(total)
    for h in range(2):
        bias[:, h * 128:(h + 1) * 128] = lanes[4 * h] + lanes[4 * h + 1] + lanes[4 * h + 2] + lanes[4 * h + 3]

    def norm_block(k, carry):
        block = rows(lax.rem(p.z + k, 4) * BLOCK, BLOCK)
        hat, _ = normalised(xg[block, :].astype(F32))
        n1[block, :] = (hat * vec_ref[0:1, :] + vec_ref[2:3, :]).astype(BF)
        return carry

    lax.fori_loop(0, 4, norm_block, 0)
    cot_ring.below()
    cot_ring.above()
    head.step3()

    def start_of(k):
        return lax.rem(p.z + k, 4) * BLOCK

    sibling = p.at(flip=True)
    near, there, cross = {}, {}, []
    for pair in ((2, 0), (3, 1)):
        values = jnp.concatenate([n1[rows(start_of(k), BLOCK), :] for k in pair], axis=0)
        keys = nn(values, wq[:, 256:512]).astype(BF)
        vals = (nn(values, wq[:, 512:768]) + bias[10:11, :]).astype(BF)
        for i, k in enumerate(pair):
            ours = rows(4 * GROUP + start_of(k), BLOCK)
            kv_ref[ours, 0:256] = keys[i * BLOCK:(i + 1) * BLOCK]
            kv_ref[ours, 256:512] = vals[i * BLOCK:(i + 1) * BLOCK]
            if k < 2:
                there[k] = copies.put(kv_ref.at[ours], mid.at[k], p.at(dy=-1))
            else:
                near[k] = copies.put(
                    kv_ref.at[ours], kv_ref.at[rows(2 * GROUP + start_of(k), BLOCK)], p.linear(1)
                )
    for k in (0, 1):
        ours = kv_ref.at[rows(4 * GROUP + start_of(k), BLOCK)]
        near[k] = copies.put(ours, kv_ref.at[rows(2 * GROUP + start_of(k), BLOCK)], p.linear(1))
    wo[rows(p.z * D, D), :] = wq[:, 768:1024]
    wo_ring = RingGather(copies, p, wo, D)
    wo_ring.start()
    tail.step2()
    q_ref[...] = (nn(n1[...], wq[:, 0:256]) + bias[9:10, :]).astype(BF)
    saves = [
        pltpu.make_async_copy(source, target, out_sem.at[i])
        for i, (source, target) in enumerate(
            (
                (n1, n1_out), (xg, xg_out), (wq.at[:, 0:768], wqkv_out), (cotg, cotg_out),
                (wo, wo_out), (wfc, wfc_out),
            )
        )
    ]
    for i in range(3):
        saves[i].start()
    heads = Attention(lengths_ref, q_ref, kv_ref, scratch)
    heads.start()
    heads.add(4, own=True)
    far = {}
    for k in (0, 1):
        there[k].wait_recv()
        far[k] = copies.put(mid.at[k], kv_ref.at[rows(start_of(k), BLOCK)], p.beside(1, 2))

    def pass_near(k, onward):
        near[k].wait_recv()
        ref = kv_ref.at[rows(2 * GROUP + start_of(k), BLOCK)]
        if onward:
            far[k] = copies.put(ref, kv_ref.at[rows(start_of(k), BLOCK)], p.linear(1))
        cross.append(
            copies.put(ref, kv_ref.at[rows((1 + 2 * p.c) * GROUP + start_of(k), BLOCK)], sibling)
        )

    pass_near(2, True)
    pass_near(3, True)
    tail.step3()
    cot_ring.far()
    saves[3].start()
    tail.step4()
    pass_near(0, False)
    pass_near(1, False)
    wo_ring.below()
    wo_ring.above()

    def pass_far(k):
        far[k].wait_recv()
        cross.append(
            copies.put(
                kv_ref.at[rows((4 - 4 * p.c) * GROUP + start_of(k), BLOCK)],
                kv_ref.at[rows((3 - 2 * p.c) * GROUP + start_of(k), BLOCK)],
                sibling,
            )
        )

    heads.add(2)
    pass_far(0)
    pass_far(1)
    tail.step5()
    for copy in cross[:4]:
        copy.wait_recv()
    heads.add(3 - 2 * p.c)
    pass_far(2)
    pass_far(3)
    tail.step6()
    saves[5].start()
    heads.add(0)
    wo_ring.far()
    saves[4].start()
    for copy in cross[4:]:
        copy.wait_recv()
    heads.add(1 + 2 * p.c)
    heads.finish(ctx_ref, lse_ref)
    for save in saves:
        save.wait()
    copies.finish()


N1_COPIES = 31 + 36 + 10 + 12 + 18


def vm(count):
    return [pl.BlockSpec(memory_space=pltpu.VMEM)] * count


def far_memory(count):
    return [pl.BlockSpec(memory_space=pl.ANY)] * count


def call_first(*operands):
    shape = jax.ShapeDtypeStruct
    return pl.pallas_call(
        first_kernel,
        out_shape=(
            shape((GROUP, 256), BF),
            shape((5 * GROUP, 512), BF),
            shape((16, D), F32),
            shape((GROUP, 256), BF),
            shape((4, 512, 128), F32),
            shape((GROUP, D), BF),
            shape((GROUP, D), BF),
            shape((GROUP, D), BF),
            shape((D, 768), BF),
            shape((4 * D, 256), BF),
            shape((D, D), BF),
        ),
        in_specs=[pl.BlockSpec(memory_space=pltpu.SMEM)] + vm(9),
        out_specs=tuple(vm(5) + far_memory(6)),
        scratch_shapes=[
            pltpu.VMEM((GROUP, D), BF),
            pltpu.VMEM((GROUP, D), BF),
            pltpu.VMEM((GROUP, D), BF),
            pltpu.VMEM((D, 1024), BF),
            pltpu.VMEM((4 * D, 256), BF),
            pltpu.VMEM((D, D), BF),
            pltpu.VMEM((4, 8, 128), F32),
            pltpu.VMEM((2, 16, 16, 128), F32),
            pltpu.VMEM((16, 256), F32),
            pltpu.VMEM((2, BLOCK, 512), BF),
            pltpu.SemaphoreType.DMA((6,)),
            pltpu.SemaphoreType.DMA((N1_COPIES,)),
            pltpu.SemaphoreType.DMA((N1_COPIES,)),
            *Attention.scratch(),
        ],
        compiler_params=pltpu.CompilerParams(
            collective_id=1, has_side_effects=True, vmem_limit_bytes=VMEM_LIMIT
        ),
        name="gather_and_project",
    )(*operands)


class PlaneScatter:
    copies_needed = 18

    def __init__(self, copies, place, g, scratch):
        self.copies, self.place, self.g = copies, place, g
        self.land, self.far, self.near, self.t, self.far2, self.near2, self.last, self.rest = scratch
        self.half = g.shape[1] // 2

    @staticmethod
    def scratch(width):
        half = width // 2
        return [
            pltpu.VMEM((1024, half), BF),
            pltpu.VMEM((2, 2, 64, half), BF),
            pltpu.VMEM((2, 4, 64, half), BF),
            pltpu.VMEM((4, 64, half), BF),
            pltpu.VMEM((2, 32, half), BF),
            pltpu.VMEM((2, 64, half), BF),
            pltpu.VMEM((32, half), F32),
            pltpu.VMEM((32, half), F32),
        ]

    def dev(self, axis, step):
        c = self.place.c
        if axis == 0:
            return self.place.at(dx=(1 - c) * step, dy=c * step)
        return self.place.at(dx=c * step, dy=(1 - c) * step)

    def first(self, step):
        p = self.place
        return lax.rem(p.x * (1 - p.c) + p.y * p.c + step + 4, 4)

    def second(self, step):
        p = self.place
        return lax.rem(p.y * (1 - p.c) + p.x * p.c + step + 4, 4)

    def block(self, f, s):
        c = self.place.c
        x, y = f * (1 - c) + s * c, s * (1 - c) + f * c
        return rows((x * 4 + y) * 64, 64)

    def start(self):
        c = self.place.c
        other = pl.ds(pl.multiple_of((1 - c) * self.half, 128), self.half)
        self.swap = self.copies.put(self.g.at[:, other], self.land, self.place.at(flip=True))

    def step1(self):
        self.swap.wait_recv()
        mine = pl.ds(pl.multiple_of(self.place.c * self.half, 128), self.half)
        self.mine = mine

        def join(k, carry):
            f = self.first(2 + k // 4)
            block = self.block(f, lax.rem(k, 4))
            self.land[block, :] = (self.land[block, :].astype(F32) + self.g[block, mine].astype(F32)).astype(BF)
            return carry

        lax.fori_loop(0, 4, join, 0)
        self.out = []
        for s in range(4):
            to = self.dev(0, 1 if s < 2 else -1)
            self.out.append(
                self.copies.put(self.land.at[self.block(self.first(2), s)], self.far.at[s // 2, s % 2], to)
            )
        lax.fori_loop(4, 16, join, 0)

    def step2(self):
        self.out2 = []
        for side, step in ((0, 1), (1, -1)):
            f = self.first(step)
            for s in range(4):
                block = self.block(f, s)
                if s // 2 == side:
                    self.out[s].wait_recv()
                    self.land[block, :] = (
                        self.land[block, :].astype(F32) + self.far[side, s % 2].astype(F32)
                    ).astype(BF)
                self.out2.append(
                    self.copies.put(self.land.at[block], self.near.at[side, s], self.dev(0, step))
                )

    def step3(self):
        f = self.first(0)
        for copy in self.out2:
            copy.wait_recv()

        def total(k, carry):
            s = self.second(2 + k)
            self.t[s] = (
                self.land[self.block(f, s), :].astype(F32)
                + self.near[0, s].astype(F32)
                + self.near[1, s].astype(F32)
            ).astype(BF)
            return carry

        lax.fori_loop(0, 1, total, 0)
        s = self.second(2)
        self.up = self.copies.put(self.t.at[s, 0:32], self.far2.at[0], self.dev(1, 1))
        self.down = self.copies.put(self.t.at[s, 32:64], self.far2.at[1], self.dev(1, -1))
        lax.fori_loop(1, 4, total, 0)

    def step4(self):
        s = self.second(1)
        self.up.wait_recv()
        self.t[s, 0:32] = (self.t[s, 0:32].astype(F32) + self.far2[0].astype(F32)).astype(BF)
        self.up2 = self.copies.put(self.t.at[s], self.near2.at[0], self.dev(1, 1))
        s = self.second(-1)
        self.down.wait_recv()
        self.t[s, 32:64] = (self.t[s, 32:64].astype(F32) + self.far2[1].astype(F32)).astype(BF)
        self.down2 = self.copies.put(self.t.at[s], self.near2.at[1], self.dev(1, -1))

    def part(self, c):
        half = rows(c * 32, 32)
        return (
            self.t[self.second(0), half].astype(F32)
            + self.near2[0, half].astype(F32)
            + self.near2[1, half].astype(F32)
        )

    def step5(self):
        self.up2.wait_recv()
        self.down2.wait_recv()
        c = self.place.c
        self.last[...] = self.part(1 - c)
        self.back = self.copies.put(self.last, self.rest, self.place.at(flip=True))

    def step6(self, out):
        out[:, self.mine] = self.part(self.place.c)
        self.back.wait_recv()
        other = pl.ds(pl.multiple_of((1 - self.place.c) * self.half, 128), self.half)
        out[:, other] = self.rest[...]


class QuickScatter:
    copies_needed = 17

    def __init__(self, copies, place, g, scratch):
        self.copies, self.place, self.g = copies, place, g
        self.land, self.near, self.t, self.near2, self.last, self.rest = scratch
        self.half = g.shape[1] // 2

    @staticmethod
    def scratch(width):
        half = width // 2
        return [
            pltpu.VMEM((1024, half), BF),
            pltpu.VMEM((3, 4, 64, half), BF),
            pltpu.VMEM((4, 64, half), BF),
            pltpu.VMEM((3, 64, half), BF),
            pltpu.VMEM((32, half), F32),
            pltpu.VMEM((32, half), F32),
        ]

    dev, first, second, block, start = (
        PlaneScatter.dev, PlaneScatter.first, PlaneScatter.second, PlaneScatter.block, PlaneScatter.start
    )

    def step1(self):
        self.swap.wait_recv()
        self.mine = pl.ds(pl.multiple_of(self.place.c * self.half, 128), self.half)
        self.out = []
        for i, step in enumerate((2, 1, -1, 0)):
            f = self.first(step)

            def join(s, carry):
                block = self.block(f, s)
                self.land[block, :] = (
                    self.land[block, :].astype(F32) + self.g[block, self.mine].astype(F32)
                ).astype(BF)
                return carry

            lax.fori_loop(0, 4, join, 0)
            if step:
                for s in range(4):
                    self.out.append(
                        self.copies.put(self.land.at[self.block(f, s)], self.near.at[i, s], self.dev(0, step))
                    )

    def step2(self):
        for copy in self.out:
            copy.wait_recv()
        f = self.first(0)

        def total(s, carry):
            value = self.land[self.block(f, s), :].astype(F32)
            for i in range(3):
                value = value + self.near[i, s].astype(F32)
            self.t[s] = value.astype(BF)
            return carry

        lax.fori_loop(0, 4, total, 0)
        self.out2 = [
            self.copies.put(self.t.at[self.second(step)], self.near2.at[i], self.dev(1, step))
            for i, step in enumerate((2, 1, -1))
        ]

    def part(self, c):
        half = rows(c * 32, 32)
        value = self.t[self.second(0), half].astype(F32)
        for i in range(3):
            value = value + self.near2[i, half].astype(F32)
        return value

    def step3(self):
        for copy in self.out2:
            copy.wait_recv()
        self.last[...] = self.part(1 - self.place.c)
        self.back = self.copies.put(self.last, self.rest, self.place.at(flip=True))

    step4 = PlaneScatter.step6


class RingScatter:
    copies_needed = 4

    def __init__(self, copies, place, scratch):
        self.copies, self.place = copies, place
        self.part, self.far, self.near = scratch

    @staticmethod
    def scratch():
        return [
            pltpu.VMEM((3, BLOCK, D), BF),
            pltpu.VMEM((2, 64, D), BF),
            pltpu.VMEM((2, BLOCK, D), BF),
        ]

    def send_far(self):
        p, c = self.place, self.copies
        self.up = c.put(self.part.at[2, 0:64], self.far.at[0], p.at(dz=1))
        self.down = c.put(self.part.at[2, 64:128], self.far.at[1], p.at(dz=-1))

    def send_above(self):
        self.up.wait_recv()
        self.part[0, 0:64] = (self.part[0, 0:64].astype(F32) + self.far[0].astype(F32)).astype(BF)
        self.up2 = self.copies.put(self.part.at[0], self.near.at[0], self.place.at(dz=1))

    def send_below(self):
        self.down.wait_recv()
        self.part[1, 64:128] = (self.part[1, 64:128].astype(F32) + self.far[1].astype(F32)).astype(BF)
        self.down2 = self.copies.put(self.part.at[1], self.near.at[1], self.place.at(dz=-1))

    def received(self):
        self.up2.wait_recv()
        self.down2.wait_recv()
        return self.near[0].astype(F32) + self.near[1].astype(F32)


class RingReturn:
    copies_needed = 6

    def __init__(self, copies, place, scratch):
        self.copies, self.place = copies, place
        self.above, self.below, self.across, self.near, self.mid, self.far = scratch

    @staticmethod
    def scratch():
        return [
            pltpu.VMEM((2, BLOCK, D), BF),
            pltpu.VMEM((2, 64, D), BF),
            pltpu.VMEM((BLOCK, D), BF),
        ]

    def send_above(self):
        self.up = self.copies.put(self.above, self.near.at[0], self.place.at(dz=1))

    def send_below(self):
        self.down = self.copies.put(self.below, self.near.at[1], self.place.at(dz=-1))

    def send_far(self):
        p, c = self.place, self.copies
        self.up1 = c.put(self.across.at[0:64], self.mid.at[0], p.at(dz=1))
        self.down1 = c.put(self.across.at[64:128], self.mid.at[1], p.at(dz=-1))

    def pass_on(self):
        p, c = self.place, self.copies
        self.up1.wait_recv()
        self.up2 = c.put(self.mid.at[0], self.far.at[0:64], p.at(dz=1))
        self.down1.wait_recv()
        self.down2 = c.put(self.mid.at[1], self.far.at[64:128], p.at(dz=-1))

    def received(self):
        for copy in (self.up, self.down, self.up2, self.down2):
            copy.wait_recv()
        return self.near[0].astype(F32) + self.near[1].astype(F32) + self.far[...].astype(F32)


def norm_back(hat, scale, grad, gain):
    inner = grad * gain
    mean = jnp.mean(inner, axis=-1, keepdims=True)
    along = jnp.mean(inner * hat, axis=-1, keepdims=True)
    return (
        scale * (inner - mean - hat * along),
        jnp.sum(grad * hat, axis=0, keepdims=True),
        jnp.sum(grad, axis=0, keepdims=True),
    )


def weight_grad(left, right, out, first):
    width = right.shape[1]

    def tile(k, carry):
        turned = left[:, pl.ds(pl.multiple_of(k * 256, 256), 256)].astype(F32).T.astype(BF)
        out[rows(k * 256, 256), first:first + width] = nn(turned, right[...]).astype(BF)
        return carry

    lax.fori_loop(0, 4, tile, 0)


def middle_kernel(
    x_ref, ctx_ref, vec_ref, wproj_ref, wo_any, wfc_any, cotg_any,
    gafter_ref, gaf_ref, dctx_ref, sums_ref, res_ref, outs_ref, dw_any,
    wo, wfc, wproj, cotg, ctxf, n2g, act, dpre, dact, part, back, own, after, dw, dctx, io_sem, send_sem, recv_sem,
    *scratch,
):
    p = Place()
    loads = [
        pltpu.make_async_copy(source, target, io_sem.at[i])
        for i, (source, target) in enumerate(((wo_any, wo), (cotg_any, cotg), (wfc_any, wfc)))
    ]
    for load in loads:
        load.start()
    wproj[rows(p.dp * 32, 32), :] = wproj_ref[...]
    greet(
        [p.at(dz=1), p.at(dz=-1), p.at(dz=2), p.at(dx=1), p.at(dx=-1), p.at(dx=2),
         p.at(dy=1), p.at(dy=-1), p.at(dy=2), p.at(flip=True)]
    )
    copies = Copies(send_sem, recv_sem)
    backs = RingReturn(copies, p, (part.at[0], part.at[1], part.at[2]) + scratch)

    def block(dz):
        return rows(lax.rem(p.z + dz + 4, 4) * BLOCK, BLOCK)

    swaps = [
        copies.put(ctx_ref.at[block(dz)], ctxf.at[p.z], p.at(dz=dz)) for dz in (2, 1, -1)
    ]
    plane = DirectGather(copies, p, wproj)
    plane.start()
    ctxf[p.z] = ctx_ref[block(0), :]
    for load in loads:
        load.wait()

    plane.step1()
    for copy in swaps:
        copy.wait_recv()
    total = x_ref[...].astype(F32) + vec_ref[4:5, :]
    for k in range(4):
        total = total + nt(ctxf[k], wo[k * D:(k + 1) * D, :])
    after[...] = total
    hat, scale = normalised(after[...])
    n2g[block(0), :] = (hat * vec_ref[1:2, :] + vec_ref[3:4, :]).astype(BF)
    ring = RingGather(copies, p, n2g)
    ring.start()
    plane.step2()
    plane.step3()

    def act_grad(t, carry):
        cols = pl.ds(pl.multiple_of(t * 256, 256), 256)
        dact[:, cols] = nn(cotg[...], wproj[:, cols])
        return carry

    lax.fori_loop(0, 4, act_grad, 0)

    def mlp(pair, put_back):
        here = [block(dz) for dz in pair]

        def both(ref, cols=slice(None)):
            return jnp.concatenate([ref[h, cols] for h in here], axis=0)

        def hidden(t, carry):
            cols = pl.ds(pl.multiple_of(t * 256, 256), 256)
            pre = nn(both(n2g), wfc[:, cols]) + vec_ref[8:9, cols]
            square = pre * pre
            bend = jnp.tanh(0.7978845608028654 * pre * (1.0 + 0.044715 * square))
            slope = 0.5 * (1.0 + bend) + 0.5 * pre * (1.0 - bend * bend) * (
                0.7978845608028654 * (1.0 + 0.134145 * square)
            )
            value = (0.5 * pre * (1.0 + bend)).astype(BF)
            grad = (both(dact, cols) * slope).astype(BF)
            for i, h in enumerate(here):
                act[h, cols] = value[i * BLOCK:(i + 1) * BLOCK]
                dpre[h, cols] = grad[i * BLOCK:(i + 1) * BLOCK]
            return carry

        lax.fori_loop(0, 4, hidden, 0)

        def project(t, carry):
            cols = pl.ds(pl.multiple_of(t * 256, 256), 256)
            value = nt(both(dpre), wfc[cols, :])
            for i in range(2):
                put_back[i](cols, value[i * BLOCK:(i + 1) * BLOCK])
            return carry

        lax.fori_loop(0, 4, project, 0)

    def into(i):
        def put(cols, value):
            part[i, :, cols] = value.astype(BF)

        return put

    def keep(cols, value):
        own[:, cols] = value

    ring.below()
    ring.above()
    mlp((1, -1), (into(0), into(1)))
    backs.send_above()
    backs.send_below()
    ring.far()
    mlp((2, 0), (into(2), keep))
    backs.send_far()
    weight_grad(n2g, dpre, dw, 0)
    backs.pass_on()
    weight_grad(cotg, act, dw, 1024)
    save = pltpu.make_async_copy(dw, dw_any, io_sem.at[3])
    save.start()
    def output_part(t, carry):
        cols = pl.ds(pl.multiple_of(t * 256, 256), 256)
        outs_ref[:, cols] = nt(act[...], wproj[cols, :]).astype(BF)
        return carry

    lax.fori_loop(0, 4, output_part, 0)
    res_ref[...] = after[...] + vec_ref[5:6, :]
    grad = own[...] + backs.received()
    hat, scale = normalised(after[...])
    grad_in, gain, shift = norm_back(hat, scale, grad, vec_ref[1:2, :])
    residual = cotg[block(0), :].astype(F32)
    back[...] = grad_in + residual
    gaf_ref[...] = back[...].astype(BF)
    for k in (2, 1, 3, 0):
        owner = lax.rem(p.z + k, 4)
        part = nn(gaf_ref[...], wo[rows(owner * D, D), :]).astype(BF)
        if k:
            dctx[k] = part
            swaps.append(copies.put(dctx.at[k], dctx_ref.at[block(0)], p.at(dz=k)))
        else:
            dctx_ref[block(0), :] = part
    sums_ref[...] = jnp.zeros_like(sums_ref)
    sums_ref[0:1, :] = gain
    sums_ref[1:2, :] = shift
    sums_ref[2:3, :] = jnp.sum(back[...], axis=0, keepdims=True)
    sums_ref[3:4, :] = jnp.sum(residual, axis=0, keepdims=True)
    sums_ref[4:5, :] = jnp.sum(dpre[...].astype(F32), axis=0, keepdims=True)
    gafter_ref[...] = back[...]

    for copy in swaps[3:]:
        copy.wait_recv()
    save.wait()
    copies.finish()


N3_COPIES = 6 + 4 + 6 + 31


def call_middle(*operands):
    shape = jax.ShapeDtypeStruct
    return pl.pallas_call(
        middle_kernel,
        out_shape=(
            shape((BLOCK, D), F32),
            shape((BLOCK, D), BF),
            shape((GROUP, 256), BF),
            shape((8, D), F32),
            shape((BLOCK, D), F32),
            shape((GROUP, D), BF),
            shape((D, 2048), BF),
        ),
        in_specs=vm(4) + far_memory(3),
        out_specs=tuple(vm(6) + far_memory(1)),
        scratch_shapes=[
            pltpu.VMEM((4 * D, 256), BF),
            pltpu.VMEM((D, D), BF),
            pltpu.VMEM((D, D), BF),
            pltpu.VMEM((GROUP, D), BF),
            pltpu.VMEM((4, BLOCK, 256), BF),
            pltpu.VMEM((GROUP, D), BF),
            pltpu.VMEM((GROUP, D), BF),
            pltpu.VMEM((GROUP, D), BF),
            pltpu.VMEM((GROUP, D), F32),
            pltpu.VMEM((3, BLOCK, D), BF),
            pltpu.VMEM((BLOCK, D), F32),
            pltpu.VMEM((BLOCK, D), F32),
            pltpu.VMEM((BLOCK, D), F32),
            pltpu.VMEM((D, 2048), BF),
            pltpu.VMEM((4, BLOCK, 256), BF),
            pltpu.SemaphoreType.DMA((4,)),
            pltpu.SemaphoreType.DMA((N3_COPIES,)),
            pltpu.SemaphoreType.DMA((N3_COPIES,)),
            *RingReturn.scratch(),
        ],
        compiler_params=pltpu.CompilerParams(
            collective_id=2, has_side_effects=True, vmem_limit_bytes=VMEM_LIMIT
        ),
        name="mlp_both_ways",
    )(*operands)


def last_kernel(
    lengths_ref, q_ref, kv_ref, lse_ref, dctx_ref, x_ref, vec_ref, gafter_ref, gaf_ref, ctx_ref, sums_ref, res_ref, outs_ref,
    n1_any, xg_any, wqkv_any, dw_any,
    gin_ref, out_ref, early_ref, late_ref, sums_out,
    dq, dkv, n1, xg, wqkv, gafg, cross, hand, land, mid, fin, dqkv, early, late, own, hats, small_ref, xsum, ysum, zsum, line,
    io_sem, send_sem, recv_sem, *scratch,
):
    p = Place()
    loads = [
        pltpu.make_async_copy(source, target, io_sem.at[i])
        for i, (source, target) in enumerate(
            ((dw_any, early), (n1_any, n1), (wqkv_any, wqkv), (xg_any, xg))
        )
    ]
    for load in loads:
        load.start()
    gafg[rows(p.z * BLOCK, BLOCK), :] = gaf_ref[...]
    greet(
        [p.at(dz=1), p.at(dz=-1), p.at(dz=2), p.at(dx=1), p.at(dx=-1), p.at(dx=2),
         p.at(dy=1), p.at(dy=-1), p.at(dy=2), p.at(flip=True), p.linear(1), p.linear(-1),
         p.at(dy=1, flip=True), p.at(dy=-1, flip=True), p.at(dy=2, flip=True),
         p.beside(-1, -2), p.beside_source(-2, 1)]
    )
    copies = Copies(send_sem, recv_sem)
    scatter = RingScatter(copies, p, scratch[0:3])
    plane = PlaneScatter(copies, p, early, scratch[6:14])
    quick = QuickScatter(copies, p, late, scratch[14:20])
    sibling = p.at(flip=True)
    even = p.c == 0

    def start_of(k):
        return lax.rem(p.z + k, 4) * BLOCK

    def block(k):
        return rows(start_of(k), BLOCK)

    outs = RingReturn(
        copies, p, (outs_ref.at[block(1)], outs_ref.at[block(3)], outs_ref.at[block(2)]) + scratch[3:6]
    )

    def spread_bias(row, value):
        for half in range(2):
            for k in range(4):
                first = (4 * half + k) * 128
                small_ref[row:row + 1, first:first + 128] = value[:, half * 128:(half + 1) * 128]

    order = (2, 1, 3, 0)
    ring = RingGather(copies, p, gafg)
    ring.start()
    outs.send_above()
    outs.send_below()
    outs.send_far()
    for load in loads:
        load.wait()
    plane.start()
    heads = AttentionBack(lengths_ref, q_ref, kv_ref, ctx_ref, lse_ref, dctx_ref, scratch[20:24])
    heads.start()

    def cross_over(side):
        ref = dkv.at[rows((1 + 2 * side) * GROUP, GROUP)]
        return copies.put(ref, cross.at[side], sibling)

    heads.add(1, dkv)
    low = cross_over(0)
    heads.add(0, dkv)
    low.wait_recv()
    far, near = {}, {}
    for k in (3, 2, 0, 1):
        i = order.index(k)
        hand[0, block(k)] = (
            dkv[rows(start_of(k), BLOCK), :].astype(F32) + jnp.where(even, 0.0, cross[0, block(k)].astype(F32))
        ).astype(BF)
        if i < 2:
            far[k] = copies.put(hand.at[0, block(k)], mid.at[i], p.at(dy=1))
        else:
            far[k] = copies.put(hand.at[0, block(k)], land.at[0, block(k)], p.linear(-1))
    heads.add(3, dkv)
    high = cross_over(1)
    plane.step1()
    for i, k in enumerate(order[:2]):
        far[k].wait_recv()
        far[k] = copies.put(mid.at[i], fin.at[i], p.beside(-1, -2))
    heads.add(2, dkv)
    high.wait_recv()

    def near_sum(k):
        beside = jnp.where(even, cross[0, block(k)].astype(F32), cross[1, block(k)].astype(F32))
        return dkv[rows(2 * GROUP + start_of(k), BLOCK), :].astype(F32) + beside

    for k in order[:2]:
        hand[1, block(k)] = near_sum(k).astype(BF)
        near[k] = copies.put(hand.at[1, block(k)], land.at[1, block(k)], p.linear(-1))
    for k in order[2:]:
        far[k].wait_recv()
        hand[1, block(k)] = (near_sum(k) + land[0, block(k)].astype(F32)).astype(BF)
        near[k] = copies.put(hand.at[1, block(k)], land.at[1, block(k)], p.linear(-1))
    plane.step2()
    heads.add(4, dkv, own=True)
    heads.finish(dq)
    dqkv[:, 0:256] = dq[...]
    ring.below()
    ring.above()
    outs.pass_on()
    ring.far()
    weight_grad(gafg, ctx_ref, late, 768)
    small_ref[...] = jnp.zeros_like(small_ref)
    small_ref[8:9, :] = sums_ref[4:5, :]
    spread_bias(9, jnp.sum(dq[...].astype(F32), axis=0, keepdims=True))
    small_ref[1:2, :] = sums_ref[0:1, :]
    small_ref[3:6, :] = sums_ref[1:4, :]
    out_ref[...] = res_ref[...] + outs_ref[block(0), :].astype(F32) + outs.received()

    def keep_hat(k, carry):
        here = rows(k * BLOCK, BLOCK)
        hats[here, :], _ = normalised(xg[here, :].astype(F32))
        return carry

    lax.fori_loop(0, 4, keep_hat, 0)
    for k in order:
        near[k].wait_recv()
        value = dkv[rows(4 * GROUP + start_of(k), BLOCK), :].astype(F32) + land[1, block(k)].astype(F32)
        value = value + jnp.where(even, cross[1, block(k)].astype(F32), 0.0)
        if k in order[:2]:
            far[k].wait_recv()
            value = value + fin[order.index(k)].astype(F32)
        dqkv[block(k), 256:768] = value.astype(BF)
    weight_grad(n1, dqkv, late, 0)
    quick.start()

    def grad_parts(first, second):
        grad = nt(jnp.concatenate([dqkv[block(first), :], dqkv[block(second), :]], axis=0), wqkv[...])
        return grad[0:BLOCK], grad[BLOCK:2 * BLOCK]

    def tally(k, grad):
        small_ref[0:1, :] += jnp.sum(grad * hats[block(k), :], axis=0, keepdims=True)
        small_ref[2:3, :] += jnp.sum(grad, axis=0, keepdims=True)

    across, above = grad_parts(2, 1)
    scatter.part[2] = across.astype(BF)
    scatter.send_far()
    scatter.part[0] = above.astype(BF)
    tally(2, across)
    tally(1, above)
    below, here = grad_parts(3, 0)
    scatter.part[1] = below.astype(BF)
    own[...] = here
    tally(3, below)
    tally(0, here)
    spread_bias(10, jnp.sum(dqkv[:, 512:768].astype(F32), axis=0, keepdims=True))

    def lanes(x, width):
        return pl.ds(pl.multiple_of(x * width, 128), width)

    sends = []
    for i, dx in enumerate((1, -1, 2)):
        to = lax.rem(p.x + dx + 4, 4)
        sends.append(copies.put(small_ref.at[:, lanes(to, 256)], xsum.at[i], p.at(dx=dx)))
    scatter.send_above()
    scatter.send_below()
    quick.step1()
    for copy in sends:
        copy.wait_recv()
    line[...] = small_ref[:, lanes(p.x, 256)] + xsum[0] + xsum[1] + xsum[2]
    sends = []
    for dy in (0, 1, -1, 2):
        for flip in (False, True):
            if dy or flip:
                to = lax.rem(p.y + dy + 4, 4) // 2
                sends.append(
                    copies.put(line.at[:, lanes(to, 128)], ysum.at[len(sends)], p.at(dy=dy, flip=flip))
                )
    plane.step3()
    hat, scale = normalised(x_ref[...].astype(F32))
    back, _, _ = norm_back(hat, scale, own[...] + scatter.received(), vec_ref[0:1, :])
    gin_ref[...] = gafter_ref[...] + back
    quick.step2()
    for copy in sends:
        copy.wait_recv()
    total = line[:, lanes(p.y // 2, 128)]
    for i in range(7):
        total = total + ysum[i]
    zsum[3] = total
    sends = [copies.put(zsum.at[3, 0:8], zsum.at[i, 0:8], p.at(dz=dz)) for i, dz in enumerate((1, -1, 2))]
    plane.step4()
    quick.step3()
    plane.step5()
    for copy in sends:
        copy.wait_recv()
    sums_out[0:8] = zsum[3, 0:8] + zsum[0, 0:8] + zsum[1, 0:8] + zsum[2, 0:8]
    sums_out[8:16] = zsum[3, 8:16]
    quick.step4(late_ref)
    plane.step6(early_ref)
    copies.finish()


N5_COPIES = 2 + 4 + 6 + 4 + 4 + 2 + 4 + 18 + 17 + 3 + 7 + 3


def call_last(*operands):
    shape = jax.ShapeDtypeStruct
    return pl.pallas_call(
        last_kernel,
        out_shape=(
            shape((BLOCK, D), F32),
            shape((BLOCK, D), F32),
            shape((32, 2048), F32),
            shape((32, 1024), F32),
            shape((16, 128), F32),
        ),
        in_specs=[pl.BlockSpec(memory_space=pltpu.SMEM)] + vm(12) + far_memory(4),
        out_specs=tuple(vm(5)),
        scratch_shapes=[
            pltpu.VMEM((GROUP, 256), BF),
            pltpu.VMEM((5 * GROUP, 512), BF),
            pltpu.VMEM((GROUP, D), BF),
            pltpu.VMEM((GROUP, D), BF),
            pltpu.VMEM((D, 768), BF),
            pltpu.VMEM((GROUP, D), BF),
            pltpu.VMEM((2, GROUP, 512), BF),
            pltpu.VMEM((2, GROUP, 512), BF),
            pltpu.VMEM((2, GROUP, 512), BF),
            pltpu.VMEM((2, BLOCK, 512), BF),
            pltpu.VMEM((2, BLOCK, 512), BF),
            pltpu.VMEM((GROUP, 768), BF),
            pltpu.VMEM((D, 2048), BF),
            pltpu.VMEM((D, 1024), BF),
            pltpu.VMEM((BLOCK, D), F32),
            pltpu.VMEM((GROUP, D), F32),
            pltpu.VMEM((16, D), F32),
            pltpu.VMEM((3, 16, 256), F32),
            pltpu.VMEM((7, 16, 128), F32),
            pltpu.VMEM((4, 16, 128), F32),
            pltpu.VMEM((16, 256), F32),
            pltpu.SemaphoreType.DMA((4,)),
            pltpu.SemaphoreType.DMA((N5_COPIES,)),
            pltpu.SemaphoreType.DMA((N5_COPIES,)),
            *RingScatter.scratch(),
            *RingReturn.scratch(),
            *PlaneScatter.scratch(2048),
            *QuickScatter.scratch(1024),
            *AttentionBack.scratch(),
        ],
        compiler_params=pltpu.CompilerParams(
            collective_id=3, has_side_effects=True, vmem_limit_bytes=VMEM_LIMIT
        ),
        name="project_back",
    )(*operands)


def finish_kernel(
    out_ref, gin_ref, early_ref, late_ref, small_ref,
    out, gin, wqkv, wout, wfc, wproj, bqv, bfc, gains, shifts,
):
    dp, z = lax.axis_index("dp"), lax.axis_index("tensor")
    out[...] = out_ref[...]
    gin[...] = gin_ref[...]
    for j in range(3):
        wqkv[j] = late_ref[:, j * 256:(j + 1) * 256]
    wout[...] = late_ref[:, 768:1024]
    wfc[...] = early_ref[:, 0:1024]
    wproj[...] = early_ref[:, 1024:2048]

    def pick(first, offset, width):
        row = lax.broadcasted_iota(jnp.int32, (128, 128), 0)
        lane = lax.broadcasted_iota(jnp.int32, (128, 128), 1)
        chosen = jnp.where(row == lane + lax.rem(offset, 128), 1.0, 0.0).astype(F32)
        return exact(small_ref[first:first + 8, :], chosen)[:, 0:width]

    eight = pick(0, (dp * 4 + z) * 8, 8)
    gains[...] = eight[0:2]
    shifts[...] = eight[2:6]
    bqv[...] = pick(8, dp * 8, 8)[1:3]
    bfc[...] = pick(8, dp * 32, 32)[0:1]


def call_finish(*operands):
    shape = jax.ShapeDtypeStruct
    return pl.pallas_call(
        finish_kernel,
        out_shape=(
            shape((BLOCK, D), F32),
            shape((BLOCK, D), F32),
            shape((3, 32, 256), F32),
            shape((32, 256), F32),
            shape((32, 1024), F32),
            shape((32, 1024), F32),
            shape((2, 8), F32),
            shape((1, 32), F32),
            shape((2, 8), F32),
            shape((4, 8), F32),
        ),
        in_specs=vm(5),
        out_specs=tuple(vm(10)),
        compiler_params=pltpu.CompilerParams(vmem_limit_bytes=VMEM_LIMIT),
        name="lay_out",
    )(*operands)


def on_device(inputs, lengths, w_qkv, w_out, w_fc, w_proj, b_qv, b_fc, gains, shifts, cotangent):
    q, kv, vec, ctx, lse, n1, xg, cotg, wqkv, wo, wfc = call_first(
        lengths, inputs, cotangent, w_qkv[0].transpose(1, 0, 2), w_out[0].T, w_fc[0],
        gains[0], shifts[0], b_qv[0], b_fc,
    )
    gafter, gaf, dctx, sums, res, outs, dw_mlp = call_middle(
        inputs, ctx, vec, w_proj[0].T, wo, wfc, cotg
    )
    gin, out, early, late, small = call_last(
        lengths, q, kv, lse, dctx, inputs, vec, gafter, gaf, ctx, sums, res, outs, n1, xg, wqkv, dw_mlp
    )
    out, gin, g_qkv, g_out, g_fc, g_proj, g_bqv, g_bfc, g_gains, g_shifts = call_finish(
        out, gin, early, late, small
    )
    return (
        out, gin, g_qkv.transpose(1, 0, 2)[None], g_out.T[None], g_fc[None], g_proj.T[None],
        g_bqv[None], g_bfc, g_gains[None], g_shifts[None],
    )


def solution(mesh):
    return jax.shard_map(
        on_device,
        mesh=mesh,
        in_specs=(
            P(("dp", "tensor"), None),
            P(),
            P(None, "dp", None, "tensor"),
            P(None, "tensor", "dp"),
            P(None, "dp", "tensor"),
            P(None, "tensor", "dp"),
            P(None, None, ("tensor", "dp")),
            P(None, ("tensor", "dp")),
            P(None, None, ("dp", "tensor")),
            P(None, None, ("dp", "tensor")),
            P(("dp", "tensor"), None),
        ),
        out_specs=(
            P(("dp", "tensor"), None),
            P(("dp", "tensor"), None),
            P(None, "dp", None, "tensor"),
            P(None, "tensor", "dp"),
            P(None, "dp", "tensor"),
            P(None, "tensor", "dp"),
            P(None, None, ("tensor", "dp")),
            P(None, ("tensor", "dp")),
            P(None, None, ("dp", "tensor")),
            P(None, None, ("dp", "tensor")),
        ),
        check_vma=False,
    )
```

```python
import functools

import jax
import jax.numpy as jnp
from jax import lax
from jax.experimental import pallas as pl
from jax.experimental.pallas import tpu as pltpu
from jax.sharding import PartitionSpec as P

HEAD_DIM = 64
BLOCK = 128
D = 1024
GROUP = 512
SPAN = 512
BF = jnp.bfloat16
F32 = jnp.float32
MESH = pl.DeviceIdType.MESH
VMEM_LIMIT = 58 * 1024 * 1024


def nn(a, b):
    return jnp.dot(a, b, preferred_element_type=F32)


def nt(a, b):
    return lax.dot_general(a, b, (((1,), (1,)), ((), ())), preferred_element_type=F32)


def tn(a, b):
    return lax.dot_general(a, b, (((0,), (0,)), ((), ())), preferred_element_type=F32)


def rows(start, size, step=None):
    return pl.ds(pl.multiple_of(start, step or size), size)


class Place:
    def __init__(self):
        self.dp = lax.axis_index("dp")
        self.z = lax.axis_index("tensor")
        self.c = lax.rem(self.dp, 2)
        self.chip = self.dp // 2
        self.y = lax.rem(self.chip, 4)
        self.x = self.chip // 4

    def at(self, dx=0, dy=0, dz=0, flip=False):
        x = lax.rem(self.x + dx + 4, 4)
        y = lax.rem(self.y + dy + 4, 4)
        c = 1 - self.c if flip else self.c
        return ((x * 4 + y) * 2 + c, lax.rem(self.z + dz + 4, 4))

    def linear(self, step):
        return (lax.rem(self.chip + step + 16, 16) * 2 + self.c, self.z)

    def beside(self, dy, step):
        chip = self.x * 4 + lax.rem(self.y + dy + 4, 4)
        return (lax.rem(chip + step + 16, 16) * 2 + self.c, self.z)

    def beside_source(self, step=2, dy=-1):
        chip = lax.rem(self.chip - step + 16, 16)
        y = lax.rem(lax.rem(chip, 4) + dy + 4, 4)
        return ((chip // 4 * 4 + y) * 2 + self.c, self.z)


class Copies:
    def __init__(self, send_sem, recv_sem):
        self.send_sem, self.recv_sem = send_sem, recv_sem
        self.started, self.settled = [], []

    def put(self, src, dst, device):
        k = len(self.started)
        copy = pltpu.make_async_remote_copy(
            src_ref=src,
            dst_ref=dst,
            send_sem=self.send_sem.at[k],
            recv_sem=self.recv_sem.at[k],
            device_id=device,
            device_id_type=MESH,
        )
        copy.start()
        self.started.append(copy)
        return copy

    def settle(self, *copies):
        for copy in copies:
            copy.wait_send()
            self.settled.append(copy)

    def finish(self):
        for copy in self.started:
            if not any(copy is other for other in self.settled):
                copy.wait_send()


def greet(devices):
    barrier = pltpu.get_barrier_semaphore()
    for device in devices:
        pl.semaphore_signal(barrier, inc=1, device_id=device, device_id_type=MESH)
    pl.semaphore_wait(barrier, len(devices))


class RingGather:
    def __init__(self, copies, place, buf, size=BLOCK):
        self.copies, self.place, self.buf, self.size = copies, place, buf, size

    def block(self, dz, part=None):
        start = lax.rem(self.place.z + dz + 4, 4) * self.size
        if part is None:
            return self.buf.at[rows(start, self.size)]
        half = self.size // 2
        return self.buf.at[rows(start + part * half, half)]

    def start(self):
        own = self.block(0)
        self.up = self.copies.put(own, own, self.place.at(dz=1))
        self.down = self.copies.put(own, own, self.place.at(dz=-1))

    def below(self):
        self.up.wait_recv()
        half = self.block(-1, 0)
        self.up2 = self.copies.put(half, half, self.place.at(dz=1))

    def above(self):
        self.down.wait_recv()
        half = self.block(1, 1)
        self.down2 = self.copies.put(half, half, self.place.at(dz=-1))

    def far(self):
        self.up2.wait_recv()
        self.down2.wait_recv()


class DirectGather:
    copies_needed = 31

    def __init__(self, copies, place, w):
        self.copies, self.place, self.w = copies, place, w
        self.shared = []

    def dev(self, axis, step):
        c = self.place.c
        if axis == 0:
            return self.place.at(dx=c * step, dy=(1 - c) * step)
        return self.place.at(dx=(1 - c) * step, dy=c * step)

    def block(self, a, b):
        p, c = self.place, self.place.c
        x = lax.rem(p.x + b * (1 - c) + a * c + 4, 4)
        y = lax.rem(p.y + a * (1 - c) + b * c + 4, 4)
        return self.w.at[rows(((x * 4 + y) * 2 + c) * 32, 32)]

    def put(self, ref, device):
        return self.copies.put(ref, ref, device)

    def spread(self, a):
        ref = self.block(a, 0)
        self.second[a] = [self.put(ref, self.dev(1, step)) for step in (1, -1, 2)]
        self.shared.append(self.put(ref, self.place.at(flip=True)))

    def start(self):
        ref = self.block(0, 0)
        self.first = [self.put(ref, self.dev(0, step)) for step in (1, -1, 2)]
        self.second = {}
        self.spread(0)

    def step1(self):
        for copy, a in zip(self.first, (-1, 1, 2)):
            copy.wait_recv()
            self.spread(a)

    def step2(self):
        for a in (0, -1, 1, 2):
            for copy, b in zip(self.second[a], (-1, 1, 2)):
                copy.wait_recv()
                self.shared.append(self.put(self.block(a, b), self.place.at(flip=True)))

    def step3(self):
        for copy in self.shared:
            copy.wait_recv()


class PlaneGather:
    def __init__(self, copies, place, w, first, width):
        self.copies, self.place, self.w = copies, place, w
        c = place.c
        self.first, self.width = first, width
        self.cols = pl.ds(pl.multiple_of(first + c * (width // 2), 128), width // 2)

    def dev(self, axis, step):
        if axis == 0:
            return self.place.at(dy=step)
        return self.place.at(dx=step)

    def block(self, first_off, second_off, part=None):
        p = self.place
        start = (lax.rem(p.x + second_off + 4, 4) * 4 + lax.rem(p.y + first_off + 4, 4)) * 64
        if part is None:
            return self.w.at[rows(start, 64), self.cols]
        return self.w.at[rows(start + 32 * part, 32), self.cols]

    def put(self, ref, device):
        return self.copies.put(ref, ref, device)

    def start(self):
        p = self.place
        mine = self.w.at[rows(p.dp * 32, 32), pl.ds(self.first, self.width)]
        self.swap = self.put(mine, p.at(flip=True))

    def spread(self, first_off):
        ref = self.block(first_off, 0)
        return (self.put(ref, self.dev(1, 1)), self.put(ref, self.dev(1, -1)))

    def share(self, first_off, second_off):
        self.shared.append(self.put(self.block(first_off, second_off), self.place.at(flip=True)))

    def step1(self):
        self.swap.wait_recv()
        ref = self.block(0, 0)
        self.shared = []
        self.up = self.put(ref, self.dev(0, 1))
        self.down = self.put(ref, self.dev(0, -1))
        self.out = {0: self.spread(0)}

    def step2(self):
        self.up.wait_recv()
        self.up2 = self.put(self.block(-1, 0, 0), self.dev(0, 1))
        self.down.wait_recv()
        self.down2 = self.put(self.block(1, 0, 1), self.dev(0, -1))
        self.out[-1] = self.spread(-1)
        self.out[1] = self.spread(1)
        self.share(-1, 0)
        self.share(1, 0)

    def step3(self):
        self.up2.wait_recv()
        self.down2.wait_recv()
        self.out[2] = self.spread(2)
        self.share(2, 0)

    def step4(self):
        self.far = []
        for first_off in (0, -1, 1, 2):
            up, down = self.out[first_off]
            up.wait_recv()
            self.far.append(self.put(self.block(first_off, -1, 0), self.dev(1, 1)))
            down.wait_recv()
            self.far.append(self.put(self.block(first_off, 1, 1), self.dev(1, -1)))
            self.share(first_off, -1)
            self.share(first_off, 1)

    def step5(self):
        for k, first_off in enumerate((0, -1, 1, 2)):
            self.far[2 * k].wait_recv()
            self.far[2 * k + 1].wait_recv()
            self.share(first_off, 2)

    def step6(self):
        for copy in self.shared:
            copy.wait_recv()


def normalised(values):
    centre = values - jnp.mean(values, axis=-1, keepdims=True)
    spread = jnp.mean(centre * centre, axis=-1, keepdims=True)
    scale = lax.rsqrt(spread + 1e-05)
    return centre * scale, scale


def first_blocks(lengths_ref):
    base = lax.axis_index("dp") * 4
    end = jnp.int32(0)
    first = [jnp.int32(0)] * 4
    for i in range(32):
        end = end + lengths_ref[i]
        first = [jnp.where(end <= base + b, end, first[b]) for b in range(4)]
    return [first[b] - base + 16 for b in range(4)]


def heads_across(tile):
    head = lax.broadcasted_iota(jnp.int32, tile.shape, 1) // HEAD_DIM
    return jnp.concatenate([jnp.where(head == h, tile, 0.0) for h in range(4)], axis=0)


def heads_together(tile):
    head = lax.broadcasted_iota(jnp.int32, (BLOCK, 256), 1) // HEAD_DIM
    return sum(jnp.where(head == h, tile[h * BLOCK:(h + 1) * BLOCK], 0.0) for h in range(4))


def causal(scores, b):
    query = lax.rem(lax.broadcasted_iota(jnp.int32, scores.shape, 0), BLOCK)
    key = lax.broadcasted_iota(jnp.int32, scores.shape, 1)
    return jnp.where(key <= query + b * BLOCK, scores, -1e30)


def outside(block, first):
    lane = lax.broadcasted_iota(jnp.int32, (1, SPAN), 1)
    return jnp.where(lane < (first - block) * BLOCK, -1e30, 0.0)


def parts(tile):
    return [tile[:, i * 128:(i + 1) * 128] for i in range(SPAN // 128)]


def pick_first(first, b):
    value = first[3]
    for k in range(3):
        value = jnp.where(b == k, first[k], value)
    return value


class Attention:
    def __init__(self, lengths_ref, q_ref, kv_ref, scratch):
        self.first = first_blocks(lengths_ref)
        self.q_ref, self.kv_ref = q_ref, kv_ref
        self.tall, self.top, self.total, self.acc = scratch

    @staticmethod
    def scratch():
        return [
            pltpu.VMEM((4, 512, 256), BF),
            pltpu.VMEM((4, 512, 128), F32),
            pltpu.VMEM((4, 512, 128), F32),
            pltpu.VMEM((4, 512, 256), F32),
        ]

    def start(self):
        for b in range(4):
            queries = self.q_ref[b * BLOCK:(b + 1) * BLOCK, :].astype(F32) * 0.125
            self.tall[b] = heads_across(queries).astype(BF)

    def add(self, slot, own=False):
        keys = rows(slot * GROUP, GROUP)

        def one(b):
            tile = nt(self.tall[b], self.kv_ref[keys, 0:256]) + outside(slot * 4, self.of_block(b))
            if own:
                tile = causal(tile, b)
            pieces = parts(tile)
            peak = jnp.max(functools.reduce(jnp.maximum, pieces), axis=1, keepdims=True)
            top = jnp.broadcast_to(peak, (512, 128))
            if not own:
                top = jnp.maximum(top, self.top[b])
            weights = [jnp.exp(piece - top) for piece in pieces]
            low = jnp.concatenate([piece.astype(BF) for piece in weights], axis=1)
            product = nn(low, self.kv_ref[keys, 256:512])
            if own:
                self.total[b] = sum(weights)
                self.acc[b] = product
            else:
                shrink = jnp.exp(self.top[b] - top)
                self.total[b] = self.total[b] * shrink + sum(weights)
                self.acc[b] = self.acc[b] * jnp.concatenate([shrink, shrink], axis=1) + product
            self.top[b] = top

        def two(i, carry):
            one(2 * i)
            one(2 * i + 1)
            return carry

        lax.fori_loop(0, 2, two, 0)

    def of_block(self, b):
        return pick_first(self.first, b)

    def finish(self, ctx_ref, lse_ref):
        for b in range(4):
            sums = jnp.sum(self.total[b], axis=1, keepdims=True)
            lse_ref[b] = self.top[b] + jnp.log(sums)
            ctx_ref[b * BLOCK:(b + 1) * BLOCK, :] = heads_together(self.acc[b] * (1.0 / sums)).astype(BF)


class AttentionBack:
    def __init__(self, lengths_ref, q_ref, kv_ref, ctx_ref, lse_ref, dctx_ref, scratch):
        self.first = first_blocks(lengths_ref)
        self.q_ref, self.kv_ref, self.ctx_ref = q_ref, kv_ref, ctx_ref
        self.lse_ref, self.dctx_ref = lse_ref, dctx_ref
        self.tall_q, self.tall_g, self.inner, self.acc, self.sum = scratch
        self.sum[...] = jnp.zeros_like(self.sum)

    @staticmethod
    def scratch():
        return [
            pltpu.VMEM((2048, 256), BF),
            pltpu.VMEM((2048, 256), BF),
            pltpu.VMEM((4, 512, 128), F32),
            pltpu.VMEM((4, 512, 256), F32),
            pltpu.VMEM((512, 512), F32),
        ]

    def start(self):
        for b in range(4):
            block, tall = slice(b * BLOCK, (b + 1) * BLOCK), slice(b * 512, (b + 1) * 512)
            grads = self.dctx_ref[block, :].astype(F32)
            self.tall_q[tall, :] = heads_across(self.q_ref[block, :].astype(F32) * 0.125).astype(BF)
            self.tall_g[tall, :] = heads_across(grads).astype(BF)
            product = heads_across(grads * self.ctx_ref[block, :].astype(F32))
            self.inner[b] = jnp.broadcast_to(jnp.sum(product, axis=1, keepdims=True), (512, 128))
            self.acc[b] = jnp.zeros((512, 256), F32)

    def add(self, slot, dkv, own=False):
        keys = rows(slot * GROUP, GROUP)

        def one(b):
            tall = rows(b * 512, 512)
            tile = nt(self.tall_q[tall, :], self.kv_ref[keys, 0:256])
            tile = tile + outside(slot * 4, pick_first(self.first, b))
            if own:
                tile = causal(tile, b)
            weight = jnp.exp(tile - jnp.concatenate([self.lse_ref[b]] * 4, axis=1))
            grad = nt(self.tall_g[tall, :], self.kv_ref[keys, 256:512])
            low = (weight * (grad - jnp.concatenate([self.inner[b]] * 4, axis=1))).astype(BF)
            self.acc[b] += nn(low, self.kv_ref[keys, 0:256])
            grads = tn(low, self.tall_q[tall, :]), tn(weight.astype(BF), self.tall_g[tall, :])
            for k, grad in enumerate(grads):
                cols = slice(k * 256, (k + 1) * 256)
                self.sum[:, cols] = jnp.where(b == 0, 0.0, self.sum[:, cols]) + grad

        def each(b, carry):
            one(b)
            return carry

        lax.fori_loop(0, 4, each, 0)
        dkv[keys, :] = self.sum[...].astype(BF)

    def finish(self, dq):
        for b in range(4):
            dq[b * BLOCK:(b + 1) * BLOCK, :] = heads_together(self.acc[b] * 0.125).astype(BF)


def one_hot(shape, offset):
    row = lax.broadcasted_iota(jnp.int32, shape, 0)
    lane = lax.broadcasted_iota(jnp.int32, shape, 1)
    return jnp.where(lane == row + offset, 1.0, 0.0).astype(F32)


def exact(a, b):
    return jnp.dot(a, b, precision=lax.Precision.HIGHEST, preferred_element_type=F32)


def first_kernel(
    lengths_ref, x_ref, cot_ref, wqkv_ref, wout_ref, wfc_ref, gains_ref, shifts_ref, bqv_ref, bfc_ref,
    q_ref, kv_ref, vec_ref, ctx_ref, lse_ref, n1_out, xg_out, cotg_out, wqkv_out, wo_out, wfc_out,
    n1, xg, cotg, wq, wo, wfc, vz, vall, bias, mid, out_sem, send_sem, recv_sem, *scratch,
):
    p = Place()
    mine = rows(p.dp * 32, 32)
    for j in range(3):
        wq[mine, j * 256:(j + 1) * 256] = wqkv_ref[j]
    wq[mine, 768:1024] = wout_ref[...]
    wfc[mine, :] = wfc_ref[...]
    xg[rows(p.z * BLOCK, BLOCK), :] = x_ref[...]
    cotg[rows(p.z * BLOCK, BLOCK), :] = cot_ref[...]
    place8 = one_hot((8, 128), lax.rem(p.dp * 4 + p.z, 16) * 8)
    own = vz.at[p.z]
    own[...] = jnp.zeros((8, 128), F32)
    own[0:2] = exact(gains_ref[...], place8)
    own[2:6] = exact(shifts_ref[...], place8)
    tile = vall.at[p.c, p.chip]
    tile[8:16] = jnp.zeros((8, 128), F32)
    tile[8:9] = exact(bfc_ref[...].astype(F32), one_hot((32, 128), lax.rem(p.dp, 4) * 32))
    tile[9:11] = exact(bqv_ref[...].astype(F32), one_hot((8, 128), lax.rem(p.dp, 16) * 8))
    greet(
        [p.at(dz=1), p.at(dz=-1), p.at(dz=2), p.at(dx=1), p.at(dx=-1), p.at(dx=2),
         p.at(dy=1), p.at(dy=-1), p.at(dy=2), p.at(flip=True), p.linear(1), p.linear(-1),
         p.beside(1, 2), p.beside_source()]
    )
    copies = Copies(send_sem, recv_sem)
    head = DirectGather(copies, p, wq)
    head.start()
    small = [copies.put(own, own, p.at(dz=dz)) for dz in (1, -1, 2)]
    ring = RingGather(copies, p, xg)
    ring.start()
    tail = PlaneGather(copies, p, wfc, 0, 1024)
    for copy in small:
        copy.wait_recv()
    tile[0:8] = vz[0] + vz[1] + vz[2] + vz[3]
    small = [copies.put(tile, tile, p.at(dy=dy)) for dy in (1, -1, 2)]
    head.step1()
    tail.start()
    for copy in small:
        copy.wait_recv()
    line = vall.at[p.c, rows(p.x * 4, 4)]
    small = [copies.put(line, line, p.at(dx=dx)) for dx in (1, -1, 2)]
    ring.below()
    ring.above()
    cot_ring = RingGather(copies, p, cotg)
    cot_ring.start()
    for copy in small:
        copy.wait_recv()
    plane = vall.at[p.c]
    last = copies.put(plane, plane, p.at(flip=True))
    head.step2()
    tail.step1()
    ring.far()
    last.wait_recv()
    lanes = []
    for k in range(8):
        total = vall[0, 2 * k] + vall[0, 2 * k + 1] + vall[1, 2 * k] + vall[1, 2 * k + 1]
        vec_ref[:, k * 128:(k + 1) * 128] = total
        lanes.append(total)
    for h in range(2):
        bias[:, h * 128:(h + 1) * 128] = lanes[4 * h] + lanes[4 * h + 1] + lanes[4 * h + 2] + lanes[4 * h + 3]

    def norm_block(k, carry):
        block = rows(lax.rem(p.z + k, 4) * BLOCK, BLOCK)
        hat, _ = normalised(xg[block, :].astype(F32))
        n1[block, :] = (hat * vec_ref[0:1, :] + vec_ref[2:3, :]).astype(BF)
        return carry

    lax.fori_loop(0, 4, norm_block, 0)
    cot_ring.below()
    cot_ring.above()
    head.step3()

    def start_of(k):
        return lax.rem(p.z + k, 4) * BLOCK

    sibling = p.at(flip=True)
    near, there, cross = {}, {}, []
    for pair in ((2, 0), (3, 1)):
        values = jnp.concatenate([n1[rows(start_of(k), BLOCK), :] for k in pair], axis=0)
        keys = nn(values, wq[:, 256:512]).astype(BF)
        vals = (nn(values, wq[:, 512:768]) + bias[10:11, :]).astype(BF)
        for i, k in enumerate(pair):
            ours = rows(4 * GROUP + start_of(k), BLOCK)
            kv_ref[ours, 0:256] = keys[i * BLOCK:(i + 1) * BLOCK]
            kv_ref[ours, 256:512] = vals[i * BLOCK:(i + 1) * BLOCK]
            if k < 2:
                there[k] = copies.put(kv_ref.at[ours], mid.at[k], p.at(dy=-1))
            else:
                near[k] = copies.put(
                    kv_ref.at[ours], kv_ref.at[rows(2 * GROUP + start_of(k), BLOCK)], p.linear(1)
                )
    for k in (0, 1):
        ours = kv_ref.at[rows(4 * GROUP + start_of(k), BLOCK)]
        near[k] = copies.put(ours, kv_ref.at[rows(2 * GROUP + start_of(k), BLOCK)], p.linear(1))
    wo[rows(p.z * D, D), :] = wq[:, 768:1024]
    wo_ring = RingGather(copies, p, wo, D)
    wo_ring.start()
    tail.step2()
    q_ref[...] = (nn(n1[...], wq[:, 0:256]) + bias[9:10, :]).astype(BF)
    saves = [
        pltpu.make_async_copy(source, target, out_sem.at[i])
        for i, (source, target) in enumerate(
            (
                (n1, n1_out), (xg, xg_out), (wq.at[:, 0:768], wqkv_out), (cotg, cotg_out),
                (wo, wo_out), (wfc, wfc_out),
            )
        )
    ]
    for i in range(3):
        saves[i].start()
    heads = Attention(lengths_ref, q_ref, kv_ref, scratch)
    heads.start()
    heads.add(4, own=True)
    far = {}
    for k in (0, 1):
        there[k].wait_recv()
        far[k] = copies.put(mid.at[k], kv_ref.at[rows(start_of(k), BLOCK)], p.beside(1, 2))

    def pass_near(k, onward):
        near[k].wait_recv()
        ref = kv_ref.at[rows(2 * GROUP + start_of(k), BLOCK)]
        if onward:
            far[k] = copies.put(ref, kv_ref.at[rows(start_of(k), BLOCK)], p.linear(1))
        cross.append(
            copies.put(ref, kv_ref.at[rows((1 + 2 * p.c) * GROUP + start_of(k), BLOCK)], sibling)
        )

    pass_near(2, True)
    pass_near(3, True)
    tail.step3()
    cot_ring.far()
    saves[3].start()
    tail.step4()
    pass_near(0, False)
    pass_near(1, False)
    wo_ring.below()
    wo_ring.above()

    def pass_far(k):
        far[k].wait_recv()
        cross.append(
            copies.put(
                kv_ref.at[rows((4 - 4 * p.c) * GROUP + start_of(k), BLOCK)],
                kv_ref.at[rows((3 - 2 * p.c) * GROUP + start_of(k), BLOCK)],
                sibling,
            )
        )

    heads.add(2)
    pass_far(0)
    pass_far(1)
    tail.step5()
    for copy in cross[:4]:
        copy.wait_recv()
    heads.add(3 - 2 * p.c)
    pass_far(2)
    pass_far(3)
    tail.step6()
    saves[5].start()
    heads.add(0)
    wo_ring.far()
    saves[4].start()
    for copy in cross[4:]:
        copy.wait_recv()
    heads.add(1 + 2 * p.c)
    heads.finish(ctx_ref, lse_ref)
    for save in saves:
        save.wait()
    copies.finish()


N1_COPIES = 31 + 36 + 10 + 12 + 18


def vm(count):
    return [pl.BlockSpec(memory_space=pltpu.VMEM)] * count


def far_memory(count):
    return [pl.BlockSpec(memory_space=pl.ANY)] * count


def call_first(*operands):
    shape = jax.ShapeDtypeStruct
    return pl.pallas_call(
        first_kernel,
        out_shape=(
            shape((GROUP, 256), BF),
            shape((5 * GROUP, 512), BF),
            shape((16, D), F32),
            shape((GROUP, 256), BF),
            shape((4, 512, 128), F32),
            shape((GROUP, D), BF),
            shape((GROUP, D), BF),
            shape((GROUP, D), BF),
            shape((D, 768), BF),
            shape((4 * D, 256), BF),
            shape((D, D), BF),
        ),
        in_specs=[pl.BlockSpec(memory_space=pltpu.SMEM)] + vm(9),
        out_specs=tuple(vm(5) + far_memory(6)),
        scratch_shapes=[
            pltpu.VMEM((GROUP, D), BF),
            pltpu.VMEM((GROUP, D), BF),
            pltpu.VMEM((GROUP, D), BF),
            pltpu.VMEM((D, 1024), BF),
            pltpu.VMEM((4 * D, 256), BF),
            pltpu.VMEM((D, D), BF),
            pltpu.VMEM((4, 8, 128), F32),
            pltpu.VMEM((2, 16, 16, 128), F32),
            pltpu.VMEM((16, 256), F32),
            pltpu.VMEM((2, BLOCK, 512), BF),
            pltpu.SemaphoreType.DMA((6,)),
            pltpu.SemaphoreType.DMA((N1_COPIES,)),
            pltpu.SemaphoreType.DMA((N1_COPIES,)),
            *Attention.scratch(),
        ],
        compiler_params=pltpu.CompilerParams(
            collective_id=1, has_side_effects=True, vmem_limit_bytes=VMEM_LIMIT
        ),
        name="gather_and_project",
    )(*operands)


class PlaneScatter:
    copies_needed = 18

    def __init__(self, copies, place, g, scratch):
        self.copies, self.place, self.g = copies, place, g
        self.land, self.far, self.near, self.t, self.far2, self.near2, self.last, self.rest = scratch
        self.half = g.shape[1] // 2

    @staticmethod
    def scratch(width):
        half = width // 2
        return [
            pltpu.VMEM((1024, half), BF),
            pltpu.VMEM((2, 2, 64, half), BF),
            pltpu.VMEM((2, 4, 64, half), BF),
            pltpu.VMEM((4, 64, half), BF),
            pltpu.VMEM((2, 32, half), BF),
            pltpu.VMEM((2, 64, half), BF),
            pltpu.VMEM((32, half), F32),
            pltpu.VMEM((32, half), F32),
        ]

    def dev(self, axis, step):
        c = self.place.c
        if axis == 0:
            return self.place.at(dx=(1 - c) * step, dy=c * step)
        return self.place.at(dx=c * step, dy=(1 - c) * step)

    def first(self, step):
        p = self.place
        return lax.rem(p.x * (1 - p.c) + p.y * p.c + step + 4, 4)

    def second(self, step):
        p = self.place
        return lax.rem(p.y * (1 - p.c) + p.x * p.c + step + 4, 4)

    def block(self, f, s):
        c = self.place.c
        x, y = f * (1 - c) + s * c, s * (1 - c) + f * c
        return rows((x * 4 + y) * 64, 64)

    def start(self):
        c = self.place.c
        other = pl.ds(pl.multiple_of((1 - c) * self.half, 128), self.half)
        self.swap = self.copies.put(self.g.at[:, other], self.land, self.place.at(flip=True))

    def step1(self):
        self.swap.wait_recv()
        mine = pl.ds(pl.multiple_of(self.place.c * self.half, 128), self.half)
        self.mine = mine

        def join(k, carry):
            f = self.first(2 + k // 4)
            block = self.block(f, lax.rem(k, 4))
            self.land[block, :] = (self.land[block, :].astype(F32) + self.g[block, mine].astype(F32)).astype(BF)
            return carry

        lax.fori_loop(0, 4, join, 0)
        self.out = []
        for s in range(4):
            to = self.dev(0, 1 if s < 2 else -1)
            self.out.append(
                self.copies.put(self.land.at[self.block(self.first(2), s)], self.far.at[s // 2, s % 2], to)
            )
        lax.fori_loop(4, 16, join, 0)

    def step2(self):
        self.out2 = []
        for side, step in ((0, 1), (1, -1)):
            f = self.first(step)
            for s in range(4):
                block = self.block(f, s)
                if s // 2 == side:
                    self.out[s].wait_recv()
                    self.land[block, :] = (
                        self.land[block, :].astype(F32) + self.far[side, s % 2].astype(F32)
                    ).astype(BF)
                self.out2.append(
                    self.copies.put(self.land.at[block], self.near.at[side, s], self.dev(0, step))
                )

    def step3(self):
        f = self.first(0)
        for copy in self.out2:
            copy.wait_recv()

        def total(k, carry):
            s = self.second(2 + k)
            self.t[s] = (
                self.land[self.block(f, s), :].astype(F32)
                + self.near[0, s].astype(F32)
                + self.near[1, s].astype(F32)
            ).astype(BF)
            return carry

        lax.fori_loop(0, 1, total, 0)
        s = self.second(2)
        self.up = self.copies.put(self.t.at[s, 0:32], self.far2.at[0], self.dev(1, 1))
        self.down = self.copies.put(self.t.at[s, 32:64], self.far2.at[1], self.dev(1, -1))
        lax.fori_loop(1, 4, total, 0)

    def step4(self):
        s = self.second(1)
        self.up.wait_recv()
        self.t[s, 0:32] = (self.t[s, 0:32].astype(F32) + self.far2[0].astype(F32)).astype(BF)
        self.up2 = self.copies.put(self.t.at[s], self.near2.at[0], self.dev(1, 1))
        s = self.second(-1)
        self.down.wait_recv()
        self.t[s, 32:64] = (self.t[s, 32:64].astype(F32) + self.far2[1].astype(F32)).astype(BF)
        self.down2 = self.copies.put(self.t.at[s], self.near2.at[1], self.dev(1, -1))

    def part(self, c):
        half = rows(c * 32, 32)
        return (
            self.t[self.second(0), half].astype(F32)
            + self.near2[0, half].astype(F32)
            + self.near2[1, half].astype(F32)
        )

    def step5(self):
        self.up2.wait_recv()
        self.down2.wait_recv()
        c = self.place.c
        self.last[...] = self.part(1 - c)
        self.back = self.copies.put(self.last, self.rest, self.place.at(flip=True))

    def step6(self, out):
        out[:, self.mine] = self.part(self.place.c)
        self.back.wait_recv()
        other = pl.ds(pl.multiple_of((1 - self.place.c) * self.half, 128), self.half)
        out[:, other] = self.rest[...]


class QuickScatter:
    copies_needed = 17

    def __init__(self, copies, place, g, scratch):
        self.copies, self.place, self.g = copies, place, g
        self.land, self.near, self.t, self.near2, self.last, self.rest = scratch
        self.half = g.shape[1] // 2

    @staticmethod
    def scratch(width):
        half = width // 2
        return [
            pltpu.VMEM((1024, half), BF),
            pltpu.VMEM((3, 4, 64, half), BF),
            pltpu.VMEM((4, 64, half), BF),
            pltpu.VMEM((3, 64, half), BF),
            pltpu.VMEM((32, half), F32),
            pltpu.VMEM((32, half), F32),
        ]

    dev, first, second, block, start = (
        PlaneScatter.dev, PlaneScatter.first, PlaneScatter.second, PlaneScatter.block, PlaneScatter.start
    )

    def step1(self):
        self.swap.wait_recv()
        self.mine = pl.ds(pl.multiple_of(self.place.c * self.half, 128), self.half)
        self.out = []
        for i, step in enumerate((2, 1, -1, 0)):
            f = self.first(step)

            def join(s, carry):
                block = self.block(f, s)
                self.land[block, :] = (
                    self.land[block, :].astype(F32) + self.g[block, self.mine].astype(F32)
                ).astype(BF)
                return carry

            lax.fori_loop(0, 4, join, 0)
            if step:
                for s in range(4):
                    self.out.append(
                        self.copies.put(self.land.at[self.block(f, s)], self.near.at[i, s], self.dev(0, step))
                    )

    def step2(self):
        for copy in self.out:
            copy.wait_recv()
        f = self.first(0)

        def total(s, carry):
            value = self.land[self.block(f, s), :].astype(F32)
            for i in range(3):
                value = value + self.near[i, s].astype(F32)
            self.t[s] = value.astype(BF)
            return carry

        lax.fori_loop(0, 4, total, 0)
        self.out2 = [
            self.copies.put(self.t.at[self.second(step)], self.near2.at[i], self.dev(1, step))
            for i, step in enumerate((2, 1, -1))
        ]

    def part(self, c):
        half = rows(c * 32, 32)
        value = self.t[self.second(0), half].astype(F32)
        for i in range(3):
            value = value + self.near2[i, half].astype(F32)
        return value

    def step3(self):
        for copy in self.out2:
            copy.wait_recv()
        self.last[...] = self.part(1 - self.place.c)
        self.back = self.copies.put(self.last, self.rest, self.place.at(flip=True))

    step4 = PlaneScatter.step6


class RingScatter:
    copies_needed = 4

    def __init__(self, copies, place, scratch):
        self.copies, self.place = copies, place
        self.part, self.far, self.near = scratch

    @staticmethod
    def scratch():
        return [
            pltpu.VMEM((3, BLOCK, D), BF),
            pltpu.VMEM((2, 64, D), BF),
            pltpu.VMEM((2, BLOCK, D), BF),
        ]

    def send_far(self):
        p, c = self.place, self.copies
        self.up = c.put(self.part.at[2, 0:64], self.far.at[0], p.at(dz=1))
        self.down = c.put(self.part.at[2, 64:128], self.far.at[1], p.at(dz=-1))

    def send_above(self):
        self.up.wait_recv()
        self.part[0, 0:64] = (self.part[0, 0:64].astype(F32) + self.far[0].astype(F32)).astype(BF)
        self.up2 = self.copies.put(self.part.at[0], self.near.at[0], self.place.at(dz=1))

    def send_below(self):
        self.down.wait_recv()
        self.part[1, 64:128] = (self.part[1, 64:128].astype(F32) + self.far[1].astype(F32)).astype(BF)
        self.down2 = self.copies.put(self.part.at[1], self.near.at[1], self.place.at(dz=-1))

    def received(self):
        self.up2.wait_recv()
        self.down2.wait_recv()
        return self.near[0].astype(F32) + self.near[1].astype(F32)


class RingReturn:
    copies_needed = 6

    def __init__(self, copies, place, scratch):
        self.copies, self.place = copies, place
        self.above, self.below, self.across, self.near, self.mid, self.far = scratch

    @staticmethod
    def scratch():
        return [
            pltpu.VMEM((2, BLOCK, D), BF),
            pltpu.VMEM((2, 64, D), BF),
            pltpu.VMEM((BLOCK, D), BF),
        ]

    def send_above(self):
        self.up = self.copies.put(self.above, self.near.at[0], self.place.at(dz=1))

    def send_below(self):
        self.down = self.copies.put(self.below, self.near.at[1], self.place.at(dz=-1))

    def send_far(self):
        p, c = self.place, self.copies
        self.up1 = c.put(self.across.at[0:64], self.mid.at[0], p.at(dz=1))
        self.down1 = c.put(self.across.at[64:128], self.mid.at[1], p.at(dz=-1))

    def pass_on(self):
        p, c = self.place, self.copies
        self.up1.wait_recv()
        self.up2 = c.put(self.mid.at[0], self.far.at[0:64], p.at(dz=1))
        self.down1.wait_recv()
        self.down2 = c.put(self.mid.at[1], self.far.at[64:128], p.at(dz=-1))

    def received(self):
        for copy in (self.up, self.down, self.up2, self.down2):
            copy.wait_recv()
        return self.near[0].astype(F32) + self.near[1].astype(F32) + self.far[...].astype(F32)


def norm_back(hat, scale, grad, gain):
    inner = grad * gain
    mean = jnp.mean(inner, axis=-1, keepdims=True)
    along = jnp.mean(inner * hat, axis=-1, keepdims=True)
    return (
        scale * (inner - mean - hat * along),
        jnp.sum(grad * hat, axis=0, keepdims=True),
        jnp.sum(grad, axis=0, keepdims=True),
    )


def weight_grad(left, right, out, first):
    width = right.shape[1]

    def tile(k, carry):
        turned = left[:, pl.ds(pl.multiple_of(k * 256, 256), 256)].astype(F32).T.astype(BF)
        out[rows(k * 256, 256), first:first + width] = nn(turned, right[...]).astype(BF)
        return carry

    lax.fori_loop(0, 4, tile, 0)


def middle_kernel(
    x_ref, ctx_ref, vec_ref, wproj_ref, wo_any, wfc_any, cotg_any,
    gafter_ref, gaf_ref, dctx_ref, sums_ref, res_ref, outs_ref, dw_any,
    wo, wfc, wproj, cotg, ctxf, n2g, act, dpre, dact, part, back, own, after, dw, dctx, io_sem, send_sem, recv_sem,
    *scratch,
):
    p = Place()
    loads = [
        pltpu.make_async_copy(source, target, io_sem.at[i])
        for i, (source, target) in enumerate(((wo_any, wo), (cotg_any, cotg), (wfc_any, wfc)))
    ]
    for load in loads:
        load.start()
    wproj[rows(p.dp * 32, 32), :] = wproj_ref[...]
    greet(
        [p.at(dz=1), p.at(dz=-1), p.at(dz=2), p.at(dx=1), p.at(dx=-1), p.at(dx=2),
         p.at(dy=1), p.at(dy=-1), p.at(dy=2), p.at(flip=True)]
    )
    copies = Copies(send_sem, recv_sem)
    backs = RingReturn(copies, p, (part.at[0], part.at[1], part.at[2]) + scratch)

    def block(dz):
        return rows(lax.rem(p.z + dz + 4, 4) * BLOCK, BLOCK)

    swaps = [
        copies.put(ctx_ref.at[block(dz)], ctxf.at[p.z], p.at(dz=dz)) for dz in (2, 1, -1)
    ]
    plane = DirectGather(copies, p, wproj)
    plane.start()
    ctxf[p.z] = ctx_ref[block(0), :]
    for load in loads:
        load.wait()

    plane.step1()
    for copy in swaps:
        copy.wait_recv()
    total = x_ref[...].astype(F32) + vec_ref[4:5, :]
    for k in range(4):
        total = total + nt(ctxf[k], wo[k * D:(k + 1) * D, :])
    after[...] = total
    hat, scale = normalised(after[...])
    n2g[block(0), :] = (hat * vec_ref[1:2, :] + vec_ref[3:4, :]).astype(BF)
    ring = RingGather(copies, p, n2g)
    ring.start()
    plane.step2()
    plane.step3()

    def act_grad(t, carry):
        cols = pl.ds(pl.multiple_of(t * 256, 256), 256)
        dact[:, cols] = nn(cotg[...], wproj[:, cols])
        return carry

    lax.fori_loop(0, 4, act_grad, 0)

    def mlp(pair, put_back):
        here = [block(dz) for dz in pair]

        def both(ref, cols=slice(None)):
            return jnp.concatenate([ref[h, cols] for h in here], axis=0)

        def hidden(t, carry):
            cols = pl.ds(pl.multiple_of(t * 256, 256), 256)
            pre = nn(both(n2g), wfc[:, cols]) + vec_ref[8:9, cols]
            square = pre * pre
            bend = jnp.tanh(0.7978845608028654 * pre * (1.0 + 0.044715 * square))
            slope = 0.5 * (1.0 + bend) + 0.5 * pre * (1.0 - bend * bend) * (
                0.7978845608028654 * (1.0 + 0.134145 * square)
            )
            value = (0.5 * pre * (1.0 + bend)).astype(BF)
            grad = (both(dact, cols) * slope).astype(BF)
            for i, h in enumerate(here):
                act[h, cols] = value[i * BLOCK:(i + 1) * BLOCK]
                dpre[h, cols] = grad[i * BLOCK:(i + 1) * BLOCK]
            return carry

        lax.fori_loop(0, 4, hidden, 0)

        def project(t, carry):
            cols = pl.ds(pl.multiple_of(t * 256, 256), 256)
            value = nt(both(dpre), wfc[cols, :])
            for i in range(2):
                put_back[i](cols, value[i * BLOCK:(i + 1) * BLOCK])
            return carry

        lax.fori_loop(0, 4, project, 0)

    def into(i):
        def put(cols, value):
            part[i, :, cols] = value.astype(BF)

        return put

    def keep(cols, value):
        own[:, cols] = value

    ring.below()
    ring.above()
    mlp((1, -1), (into(0), into(1)))
    backs.send_above()
    backs.send_below()
    ring.far()
    mlp((2, 0), (into(2), keep))
    backs.send_far()
    weight_grad(n2g, dpre, dw, 0)
    backs.pass_on()
    weight_grad(cotg, act, dw, 1024)
    save = pltpu.make_async_copy(dw, dw_any, io_sem.at[3])
    save.start()
    def output_part(t, carry):
        cols = pl.ds(pl.multiple_of(t * 256, 256), 256)
        outs_ref[:, cols] = nt(act[...], wproj[cols, :]).astype(BF)
        return carry

    lax.fori_loop(0, 4, output_part, 0)
    res_ref[...] = after[...] + vec_ref[5:6, :]
    grad = own[...] + backs.received()
    hat, scale = normalised(after[...])
    grad_in, gain, shift = norm_back(hat, scale, grad, vec_ref[1:2, :])
    residual = cotg[block(0), :].astype(F32)
    back[...] = grad_in + residual
    gaf_ref[...] = back[...].astype(BF)
    for k in (2, 1, 3, 0):
        owner = lax.rem(p.z + k, 4)
        part = nn(gaf_ref[...], wo[rows(owner * D, D), :]).astype(BF)
        if k:
            dctx[k] = part
            swaps.append(copies.put(dctx.at[k], dctx_ref.at[block(0)], p.at(dz=k)))
        else:
            dctx_ref[block(0), :] = part
    sums_ref[...] = jnp.zeros_like(sums_ref)
    sums_ref[0:1, :] = gain
    sums_ref[1:2, :] = shift
    sums_ref[2:3, :] = jnp.sum(back[...], axis=0, keepdims=True)
    sums_ref[3:4, :] = jnp.sum(residual, axis=0, keepdims=True)
    sums_ref[4:5, :] = jnp.sum(dpre[...].astype(F32), axis=0, keepdims=True)
    gafter_ref[...] = back[...]

    for copy in swaps[3:]:
        copy.wait_recv()
    save.wait()
    copies.finish()


N3_COPIES = 6 + 4 + 6 + 31


def call_middle(*operands):
    shape = jax.ShapeDtypeStruct
    return pl.pallas_call(
        middle_kernel,
        out_shape=(
            shape((BLOCK, D), F32),
            shape((BLOCK, D), BF),
            shape((GROUP, 256), BF),
            shape((8, D), F32),
            shape((BLOCK, D), F32),
            shape((GROUP, D), BF),
            shape((D, 2048), BF),
        ),
        in_specs=vm(4) + far_memory(3),
        out_specs=tuple(vm(6) + far_memory(1)),
        scratch_shapes=[
            pltpu.VMEM((4 * D, 256), BF),
            pltpu.VMEM((D, D), BF),
            pltpu.VMEM((D, D), BF),
            pltpu.VMEM((GROUP, D), BF),
            pltpu.VMEM((4, BLOCK, 256), BF),
            pltpu.VMEM((GROUP, D), BF),
            pltpu.VMEM((GROUP, D), BF),
            pltpu.VMEM((GROUP, D), BF),
            pltpu.VMEM((GROUP, D), F32),
            pltpu.VMEM((3, BLOCK, D), BF),
            pltpu.VMEM((BLOCK, D), F32),
            pltpu.VMEM((BLOCK, D), F32),
            pltpu.VMEM((BLOCK, D), F32),
            pltpu.VMEM((D, 2048), BF),
            pltpu.VMEM((4, BLOCK, 256), BF),
            pltpu.SemaphoreType.DMA((4,)),
            pltpu.SemaphoreType.DMA((N3_COPIES,)),
            pltpu.SemaphoreType.DMA((N3_COPIES,)),
            *RingReturn.scratch(),
        ],
        compiler_params=pltpu.CompilerParams(
            collective_id=2, has_side_effects=True, vmem_limit_bytes=VMEM_LIMIT
        ),
        name="mlp_both_ways",
    )(*operands)


def last_kernel(
    lengths_ref, q_ref, kv_ref, lse_ref, dctx_ref, x_ref, vec_ref, gafter_ref, gaf_ref, ctx_ref, sums_ref, res_ref, outs_ref,
    n1_any, xg_any, wqkv_any, dw_any,
    gin_ref, out_ref, early_ref, mid_ref, late_ref, sums_out,
    dq, dkv, n1, xg, wqkv, gafg, cross, hand, land, mid, fin, dqkv, early, middle, late, own, hats, small_ref, xsum, ysum, zsum, line,
    io_sem, send_sem, recv_sem, *scratch,
):
    p = Place()
    loads = [
        pltpu.make_async_copy(source, target, io_sem.at[i])
        for i, (source, target) in enumerate(
            ((dw_any, early), (n1_any, n1), (wqkv_any, wqkv), (xg_any, xg))
        )
    ]
    for load in loads:
        load.start()
    gafg[rows(p.z * BLOCK, BLOCK), :] = gaf_ref[...]
    greet(
        [p.at(dz=1), p.at(dz=-1), p.at(dz=2), p.at(dx=1), p.at(dx=-1), p.at(dx=2),
         p.at(dy=1), p.at(dy=-1), p.at(dy=2), p.at(flip=True), p.linear(1), p.linear(-1),
         p.at(dy=1, flip=True), p.at(dy=-1, flip=True), p.at(dy=2, flip=True),
         p.beside(-1, -2), p.beside_source(-2, 1)]
    )
    copies = Copies(send_sem, recv_sem)
    scatter = RingScatter(copies, p, scratch[0:3])
    plane = PlaneScatter(copies, p, early, scratch[6:14])
    quick = QuickScatter(copies, p, late, scratch[14:20])
    quick2 = QuickScatter(copies, p, middle, scratch[25:31])
    sibling = p.at(flip=True)
    even = p.c == 0

    def start_of(k):
        return lax.rem(p.z + k, 4) * BLOCK

    def block(k):
        return rows(start_of(k), BLOCK)

    outs = RingReturn(
        copies, p, (outs_ref.at[block(1)], outs_ref.at[block(3)], outs_ref.at[block(2)]) + scratch[3:6]
    )

    def spread_bias(row, value):
        for half in range(2):
            for k in range(4):
                first = (4 * half + k) * 128
                small_ref[row:row + 1, first:first + 128] = value[:, half * 128:(half + 1) * 128]

    order = (2, 1, 3, 0)
    ring = RingGather(copies, p, gafg)
    ring.start()
    outs.send_above()
    outs.send_below()
    outs.send_far()
    for load in loads:
        load.wait()
    plane.start()
    heads = AttentionBack(lengths_ref, q_ref, kv_ref, ctx_ref, lse_ref, dctx_ref, scratch[20:25])
    heads.start()

    def cross_over(side):
        ref = dkv.at[rows((1 + 2 * side) * GROUP, GROUP)]
        return copies.put(ref, cross.at[side], sibling)

    heads.add(1, dkv)
    low = cross_over(0)
    heads.add(0, dkv)
    low.wait_recv()
    far, near = {}, {}
    for k in (3, 2, 0, 1):
        i = order.index(k)
        hand[0, block(k)] = (
            dkv[rows(start_of(k), BLOCK), :].astype(F32) + jnp.where(even, 0.0, cross[0, block(k)].astype(F32))
        ).astype(BF)
        if i < 2:
            far[k] = copies.put(hand.at[0, block(k)], mid.at[i], p.at(dy=1))
        else:
            far[k] = copies.put(hand.at[0, block(k)], land.at[0, block(k)], p.linear(-1))
    heads.add(3, dkv)
    high = cross_over(1)
    for i, k in enumerate(order[:2]):
        far[k].wait_recv()
        far[k] = copies.put(mid.at[i], fin.at[i], p.beside(-1, -2))
    ring.below()
    ring.above()
    outs.pass_on()
    plane.step1()
    heads.add(2, dkv)
    high.wait_recv()

    def near_sum(k):
        beside = jnp.where(even, cross[0, block(k)].astype(F32), cross[1, block(k)].astype(F32))
        return dkv[rows(2 * GROUP + start_of(k), BLOCK), :].astype(F32) + beside

    for k in order[:2]:
        hand[1, block(k)] = near_sum(k).astype(BF)
        near[k] = copies.put(hand.at[1, block(k)], land.at[1, block(k)], p.linear(-1))
    for k in order[2:]:
        far[k].wait_recv()
        hand[1, block(k)] = (near_sum(k) + land[0, block(k)].astype(F32)).astype(BF)
        near[k] = copies.put(hand.at[1, block(k)], land.at[1, block(k)], p.linear(-1))
    plane.step2()
    heads.add(4, dkv, own=True)
    heads.finish(dq)
    ring.far()
    weight_grad(n1, dq, middle, 0)
    weight_grad(gafg, ctx_ref, middle, 256)
    quick2.start()
    dqkv[:, 0:256] = dq[...]
    small_ref[...] = jnp.zeros_like(small_ref)
    small_ref[8:9, :] = sums_ref[4:5, :]
    spread_bias(9, jnp.sum(dq[...].astype(F32), axis=0, keepdims=True))
    small_ref[1:2, :] = sums_ref[0:1, :]
    small_ref[3:6, :] = sums_ref[1:4, :]
    out_ref[...] = res_ref[...] + outs_ref[block(0), :].astype(F32) + outs.received()

    def keep_hat(k, carry):
        here = rows(k * BLOCK, BLOCK)
        hats[here, :], _ = normalised(xg[here, :].astype(F32))
        return carry

    lax.fori_loop(0, 4, keep_hat, 0)
    quick2.step1()

    def own_keys(k):
        near[k].wait_recv()
        value = dkv[rows(4 * GROUP + start_of(k), BLOCK), :].astype(F32) + land[1, block(k)].astype(F32)
        value = value + jnp.where(even, cross[1, block(k)].astype(F32), 0.0)
        if k in order[:2]:
            far[k].wait_recv()
            value = value + fin[order.index(k)].astype(F32)
        dqkv[block(k), 256:768] = value.astype(BF)

    def grad_parts(first, second):
        grad = nt(jnp.concatenate([dqkv[block(first), :], dqkv[block(second), :]], axis=0), wqkv[...])
        return grad[0:BLOCK], grad[BLOCK:2 * BLOCK]

    def tally(k, grad):
        small_ref[0:1, :] += jnp.sum(grad * hats[block(k), :], axis=0, keepdims=True)
        small_ref[2:3, :] += jnp.sum(grad, axis=0, keepdims=True)

    own_keys(2)
    own_keys(1)
    across, above = grad_parts(2, 1)
    scatter.part[2] = across.astype(BF)
    scatter.send_far()
    scatter.part[0] = above.astype(BF)
    tally(2, across)
    tally(1, above)
    own_keys(3)
    own_keys(0)
    weight_grad(n1, dqkv.at[:, 256:768], late, 0)
    quick.start()
    below, here = grad_parts(3, 0)
    scatter.part[1] = below.astype(BF)
    own[...] = here
    tally(3, below)
    tally(0, here)
    spread_bias(10, jnp.sum(dqkv[:, 512:768].astype(F32), axis=0, keepdims=True))

    def lanes(x, width):
        return pl.ds(pl.multiple_of(x * width, 128), width)

    sends = []
    for i, dx in enumerate((1, -1, 2)):
        to = lax.rem(p.x + dx + 4, 4)
        sends.append(copies.put(small_ref.at[:, lanes(to, 256)], xsum.at[i], p.at(dx=dx)))
    scatter.send_above()
    scatter.send_below()
    quick2.step2()
    quick.step1()
    for copy in sends:
        copy.wait_recv()
    line[...] = small_ref[:, lanes(p.x, 256)] + xsum[0] + xsum[1] + xsum[2]
    sends = []
    for dy in (0, 1, -1, 2):
        for flip in (False, True):
            if dy or flip:
                to = lax.rem(p.y + dy + 4, 4) // 2
                sends.append(
                    copies.put(line.at[:, lanes(to, 128)], ysum.at[len(sends)], p.at(dy=dy, flip=flip))
                )
    plane.step3()
    quick.step2()
    hat, scale = normalised(x_ref[...].astype(F32))
    back, _, _ = norm_back(hat, scale, own[...] + scatter.received(), vec_ref[0:1, :])
    gin_ref[...] = gafter_ref[...] + back
    for copy in sends:
        copy.wait_recv()
    total = line[:, lanes(p.y // 2, 128)]
    for i in range(7):
        total = total + ysum[i]
    zsum[3] = total
    sends = [copies.put(zsum.at[3, 0:8], zsum.at[i, 0:8], p.at(dz=dz)) for i, dz in enumerate((1, -1, 2))]
    plane.step4()
    quick2.step3()
    quick.step3()
    plane.step5()
    for copy in sends:
        copy.wait_recv()
    sums_out[0:8] = zsum[3, 0:8] + zsum[0, 0:8] + zsum[1, 0:8] + zsum[2, 0:8]
    sums_out[8:16] = zsum[3, 8:16]
    quick2.step4(mid_ref)
    quick.step4(late_ref)
    plane.step6(early_ref)
    copies.finish()


N5_COPIES = 2 + 4 + 6 + 4 + 4 + 2 + 4 + 18 + 2 * 17 + 3 + 7 + 3


def call_last(*operands):
    shape = jax.ShapeDtypeStruct
    return pl.pallas_call(
        last_kernel,
        out_shape=(
            shape((BLOCK, D), F32),
            shape((BLOCK, D), F32),
            shape((32, 2048), F32),
            shape((32, 512), F32),
            shape((32, 512), F32),
            shape((16, 128), F32),
        ),
        in_specs=[pl.BlockSpec(memory_space=pltpu.SMEM)] + vm(12) + far_memory(4),
        out_specs=tuple(vm(6)),
        scratch_shapes=[
            pltpu.VMEM((GROUP, 256), BF),
            pltpu.VMEM((5 * GROUP, 512), BF),
            pltpu.VMEM((GROUP, D), BF),
            pltpu.VMEM((GROUP, D), BF),
            pltpu.VMEM((D, 768), BF),
            pltpu.VMEM((GROUP, D), BF),
            pltpu.VMEM((2, GROUP, 512), BF),
            pltpu.VMEM((2, GROUP, 512), BF),
            pltpu.VMEM((2, GROUP, 512), BF),
            pltpu.VMEM((2, BLOCK, 512), BF),
            pltpu.VMEM((2, BLOCK, 512), BF),
            pltpu.VMEM((GROUP, 768), BF),
            pltpu.VMEM((D, 2048), BF),
            pltpu.VMEM((D, 512), BF),
            pltpu.VMEM((D, 512), BF),
            pltpu.VMEM((BLOCK, D), F32),
            pltpu.VMEM((GROUP, D), F32),
            pltpu.VMEM((16, D), F32),
            pltpu.VMEM((3, 16, 256), F32),
            pltpu.VMEM((7, 16, 128), F32),
            pltpu.VMEM((4, 16, 128), F32),
            pltpu.VMEM((16, 256), F32),
            pltpu.SemaphoreType.DMA((4,)),
            pltpu.SemaphoreType.DMA((N5_COPIES,)),
            pltpu.SemaphoreType.DMA((N5_COPIES,)),
            *RingScatter.scratch(),
            *RingReturn.scratch(),
            *PlaneScatter.scratch(2048),
            *QuickScatter.scratch(512),
            *AttentionBack.scratch(),
            *QuickScatter.scratch(512),
        ],
        compiler_params=pltpu.CompilerParams(
            collective_id=3, has_side_effects=True, vmem_limit_bytes=VMEM_LIMIT
        ),
        name="project_back",
    )(*operands)


def finish_kernel(
    out_ref, gin_ref, early_ref, mid_ref, late_ref, small_ref,
    out, gin, wqkv, wout, wfc, wproj, bqv, bfc, gains, shifts,
):
    dp, z = lax.axis_index("dp"), lax.axis_index("tensor")
    out[...] = out_ref[...]
    gin[...] = gin_ref[...]
    wqkv[0] = mid_ref[:, 0:256]
    wqkv[1] = late_ref[:, 0:256]
    wqkv[2] = late_ref[:, 256:512]
    wout[...] = mid_ref[:, 256:512]
    wfc[...] = early_ref[:, 0:1024]
    wproj[...] = early_ref[:, 1024:2048]

    def pick(first, offset, width):
        row = lax.broadcasted_iota(jnp.int32, (128, 128), 0)
        lane = lax.broadcasted_iota(jnp.int32, (128, 128), 1)
        chosen = jnp.where(row == lane + lax.rem(offset, 128), 1.0, 0.0).astype(F32)
        return exact(small_ref[first:first + 8, :], chosen)[:, 0:width]

    eight = pick(0, (dp * 4 + z) * 8, 8)
    gains[...] = eight[0:2]
    shifts[...] = eight[2:6]
    bqv[...] = pick(8, dp * 8, 8)[1:3]
    bfc[...] = pick(8, dp * 32, 32)[0:1]


def call_finish(*operands):
    shape = jax.ShapeDtypeStruct
    return pl.pallas_call(
        finish_kernel,
        out_shape=(
            shape((BLOCK, D), F32),
            shape((BLOCK, D), F32),
            shape((3, 32, 256), F32),
            shape((32, 256), F32),
            shape((32, 1024), F32),
            shape((32, 1024), F32),
            shape((2, 8), F32),
            shape((1, 32), F32),
            shape((2, 8), F32),
            shape((4, 8), F32),
        ),
        in_specs=vm(6),
        out_specs=tuple(vm(10)),
        compiler_params=pltpu.CompilerParams(vmem_limit_bytes=VMEM_LIMIT),
        name="lay_out",
    )(*operands)


def on_device(inputs, lengths, w_qkv, w_out, w_fc, w_proj, b_qv, b_fc, gains, shifts, cotangent):
    q, kv, vec, ctx, lse, n1, xg, cotg, wqkv, wo, wfc = call_first(
        lengths, inputs, cotangent, w_qkv[0].transpose(1, 0, 2), w_out[0].T, w_fc[0],
        gains[0], shifts[0], b_qv[0], b_fc,
    )
    gafter, gaf, dctx, sums, res, outs, dw_mlp = call_middle(
        inputs, ctx, vec, w_proj[0].T, wo, wfc, cotg
    )
    gin, out, early, mid, late, small = call_last(
        lengths, q, kv, lse, dctx, inputs, vec, gafter, gaf, ctx, sums, res, outs, n1, xg, wqkv, dw_mlp
    )
    out, gin, g_qkv, g_out, g_fc, g_proj, g_bqv, g_bfc, g_gains, g_shifts = call_finish(
        out, gin, early, mid, late, small
    )
    return (
        out, gin, g_qkv.transpose(1, 0, 2)[None], g_out.T[None], g_fc[None], g_proj.T[None],
        g_bqv[None], g_bfc, g_gains[None], g_shifts[None],
    )


def solution(mesh):
    return jax.shard_map(
        on_device,
        mesh=mesh,
        in_specs=(
            P(("dp", "tensor"), None),
            P(),
            P(None, "dp", None, "tensor"),
            P(None, "tensor", "dp"),
            P(None, "dp", "tensor"),
            P(None, "tensor", "dp"),
            P(None, None, ("tensor", "dp")),
            P(None, ("tensor", "dp")),
            P(None, None, ("dp", "tensor")),
            P(None, None, ("dp", "tensor")),
            P(("dp", "tensor"), None),
        ),
        out_specs=(
            P(("dp", "tensor"), None),
            P(("dp", "tensor"), None),
            P(None, "dp", None, "tensor"),
            P(None, "tensor", "dp"),
            P(None, "dp", "tensor"),
            P(None, "tensor", "dp"),
            P(None, None, ("tensor", "dp")),
            P(None, ("tensor", "dp")),
            P(None, None, ("dp", "tensor")),
            P(None, None, ("dp", "tensor")),
        ),
        check_vma=False,
    )
```

```python
import functools

import jax
import jax.numpy as jnp
from jax import lax
from jax.experimental import pallas as pl
from jax.experimental.pallas import tpu as pltpu
from jax.sharding import PartitionSpec as P

HEAD_DIM = 64
BLOCK = 128
D = 1024
GROUP = 512
SPAN = 512
BF = jnp.bfloat16
F32 = jnp.float32
MESH = pl.DeviceIdType.MESH
VMEM_LIMIT = 58 * 1024 * 1024


def nn(a, b):
    return jnp.dot(a, b, preferred_element_type=F32)


def nt(a, b):
    return lax.dot_general(a, b, (((1,), (1,)), ((), ())), preferred_element_type=F32)


def tn(a, b):
    return lax.dot_general(a, b, (((0,), (0,)), ((), ())), preferred_element_type=F32)


def rows(start, size, step=None):
    return pl.ds(pl.multiple_of(start, step or size), size)


class Place:
    def __init__(self):
        self.dp = lax.axis_index("dp")
        self.z = lax.axis_index("tensor")
        self.c = lax.rem(self.dp, 2)
        self.chip = self.dp // 2
        self.y = lax.rem(self.chip, 4)
        self.x = self.chip // 4

    def at(self, dx=0, dy=0, dz=0, flip=False):
        x = lax.rem(self.x + dx + 4, 4)
        y = lax.rem(self.y + dy + 4, 4)
        c = 1 - self.c if flip else self.c
        return ((x * 4 + y) * 2 + c, lax.rem(self.z + dz + 4, 4))

    def linear(self, step):
        return (lax.rem(self.chip + step + 16, 16) * 2 + self.c, self.z)

    def beside(self, dy, step):
        chip = self.x * 4 + lax.rem(self.y + dy + 4, 4)
        return (lax.rem(chip + step + 16, 16) * 2 + self.c, self.z)

    def beside_source(self, step=2, dy=-1):
        chip = lax.rem(self.chip - step + 16, 16)
        y = lax.rem(lax.rem(chip, 4) + dy + 4, 4)
        return ((chip // 4 * 4 + y) * 2 + self.c, self.z)


class Copies:
    def __init__(self, send_sem, recv_sem):
        self.send_sem, self.recv_sem = send_sem, recv_sem
        self.started, self.settled = [], []

    def put(self, src, dst, device):
        k = len(self.started)
        copy = pltpu.make_async_remote_copy(
            src_ref=src,
            dst_ref=dst,
            send_sem=self.send_sem.at[k],
            recv_sem=self.recv_sem.at[k],
            device_id=device,
            device_id_type=MESH,
        )
        copy.start()
        self.started.append(copy)
        return copy

    def settle(self, *copies):
        for copy in copies:
            copy.wait_send()
            self.settled.append(copy)

    def finish(self):
        for copy in self.started:
            if not any(copy is other for other in self.settled):
                copy.wait_send()


def greet(devices):
    barrier = pltpu.get_barrier_semaphore()
    for device in devices:
        pl.semaphore_signal(barrier, inc=1, device_id=device, device_id_type=MESH)
    pl.semaphore_wait(barrier, len(devices))


class RingGather:
    def __init__(self, copies, place, buf, size=BLOCK):
        self.copies, self.place, self.buf, self.size = copies, place, buf, size

    def block(self, dz, part=None):
        start = lax.rem(self.place.z + dz + 4, 4) * self.size
        if part is None:
            return self.buf.at[rows(start, self.size)]
        half = self.size // 2
        return self.buf.at[rows(start + part * half, half)]

    def start(self):
        own = self.block(0)
        self.up = self.copies.put(own, own, self.place.at(dz=1))
        self.down = self.copies.put(own, own, self.place.at(dz=-1))

    def below(self):
        self.up.wait_recv()
        half = self.block(-1, 0)
        self.up2 = self.copies.put(half, half, self.place.at(dz=1))

    def above(self):
        self.down.wait_recv()
        half = self.block(1, 1)
        self.down2 = self.copies.put(half, half, self.place.at(dz=-1))

    def far(self):
        self.up2.wait_recv()
        self.down2.wait_recv()


class DirectGather:
    copies_needed = 31

    def __init__(self, copies, place, w):
        self.copies, self.place, self.w = copies, place, w
        self.shared = []

    def dev(self, axis, step):
        c = self.place.c
        if axis == 0:
            return self.place.at(dx=c * step, dy=(1 - c) * step)
        return self.place.at(dx=(1 - c) * step, dy=c * step)

    def block(self, a, b):
        p, c = self.place, self.place.c
        x = lax.rem(p.x + b * (1 - c) + a * c + 4, 4)
        y = lax.rem(p.y + a * (1 - c) + b * c + 4, 4)
        return self.w.at[rows(((x * 4 + y) * 2 + c) * 32, 32)]

    def put(self, ref, device):
        return self.copies.put(ref, ref, device)

    def spread(self, a):
        ref = self.block(a, 0)
        self.second[a] = [self.put(ref, self.dev(1, step)) for step in (1, -1, 2)]
        self.shared.append(self.put(ref, self.place.at(flip=True)))

    def start(self):
        ref = self.block(0, 0)
        self.first = [self.put(ref, self.dev(0, step)) for step in (1, -1, 2)]
        self.second = {}
        self.spread(0)

    def step1(self):
        for copy, a in zip(self.first, (-1, 1, 2)):
            copy.wait_recv()
            self.spread(a)

    def step2(self):
        for a in (0, -1, 1, 2):
            for copy, b in zip(self.second[a], (-1, 1, 2)):
                copy.wait_recv()
                self.shared.append(self.put(self.block(a, b), self.place.at(flip=True)))

    def step3(self):
        for copy in self.shared:
            copy.wait_recv()


class PlaneGather:
    def __init__(self, copies, place, w, first, width):
        self.copies, self.place, self.w = copies, place, w
        c = place.c
        self.first, self.width = first, width
        self.cols = pl.ds(pl.multiple_of(first + c * (width // 2), 128), width // 2)

    def dev(self, axis, step):
        if axis == 0:
            return self.place.at(dy=step)
        return self.place.at(dx=step)

    def block(self, first_off, second_off, part=None):
        p = self.place
        start = (lax.rem(p.x + second_off + 4, 4) * 4 + lax.rem(p.y + first_off + 4, 4)) * 64
        if part is None:
            return self.w.at[rows(start, 64), self.cols]
        return self.w.at[rows(start + 32 * part, 32), self.cols]

    def put(self, ref, device):
        return self.copies.put(ref, ref, device)

    def start(self):
        p = self.place
        mine = self.w.at[rows(p.dp * 32, 32), pl.ds(self.first, self.width)]
        self.swap = self.put(mine, p.at(flip=True))

    def spread(self, first_off):
        ref = self.block(first_off, 0)
        return (self.put(ref, self.dev(1, 1)), self.put(ref, self.dev(1, -1)))

    def share(self, first_off, second_off):
        self.shared.append(self.put(self.block(first_off, second_off), self.place.at(flip=True)))

    def step1(self):
        self.swap.wait_recv()
        ref = self.block(0, 0)
        self.shared = []
        self.up = self.put(ref, self.dev(0, 1))
        self.down = self.put(ref, self.dev(0, -1))
        self.out = {0: self.spread(0)}

    def step2(self):
        self.up.wait_recv()
        self.up2 = self.put(self.block(-1, 0, 0), self.dev(0, 1))
        self.down.wait_recv()
        self.down2 = self.put(self.block(1, 0, 1), self.dev(0, -1))
        self.out[-1] = self.spread(-1)
        self.out[1] = self.spread(1)
        self.share(-1, 0)
        self.share(1, 0)

    def step3(self):
        self.up2.wait_recv()
        self.down2.wait_recv()
        self.out[2] = self.spread(2)
        self.share(2, 0)

    def step4(self):
        self.far = []
        for first_off in (0, -1, 1, 2):
            up, down = self.out[first_off]
            up.wait_recv()
            self.far.append(self.put(self.block(first_off, -1, 0), self.dev(1, 1)))
            down.wait_recv()
            self.far.append(self.put(self.block(first_off, 1, 1), self.dev(1, -1)))
            self.share(first_off, -1)
            self.share(first_off, 1)

    def step5(self):
        for k, first_off in enumerate((0, -1, 1, 2)):
            self.far[2 * k].wait_recv()
            self.far[2 * k + 1].wait_recv()
            self.share(first_off, 2)

    def step6(self):
        for copy in self.shared:
            copy.wait_recv()


def normalised(values):
    centre = values - jnp.mean(values, axis=-1, keepdims=True)
    spread = jnp.mean(centre * centre, axis=-1, keepdims=True)
    scale = lax.rsqrt(spread + 1e-05)
    return centre * scale, scale


def first_blocks(lengths_ref):
    base = lax.axis_index("dp") * 4
    end = jnp.int32(0)
    first = [jnp.int32(0)] * 4
    for i in range(32):
        end = end + lengths_ref[i]
        first = [jnp.where(end <= base + b, end, first[b]) for b in range(4)]
    return [first[b] - base + 16 for b in range(4)]


def heads_across(tile):
    head = lax.broadcasted_iota(jnp.int32, tile.shape, 1) // HEAD_DIM
    return jnp.concatenate([jnp.where(head == h, tile, 0.0) for h in range(4)], axis=0)


def heads_together(tile):
    head = lax.broadcasted_iota(jnp.int32, (BLOCK, 256), 1) // HEAD_DIM
    return sum(jnp.where(head == h, tile[h * BLOCK:(h + 1) * BLOCK], 0.0) for h in range(4))


def causal(scores, b):
    query = lax.rem(lax.broadcasted_iota(jnp.int32, scores.shape, 0), BLOCK)
    key = lax.broadcasted_iota(jnp.int32, scores.shape, 1)
    return jnp.where(key <= query + b * BLOCK, scores, -1e30)


def outside(block, first):
    lane = lax.broadcasted_iota(jnp.int32, (1, SPAN), 1)
    return jnp.where(lane < (first - block) * BLOCK, -1e30, 0.0)


def parts(tile):
    return [tile[:, i * 128:(i + 1) * 128] for i in range(SPAN // 128)]


def pick_first(first, b):
    value = first[3]
    for k in range(3):
        value = jnp.where(b == k, first[k], value)
    return value


class Attention:
    def __init__(self, lengths_ref, q_ref, kv_ref, scratch):
        self.first = first_blocks(lengths_ref)
        self.q_ref, self.kv_ref = q_ref, kv_ref
        self.tall, self.top, self.total, self.acc = scratch

    @staticmethod
    def scratch():
        return [
            pltpu.VMEM((4, 512, 256), BF),
            pltpu.VMEM((4, 512, 128), F32),
            pltpu.VMEM((4, 512, 128), F32),
            pltpu.VMEM((4, 512, 256), F32),
        ]

    def start(self):
        for b in range(4):
            queries = self.q_ref[b * BLOCK:(b + 1) * BLOCK, :].astype(F32) * 0.125
            self.tall[b] = heads_across(queries).astype(BF)

    def add(self, slot, own=False):
        keys = rows(slot * GROUP, GROUP)

        def one(b):
            tile = nt(self.tall[b], self.kv_ref[keys, 0:256]) + outside(slot * 4, self.of_block(b))
            if own:
                tile = causal(tile, b)
            pieces = parts(tile)
            peak = jnp.max(functools.reduce(jnp.maximum, pieces), axis=1, keepdims=True)
            top = jnp.broadcast_to(peak, (512, 128))
            if not own:
                top = jnp.maximum(top, self.top[b])
            weights = [jnp.exp(piece - top) for piece in pieces]
            low = jnp.concatenate([piece.astype(BF) for piece in weights], axis=1)
            product = nn(low, self.kv_ref[keys, 256:512])
            if own:
                self.total[b] = sum(weights)
                self.acc[b] = product
            else:
                shrink = jnp.exp(self.top[b] - top)
                self.total[b] = self.total[b] * shrink + sum(weights)
                self.acc[b] = self.acc[b] * jnp.concatenate([shrink, shrink], axis=1) + product
            self.top[b] = top

        def two(i, carry):
            one(2 * i)
            one(2 * i + 1)
            return carry

        lax.fori_loop(0, 2, two, 0)

    def of_block(self, b):
        return pick_first(self.first, b)

    def finish(self, ctx_ref, lse_ref):
        for b in range(4):
            sums = jnp.sum(self.total[b], axis=1, keepdims=True)
            lse_ref[b] = self.top[b] + jnp.log(sums)
            ctx_ref[b * BLOCK:(b + 1) * BLOCK, :] = heads_together(self.acc[b] * (1.0 / sums)).astype(BF)


class AttentionBack:
    def __init__(self, lengths_ref, q_ref, kv_ref, ctx_ref, lse_ref, dctx_ref, scratch):
        self.first = first_blocks(lengths_ref)
        self.q_ref, self.kv_ref, self.ctx_ref = q_ref, kv_ref, ctx_ref
        self.lse_ref, self.dctx_ref = lse_ref, dctx_ref
        self.tall_q, self.tall_g, self.inner, self.acc, self.sum = scratch
        self.sum[...] = jnp.zeros_like(self.sum)

    @staticmethod
    def scratch():
        return [
            pltpu.VMEM((2048, 256), BF),
            pltpu.VMEM((2048, 256), BF),
            pltpu.VMEM((4, 512, 128), F32),
            pltpu.VMEM((4, 512, 256), F32),
            pltpu.VMEM((512, 512), F32),
        ]

    def start(self):
        for b in range(4):
            block, tall = slice(b * BLOCK, (b + 1) * BLOCK), slice(b * 512, (b + 1) * 512)
            grads = self.dctx_ref[block, :].astype(F32)
            self.tall_q[tall, :] = heads_across(self.q_ref[block, :].astype(F32) * 0.125).astype(BF)
            self.tall_g[tall, :] = heads_across(grads).astype(BF)
            product = heads_across(grads * self.ctx_ref[block, :].astype(F32))
            self.inner[b] = jnp.broadcast_to(jnp.sum(product, axis=1, keepdims=True), (512, 128))
            self.acc[b] = jnp.zeros((512, 256), F32)

    def add(self, slot, dkv, own=False):
        keys = rows(slot * GROUP, GROUP)

        def one(b):
            tall = rows(b * 512, 512)
            tile = nt(self.tall_q[tall, :], self.kv_ref[keys, 0:256])
            tile = tile + outside(slot * 4, pick_first(self.first, b))
            if own:
                tile = causal(tile, b)
            weight = jnp.exp(tile - jnp.concatenate([self.lse_ref[b]] * 4, axis=1))
            grad = nt(self.tall_g[tall, :], self.kv_ref[keys, 256:512])
            low = (weight * (grad - jnp.concatenate([self.inner[b]] * 4, axis=1))).astype(BF)
            self.acc[b] += nn(low, self.kv_ref[keys, 0:256])
            return low, weight.astype(BF)

        def two(i, carry):
            low, weights = zip(one(2 * i), one(2 * i + 1))
            tall = rows(i * 1024, 1024)
            grads = (
                tn(jnp.concatenate(low, axis=0), self.tall_q[tall, :]),
                tn(jnp.concatenate(weights, axis=0), self.tall_g[tall, :]),
            )
            for k, grad in enumerate(grads):
                cols = slice(k * 256, (k + 1) * 256)
                total = jnp.where(i == 0, 0.0, self.sum[:, cols]) + grad
                self.sum[:, cols] = total
                dkv[keys, cols] = total.astype(BF)
            return carry

        lax.fori_loop(0, 2, two, 0)

    def finish(self, dq):
        for b in range(4):
            dq[b * BLOCK:(b + 1) * BLOCK, :] = heads_together(self.acc[b] * 0.125).astype(BF)


def one_hot(shape, offset):
    row = lax.broadcasted_iota(jnp.int32, shape, 0)
    lane = lax.broadcasted_iota(jnp.int32, shape, 1)
    return jnp.where(lane == row + offset, 1.0, 0.0).astype(F32)


def exact(a, b):
    return jnp.dot(a, b, precision=lax.Precision.HIGHEST, preferred_element_type=F32)


def first_kernel(
    lengths_ref, x_ref, cot_ref, wqkv_ref, wout_ref, wfc_ref, gains_ref, shifts_ref, bqv_ref, bfc_ref,
    q_ref, kv_ref, vec_ref, ctx_ref, lse_ref, n1_out, xg_out, cotg_out, wqkv_out, wo_out, wfc_out,
    n1, xg, cotg, wq, wo, wfc, vz, vall, bias, mid, out_sem, send_sem, recv_sem, *scratch,
):
    p = Place()
    mine = rows(p.dp * 32, 32)
    for j in range(3):
        wq[mine, j * 256:(j + 1) * 256] = wqkv_ref[j]
    wq[mine, 768:1024] = wout_ref[...]
    wfc[mine, :] = wfc_ref[...]
    xg[rows(p.z * BLOCK, BLOCK), :] = x_ref[...]
    cotg[rows(p.z * BLOCK, BLOCK), :] = cot_ref[...]
    place8 = one_hot((8, 128), lax.rem(p.dp * 4 + p.z, 16) * 8)
    own = vz.at[p.z]
    own[...] = jnp.zeros((8, 128), F32)
    own[0:2] = exact(gains_ref[...], place8)
    own[2:6] = exact(shifts_ref[...], place8)
    tile = vall.at[p.c, p.chip]
    tile[8:16] = jnp.zeros((8, 128), F32)
    tile[8:9] = exact(bfc_ref[...].astype(F32), one_hot((32, 128), lax.rem(p.dp, 4) * 32))
    tile[9:11] = exact(bqv_ref[...].astype(F32), one_hot((8, 128), lax.rem(p.dp, 16) * 8))
    greet(
        [p.at(dz=1), p.at(dz=-1), p.at(dz=2), p.at(dx=1), p.at(dx=-1), p.at(dx=2),
         p.at(dy=1), p.at(dy=-1), p.at(dy=2), p.at(flip=True), p.linear(1), p.linear(-1),
         p.beside(1, 2), p.beside_source()]
    )
    copies = Copies(send_sem, recv_sem)
    head = DirectGather(copies, p, wq)
    head.start()
    small = [copies.put(own, own, p.at(dz=dz)) for dz in (1, -1, 2)]
    ring = RingGather(copies, p, xg)
    ring.start()
    tail = PlaneGather(copies, p, wfc, 0, 1024)
    for copy in small:
        copy.wait_recv()
    tile[0:8] = vz[0] + vz[1] + vz[2] + vz[3]
    small = [copies.put(tile, tile, p.at(dy=dy)) for dy in (1, -1, 2)]
    head.step1()
    tail.start()
    for copy in small:
        copy.wait_recv()
    line = vall.at[p.c, rows(p.x * 4, 4)]
    small = [copies.put(line, line, p.at(dx=dx)) for dx in (1, -1, 2)]
    ring.below()
    ring.above()
    cot_ring = RingGather(copies, p, cotg)
    cot_ring.start()
    for copy in small:
        copy.wait_recv()
    plane = vall.at[p.c]
    last = copies.put(plane, plane, p.at(flip=True))
    head.step2()
    tail.step1()
    ring.far()
    last.wait_recv()
    lanes = []
    for k in range(8):
        total = vall[0, 2 * k] + vall[0, 2 * k + 1] + vall[1, 2 * k] + vall[1, 2 * k + 1]
        vec_ref[:, k * 128:(k + 1) * 128] = total
        lanes.append(total)
    for h in range(2):
        bias[:, h * 128:(h + 1) * 128] = lanes[4 * h] + lanes[4 * h + 1] + lanes[4 * h + 2] + lanes[4 * h + 3]

    def norm_block(k, carry):
        block = rows(lax.rem(p.z + k, 4) * BLOCK, BLOCK)
        hat, _ = normalised(xg[block, :].astype(F32))
        n1[block, :] = (hat * vec_ref[0:1, :] + vec_ref[2:3, :]).astype(BF)
        return carry

    lax.fori_loop(0, 4, norm_block, 0)
    cot_ring.below()
    cot_ring.above()
    head.step3()

    def start_of(k):
        return lax.rem(p.z + k, 4) * BLOCK

    sibling = p.at(flip=True)
    near, there, cross = {}, {}, []
    for pair in ((2, 0), (3, 1)):
        values = jnp.concatenate([n1[rows(start_of(k), BLOCK), :] for k in pair], axis=0)
        keys = nn(values, wq[:, 256:512]).astype(BF)
        vals = (nn(values, wq[:, 512:768]) + bias[10:11, :]).astype(BF)
        for i, k in enumerate(pair):
            ours = rows(4 * GROUP + start_of(k), BLOCK)
            kv_ref[ours, 0:256] = keys[i * BLOCK:(i + 1) * BLOCK]
            kv_ref[ours, 256:512] = vals[i * BLOCK:(i + 1) * BLOCK]
            if k < 2:
                there[k] = copies.put(kv_ref.at[ours], mid.at[k], p.at(dy=-1))
            else:
                near[k] = copies.put(
                    kv_ref.at[ours], kv_ref.at[rows(2 * GROUP + start_of(k), BLOCK)], p.linear(1)
                )
    for k in (0, 1):
        ours = kv_ref.at[rows(4 * GROUP + start_of(k), BLOCK)]
        near[k] = copies.put(ours, kv_ref.at[rows(2 * GROUP + start_of(k), BLOCK)], p.linear(1))
    wo[rows(p.z * D, D), :] = wq[:, 768:1024]
    wo_ring = RingGather(copies, p, wo, D)
    wo_ring.start()
    tail.step2()
    q_ref[...] = (nn(n1[...], wq[:, 0:256]) + bias[9:10, :]).astype(BF)
    saves = [
        pltpu.make_async_copy(source, target, out_sem.at[i])
        for i, (source, target) in enumerate(
            (
                (n1, n1_out), (xg, xg_out), (wq.at[:, 0:768], wqkv_out), (cotg, cotg_out),
                (wo, wo_out), (wfc, wfc_out),
            )
        )
    ]
    for i in range(3):
        saves[i].start()
    heads = Attention(lengths_ref, q_ref, kv_ref, scratch)
    heads.start()
    heads.add(4, own=True)
    far = {}
    for k in (0, 1):
        there[k].wait_recv()
        far[k] = copies.put(mid.at[k], kv_ref.at[rows(start_of(k), BLOCK)], p.beside(1, 2))

    def pass_near(k, onward):
        near[k].wait_recv()
        ref = kv_ref.at[rows(2 * GROUP + start_of(k), BLOCK)]
        if onward:
            far[k] = copies.put(ref, kv_ref.at[rows(start_of(k), BLOCK)], p.linear(1))
        cross.append(
            copies.put(ref, kv_ref.at[rows((1 + 2 * p.c) * GROUP + start_of(k), BLOCK)], sibling)
        )

    pass_near(2, True)
    pass_near(3, True)
    tail.step3()
    cot_ring.far()
    saves[3].start()
    tail.step4()
    pass_near(0, False)
    pass_near(1, False)
    wo_ring.below()
    wo_ring.above()

    def pass_far(k):
        far[k].wait_recv()
        cross.append(
            copies.put(
                kv_ref.at[rows((4 - 4 * p.c) * GROUP + start_of(k), BLOCK)],
                kv_ref.at[rows((3 - 2 * p.c) * GROUP + start_of(k), BLOCK)],
                sibling,
            )
        )

    heads.add(2)
    pass_far(0)
    pass_far(1)
    tail.step5()
    for copy in cross[:4]:
        copy.wait_recv()
    heads.add(3 - 2 * p.c)
    pass_far(2)
    pass_far(3)
    tail.step6()
    saves[5].start()
    heads.add(0)
    wo_ring.far()
    saves[4].start()
    for copy in cross[4:]:
        copy.wait_recv()
    heads.add(1 + 2 * p.c)
    heads.finish(ctx_ref, lse_ref)
    for save in saves:
        save.wait()
    copies.finish()


N1_COPIES = 31 + 36 + 10 + 12 + 18


def vm(count):
    return [pl.BlockSpec(memory_space=pltpu.VMEM)] * count


def far_memory(count):
    return [pl.BlockSpec(memory_space=pl.ANY)] * count


def call_first(*operands):
    shape = jax.ShapeDtypeStruct
    return pl.pallas_call(
        first_kernel,
        out_shape=(
            shape((GROUP, 256), BF),
            shape((5 * GROUP, 512), BF),
            shape((16, D), F32),
            shape((GROUP, 256), BF),
            shape((4, 512, 128), F32),
            shape((GROUP, D), BF),
            shape((GROUP, D), BF),
            shape((GROUP, D), BF),
            shape((D, 768), BF),
            shape((4 * D, 256), BF),
            shape((D, D), BF),
        ),
        in_specs=[pl.BlockSpec(memory_space=pltpu.SMEM)] + vm(9),
        out_specs=tuple(vm(5) + far_memory(6)),
        scratch_shapes=[
            pltpu.VMEM((GROUP, D), BF),
            pltpu.VMEM((GROUP, D), BF),
            pltpu.VMEM((GROUP, D), BF),
            pltpu.VMEM((D, 1024), BF),
            pltpu.VMEM((4 * D, 256), BF),
            pltpu.VMEM((D, D), BF),
            pltpu.VMEM((4, 8, 128), F32),
            pltpu.VMEM((2, 16, 16, 128), F32),
            pltpu.VMEM((16, 256), F32),
            pltpu.VMEM((2, BLOCK, 512), BF),
            pltpu.SemaphoreType.DMA((6,)),
            pltpu.SemaphoreType.DMA((N1_COPIES,)),
            pltpu.SemaphoreType.DMA((N1_COPIES,)),
            *Attention.scratch(),
        ],
        compiler_params=pltpu.CompilerParams(
            collective_id=1, has_side_effects=True, vmem_limit_bytes=VMEM_LIMIT
        ),
        name="gather_and_project",
    )(*operands)


class PlaneScatter:
    copies_needed = 18

    def __init__(self, copies, place, g, scratch):
        self.copies, self.place, self.g = copies, place, g
        self.land, self.far, self.near, self.t, self.far2, self.near2, self.last, self.rest = scratch
        self.half = g.shape[1] // 2

    @staticmethod
    def scratch(width):
        half = width // 2
        return [
            pltpu.VMEM((1024, half), BF),
            pltpu.VMEM((2, 2, 64, half), BF),
            pltpu.VMEM((2, 4, 64, half), BF),
            pltpu.VMEM((4, 64, half), BF),
            pltpu.VMEM((2, 32, half), BF),
            pltpu.VMEM((2, 64, half), BF),
            pltpu.VMEM((32, half), F32),
            pltpu.VMEM((32, half), F32),
        ]

    def dev(self, axis, step):
        c = self.place.c
        if axis == 0:
            return self.place.at(dx=(1 - c) * step, dy=c * step)
        return self.place.at(dx=c * step, dy=(1 - c) * step)

    def first(self, step):
        p = self.place
        return lax.rem(p.x * (1 - p.c) + p.y * p.c + step + 4, 4)

    def second(self, step):
        p = self.place
        return lax.rem(p.y * (1 - p.c) + p.x * p.c + step + 4, 4)

    def block(self, f, s):
        c = self.place.c
        x, y = f * (1 - c) + s * c, s * (1 - c) + f * c
        return rows((x * 4 + y) * 64, 64)

    def start(self):
        c = self.place.c
        other = pl.ds(pl.multiple_of((1 - c) * self.half, 128), self.half)
        self.swap = self.copies.put(self.g.at[:, other], self.land, self.place.at(flip=True))

    def step1(self):
        self.swap.wait_recv()
        mine = pl.ds(pl.multiple_of(self.place.c * self.half, 128), self.half)
        self.mine = mine

        def join(k, carry):
            f = self.first(2 + k // 4)
            block = self.block(f, lax.rem(k, 4))
            self.land[block, :] = (self.land[block, :].astype(F32) + self.g[block, mine].astype(F32)).astype(BF)
            return carry

        lax.fori_loop(0, 4, join, 0)
        self.out = []
        for s in range(4):
            to = self.dev(0, 1 if s < 2 else -1)
            self.out.append(
                self.copies.put(self.land.at[self.block(self.first(2), s)], self.far.at[s // 2, s % 2], to)
            )
        lax.fori_loop(4, 16, join, 0)

    def step2(self):
        self.out2 = []
        for side, step in ((0, 1), (1, -1)):
            f = self.first(step)
            for s in range(4):
                block = self.block(f, s)
                if s // 2 == side:
                    self.out[s].wait_recv()
                    self.land[block, :] = (
                        self.land[block, :].astype(F32) + self.far[side, s % 2].astype(F32)
                    ).astype(BF)
                self.out2.append(
                    self.copies.put(self.land.at[block], self.near.at[side, s], self.dev(0, step))
                )

    def step3(self):
        f = self.first(0)
        for copy in self.out2:
            copy.wait_recv()

        def total(k, carry):
            s = self.second(2 + k)
            self.t[s] = (
                self.land[self.block(f, s), :].astype(F32)
                + self.near[0, s].astype(F32)
                + self.near[1, s].astype(F32)
            ).astype(BF)
            return carry

        lax.fori_loop(0, 1, total, 0)
        s = self.second(2)
        self.up = self.copies.put(self.t.at[s, 0:32], self.far2.at[0], self.dev(1, 1))
        self.down = self.copies.put(self.t.at[s, 32:64], self.far2.at[1], self.dev(1, -1))
        lax.fori_loop(1, 4, total, 0)

    def step4(self):
        s = self.second(1)
        self.up.wait_recv()
        self.t[s, 0:32] = (self.t[s, 0:32].astype(F32) + self.far2[0].astype(F32)).astype(BF)
        self.up2 = self.copies.put(self.t.at[s], self.near2.at[0], self.dev(1, 1))
        s = self.second(-1)
        self.down.wait_recv()
        self.t[s, 32:64] = (self.t[s, 32:64].astype(F32) + self.far2[1].astype(F32)).astype(BF)
        self.down2 = self.copies.put(self.t.at[s], self.near2.at[1], self.dev(1, -1))

    def part(self, c):
        half = rows(c * 32, 32)
        return (
            self.t[self.second(0), half].astype(F32)
            + self.near2[0, half].astype(F32)
            + self.near2[1, half].astype(F32)
        )

    def step5(self):
        self.up2.wait_recv()
        self.down2.wait_recv()
        c = self.place.c
        self.last[...] = self.part(1 - c)
        self.back = self.copies.put(self.last, self.rest, self.place.at(flip=True))

    def step6(self, out):
        out[:, self.mine] = self.part(self.place.c)
        self.back.wait_recv()
        other = pl.ds(pl.multiple_of((1 - self.place.c) * self.half, 128), self.half)
        out[:, other] = self.rest[...]


class QuickScatter:
    copies_needed = 17

    def __init__(self, copies, place, g, scratch):
        self.copies, self.place, self.g = copies, place, g
        self.land, self.near, self.t, self.near2, self.last, self.rest = scratch
        self.half = g.shape[1] // 2

    @staticmethod
    def scratch(width):
        half = width // 2
        return [
            pltpu.VMEM((1024, half), BF),
            pltpu.VMEM((3, 4, 64, half), BF),
            pltpu.VMEM((4, 64, half), BF),
            pltpu.VMEM((3, 64, half), BF),
            pltpu.VMEM((32, half), F32),
            pltpu.VMEM((32, half), F32),
        ]

    dev, first, second, block, start = (
        PlaneScatter.dev, PlaneScatter.first, PlaneScatter.second, PlaneScatter.block, PlaneScatter.start
    )

    def step1(self):
        self.swap.wait_recv()
        self.mine = pl.ds(pl.multiple_of(self.place.c * self.half, 128), self.half)
        self.out = []
        for i, step in enumerate((2, 1, -1, 0)):
            f = self.first(step)

            def join(s, carry):
                block = self.block(f, s)
                self.land[block, :] = (
                    self.land[block, :].astype(F32) + self.g[block, self.mine].astype(F32)
                ).astype(BF)
                return carry

            lax.fori_loop(0, 4, join, 0)
            if step:
                for s in range(4):
                    self.out.append(
                        self.copies.put(self.land.at[self.block(f, s)], self.near.at[i, s], self.dev(0, step))
                    )

    def step2(self):
        for copy in self.out:
            copy.wait_recv()
        f = self.first(0)

        def total(s, carry):
            value = self.land[self.block(f, s), :].astype(F32)
            for i in range(3):
                value = value + self.near[i, s].astype(F32)
            self.t[s] = value.astype(BF)
            return carry

        lax.fori_loop(0, 4, total, 0)
        self.out2 = [
            self.copies.put(self.t.at[self.second(step)], self.near2.at[i], self.dev(1, step))
            for i, step in enumerate((2, 1, -1))
        ]

    def part(self, c):
        half = rows(c * 32, 32)
        value = self.t[self.second(0), half].astype(F32)
        for i in range(3):
            value = value + self.near2[i, half].astype(F32)
        return value

    def step3(self):
        for copy in self.out2:
            copy.wait_recv()
        self.last[...] = self.part(1 - self.place.c)
        self.back = self.copies.put(self.last, self.rest, self.place.at(flip=True))

    step4 = PlaneScatter.step6


class RingScatter:
    copies_needed = 4

    def __init__(self, copies, place, scratch):
        self.copies, self.place = copies, place
        self.part, self.far, self.near = scratch

    @staticmethod
    def scratch():
        return [
            pltpu.VMEM((3, BLOCK, D), BF),
            pltpu.VMEM((2, 64, D), BF),
            pltpu.VMEM((2, BLOCK, D), BF),
        ]

    def send_far(self):
        p, c = self.place, self.copies
        self.up = c.put(self.part.at[2, 0:64], self.far.at[0], p.at(dz=1))
        self.down = c.put(self.part.at[2, 64:128], self.far.at[1], p.at(dz=-1))

    def send_above(self):
        self.up.wait_recv()
        self.part[0, 0:64] = (self.part[0, 0:64].astype(F32) + self.far[0].astype(F32)).astype(BF)
        self.up2 = self.copies.put(self.part.at[0], self.near.at[0], self.place.at(dz=1))

    def send_below(self):
        self.down.wait_recv()
        self.part[1, 64:128] = (self.part[1, 64:128].astype(F32) + self.far[1].astype(F32)).astype(BF)
        self.down2 = self.copies.put(self.part.at[1], self.near.at[1], self.place.at(dz=-1))

    def received(self):
        self.up2.wait_recv()
        self.down2.wait_recv()
        return self.near[0].astype(F32) + self.near[1].astype(F32)


class RingReturn:
    copies_needed = 6

    def __init__(self, copies, place, scratch):
        self.copies, self.place = copies, place
        self.above, self.below, self.across, self.near, self.mid, self.far = scratch

    @staticmethod
    def scratch():
        return [
            pltpu.VMEM((2, BLOCK, D), BF),
            pltpu.VMEM((2, 64, D), BF),
            pltpu.VMEM((BLOCK, D), BF),
        ]

    def send_above(self):
        self.up = self.copies.put(self.above, self.near.at[0], self.place.at(dz=1))

    def send_below(self):
        self.down = self.copies.put(self.below, self.near.at[1], self.place.at(dz=-1))

    def send_far(self):
        p, c = self.place, self.copies
        self.up1 = c.put(self.across.at[0:64], self.mid.at[0], p.at(dz=1))
        self.down1 = c.put(self.across.at[64:128], self.mid.at[1], p.at(dz=-1))

    def pass_on(self):
        p, c = self.place, self.copies
        self.up1.wait_recv()
        self.up2 = c.put(self.mid.at[0], self.far.at[0:64], p.at(dz=1))
        self.down1.wait_recv()
        self.down2 = c.put(self.mid.at[1], self.far.at[64:128], p.at(dz=-1))

    def received(self):
        for copy in (self.up, self.down, self.up2, self.down2):
            copy.wait_recv()
        return self.near[0].astype(F32) + self.near[1].astype(F32) + self.far[...].astype(F32)


def norm_back(hat, scale, grad, gain):
    inner = grad * gain
    mean = jnp.mean(inner, axis=-1, keepdims=True)
    along = jnp.mean(inner * hat, axis=-1, keepdims=True)
    return (
        scale * (inner - mean - hat * along),
        jnp.sum(grad * hat, axis=0, keepdims=True),
        jnp.sum(grad, axis=0, keepdims=True),
    )


def weight_grad(left, right, out, first):
    width = right.shape[1]

    def tile(k, carry):
        turned = left[:, pl.ds(pl.multiple_of(k * 256, 256), 256)].astype(F32).T.astype(BF)
        out[rows(k * 256, 256), first:first + width] = nn(turned, right[...]).astype(BF)
        return carry

    lax.fori_loop(0, 4, tile, 0)


def middle_kernel(
    x_ref, ctx_ref, vec_ref, wproj_ref, wo_any, wfc_any, cotg_any,
    gafter_ref, gaf_ref, dctx_ref, sums_ref, res_ref, outs_ref, dw_any,
    wo, wfc, wproj, cotg, ctxf, n2g, act, dpre, dact, part, back, own, after, dw, dctx, io_sem, send_sem, recv_sem,
    *scratch,
):
    p = Place()
    loads = [
        pltpu.make_async_copy(source, target, io_sem.at[i])
        for i, (source, target) in enumerate(((wo_any, wo), (cotg_any, cotg), (wfc_any, wfc)))
    ]
    for load in loads:
        load.start()
    wproj[rows(p.dp * 32, 32), :] = wproj_ref[...]
    greet(
        [p.at(dz=1), p.at(dz=-1), p.at(dz=2), p.at(dx=1), p.at(dx=-1), p.at(dx=2),
         p.at(dy=1), p.at(dy=-1), p.at(dy=2), p.at(flip=True)]
    )
    copies = Copies(send_sem, recv_sem)
    backs = RingReturn(copies, p, (part.at[0], part.at[1], part.at[2]) + scratch)

    def block(dz):
        return rows(lax.rem(p.z + dz + 4, 4) * BLOCK, BLOCK)

    swaps = [
        copies.put(ctx_ref.at[block(dz)], ctxf.at[p.z], p.at(dz=dz)) for dz in (2, 1, -1)
    ]
    plane = DirectGather(copies, p, wproj)
    plane.start()
    ctxf[p.z] = ctx_ref[block(0), :]
    for load in loads:
        load.wait()

    plane.step1()
    for copy in swaps:
        copy.wait_recv()
    total = x_ref[...].astype(F32) + vec_ref[4:5, :]
    for k in range(4):
        total = total + nt(ctxf[k], wo[k * D:(k + 1) * D, :])
    after[...] = total
    hat, scale = normalised(after[...])
    n2g[block(0), :] = (hat * vec_ref[1:2, :] + vec_ref[3:4, :]).astype(BF)
    ring = RingGather(copies, p, n2g)
    ring.start()
    plane.step2()
    ring.below()
    ring.above()
    plane.step3()

    def act_grad(t, carry):
        cols = pl.ds(pl.multiple_of(t * 256, 256), 256)
        dact[:, cols] = nn(cotg[...], wproj[:, cols])
        return carry

    lax.fori_loop(0, 4, act_grad, 0)

    def mlp(pair, put_back):
        here = [block(dz) for dz in pair]

        def both(ref, cols=slice(None)):
            return jnp.concatenate([ref[h, cols] for h in here], axis=0)

        def hidden(t, carry):
            cols = pl.ds(pl.multiple_of(t * 256, 256), 256)
            pre = nn(both(n2g), wfc[:, cols]) + vec_ref[8:9, cols]
            square = pre * pre
            bend = jnp.tanh(0.7978845608028654 * pre * (1.0 + 0.044715 * square))
            slope = 0.5 * (1.0 + bend) + 0.5 * pre * (1.0 - bend * bend) * (
                0.7978845608028654 * (1.0 + 0.134145 * square)
            )
            value = (0.5 * pre * (1.0 + bend)).astype(BF)
            grad = (both(dact, cols) * slope).astype(BF)
            for i, h in enumerate(here):
                act[h, cols] = value[i * BLOCK:(i + 1) * BLOCK]
                dpre[h, cols] = grad[i * BLOCK:(i + 1) * BLOCK]
            return carry

        lax.fori_loop(0, 4, hidden, 0)

        def project(t, carry):
            cols = pl.ds(pl.multiple_of(t * 256, 256), 256)
            value = nt(both(dpre), wfc[cols, :])
            for i in range(2):
                put_back[i](cols, value[i * BLOCK:(i + 1) * BLOCK])
            return carry

        lax.fori_loop(0, 4, project, 0)

    def into(i):
        def put(cols, value):
            part[i, :, cols] = value.astype(BF)

        return put

    def keep(cols, value):
        own[:, cols] = value

    mlp((1, -1), (into(0), into(1)))
    backs.send_above()
    backs.send_below()
    ring.far()
    mlp((2, 0), (into(2), keep))
    backs.send_far()
    weight_grad(n2g, dpre, dw, 0)
    backs.pass_on()
    weight_grad(cotg, act, dw, 1024)
    save = pltpu.make_async_copy(dw, dw_any, io_sem.at[3])
    save.start()
    def output_part(t, carry):
        cols = pl.ds(pl.multiple_of(t * 256, 256), 256)
        outs_ref[:, cols] = nt(act[...], wproj[cols, :]).astype(BF)
        return carry

    lax.fori_loop(0, 4, output_part, 0)
    res_ref[...] = after[...] + vec_ref[5:6, :]
    grad = own[...] + backs.received()
    hat, scale = normalised(after[...])
    grad_in, gain, shift = norm_back(hat, scale, grad, vec_ref[1:2, :])
    residual = cotg[block(0), :].astype(F32)
    back[...] = grad_in + residual
    gaf_ref[...] = back[...].astype(BF)
    for k in (2, 1, 3, 0):
        owner = lax.rem(p.z + k, 4)
        part = nn(gaf_ref[...], wo[rows(owner * D, D), :]).astype(BF)
        if k:
            dctx[k] = part
            swaps.append(copies.put(dctx.at[k], dctx_ref.at[block(0)], p.at(dz=k)))
        else:
            dctx_ref[block(0), :] = part
    sums_ref[...] = jnp.zeros_like(sums_ref)
    sums_ref[0:1, :] = gain
    sums_ref[1:2, :] = shift
    sums_ref[2:3, :] = jnp.sum(back[...], axis=0, keepdims=True)
    sums_ref[3:4, :] = jnp.sum(residual, axis=0, keepdims=True)
    sums_ref[4:5, :] = jnp.sum(dpre[...].astype(F32), axis=0, keepdims=True)
    gafter_ref[...] = back[...]

    for copy in swaps[3:]:
        copy.wait_recv()
    save.wait()
    copies.finish()


N3_COPIES = 6 + 4 + 6 + 31


def call_middle(*operands):
    shape = jax.ShapeDtypeStruct
    return pl.pallas_call(
        middle_kernel,
        out_shape=(
            shape((BLOCK, D), F32),
            shape((BLOCK, D), BF),
            shape((GROUP, 256), BF),
            shape((8, D), F32),
            shape((BLOCK, D), F32),
            shape((GROUP, D), BF),
            shape((D, 2048), BF),
        ),
        in_specs=vm(4) + far_memory(3),
        out_specs=tuple(vm(6) + far_memory(1)),
        scratch_shapes=[
            pltpu.VMEM((4 * D, 256), BF),
            pltpu.VMEM((D, D), BF),
            pltpu.VMEM((D, D), BF),
            pltpu.VMEM((GROUP, D), BF),
            pltpu.VMEM((4, BLOCK, 256), BF),
            pltpu.VMEM((GROUP, D), BF),
            pltpu.VMEM((GROUP, D), BF),
            pltpu.VMEM((GROUP, D), BF),
            pltpu.VMEM((GROUP, D), F32),
            pltpu.VMEM((3, BLOCK, D), BF),
            pltpu.VMEM((BLOCK, D), F32),
            pltpu.VMEM((BLOCK, D), F32),
            pltpu.VMEM((BLOCK, D), F32),
            pltpu.VMEM((D, 2048), BF),
            pltpu.VMEM((4, BLOCK, 256), BF),
            pltpu.SemaphoreType.DMA((4,)),
            pltpu.SemaphoreType.DMA((N3_COPIES,)),
            pltpu.SemaphoreType.DMA((N3_COPIES,)),
            *RingReturn.scratch(),
        ],
        compiler_params=pltpu.CompilerParams(
            collective_id=2, has_side_effects=True, vmem_limit_bytes=VMEM_LIMIT
        ),
        name="mlp_both_ways",
    )(*operands)


def last_kernel(
    lengths_ref, q_ref, kv_ref, lse_ref, dctx_ref, x_ref, vec_ref, gafter_ref, gaf_ref, ctx_ref, sums_ref, res_ref, outs_ref,
    n1_any, xg_any, wqkv_any, dw_any,
    gin_ref, out_ref, early_ref, mid_ref, late_ref, sums_out,
    dq, dkv, n1, xg, wqkv, gafg, cross, hand, land, mid, fin, dqkv, early, middle, late, own, hats, small_ref, xsum, ysum, zsum, line,
    io_sem, send_sem, recv_sem, *scratch,
):
    p = Place()
    loads = [
        pltpu.make_async_copy(source, target, io_sem.at[i])
        for i, (source, target) in enumerate(
            ((dw_any, early), (n1_any, n1), (wqkv_any, wqkv), (xg_any, xg))
        )
    ]
    for load in loads:
        load.start()
    gafg[rows(p.z * BLOCK, BLOCK), :] = gaf_ref[...]
    greet(
        [p.at(dz=1), p.at(dz=-1), p.at(dz=2), p.at(dx=1), p.at(dx=-1), p.at(dx=2),
         p.at(dy=1), p.at(dy=-1), p.at(dy=2), p.at(flip=True), p.linear(1), p.linear(-1),
         p.at(dy=1, flip=True), p.at(dy=-1, flip=True), p.at(dy=2, flip=True),
         p.beside(-1, -2), p.beside_source(-2, 1)]
    )
    copies = Copies(send_sem, recv_sem)
    scatter = RingScatter(copies, p, scratch[0:3])
    plane = PlaneScatter(copies, p, early, scratch[6:14])
    quick = QuickScatter(copies, p, late, scratch[14:20])
    quick2 = QuickScatter(copies, p, middle, scratch[25:31])
    sibling = p.at(flip=True)
    even = p.c == 0

    def start_of(k):
        return lax.rem(p.z + k, 4) * BLOCK

    def block(k):
        return rows(start_of(k), BLOCK)

    outs = RingReturn(
        copies, p, (outs_ref.at[block(1)], outs_ref.at[block(3)], outs_ref.at[block(2)]) + scratch[3:6]
    )

    def spread_bias(row, value):
        for half in range(2):
            for k in range(4):
                first = (4 * half + k) * 128
                small_ref[row:row + 1, first:first + 128] = value[:, half * 128:(half + 1) * 128]

    order = (2, 1, 3, 0)
    ring = RingGather(copies, p, gafg)
    ring.start()
    outs.send_above()
    outs.send_below()
    outs.send_far()
    heads = AttentionBack(lengths_ref, q_ref, kv_ref, ctx_ref, lse_ref, dctx_ref, scratch[20:25])
    heads.start()

    def cross_over(side):
        ref = dkv.at[rows((1 + 2 * side) * GROUP, GROUP)]
        return copies.put(ref, cross.at[side], sibling)

    heads.add(1, dkv)
    low = cross_over(0)
    heads.add(0, dkv)
    low.wait_recv()
    far, near = {}, {}
    for k in (3, 2, 0, 1):
        i = order.index(k)
        hand[0, block(k)] = (
            dkv[rows(start_of(k), BLOCK), :].astype(F32) + jnp.where(even, 0.0, cross[0, block(k)].astype(F32))
        ).astype(BF)
        if i < 2:
            far[k] = copies.put(hand.at[0, block(k)], mid.at[i], p.at(dy=1))
        else:
            far[k] = copies.put(hand.at[0, block(k)], land.at[0, block(k)], p.linear(-1))
    heads.add(3, dkv)
    high = cross_over(1)
    for load in loads:
        load.wait()
    for i, k in enumerate(order[:2]):
        far[k].wait_recv()
        far[k] = copies.put(mid.at[i], fin.at[i], p.beside(-1, -2))
    ring.below()
    ring.above()
    outs.pass_on()
    heads.add(2, dkv)
    high.wait_recv()
    plane.start()

    def near_sum(k):
        beside = jnp.where(even, cross[0, block(k)].astype(F32), cross[1, block(k)].astype(F32))
        return dkv[rows(2 * GROUP + start_of(k), BLOCK), :].astype(F32) + beside

    for k in order[:2]:
        hand[1, block(k)] = near_sum(k).astype(BF)
        near[k] = copies.put(hand.at[1, block(k)], land.at[1, block(k)], p.linear(-1))
    for k in order[2:]:
        far[k].wait_recv()
        hand[1, block(k)] = (near_sum(k) + land[0, block(k)].astype(F32)).astype(BF)
        near[k] = copies.put(hand.at[1, block(k)], land.at[1, block(k)], p.linear(-1))
    heads.add(4, dkv, own=True)
    heads.finish(dq)
    plane.step1()
    ring.far()
    weight_grad(n1, dq, middle, 0)
    weight_grad(gafg, ctx_ref, middle, 256)
    quick2.start()
    dqkv[:, 0:256] = dq[...]
    small_ref[...] = jnp.zeros_like(small_ref)
    small_ref[8:9, :] = sums_ref[4:5, :]
    spread_bias(9, jnp.sum(dq[...].astype(F32), axis=0, keepdims=True))
    small_ref[1:2, :] = sums_ref[0:1, :]
    small_ref[3:6, :] = sums_ref[1:4, :]
    out_ref[...] = res_ref[...] + outs_ref[block(0), :].astype(F32) + outs.received()

    def keep_hat(k, carry):
        here = rows(k * BLOCK, BLOCK)
        hats[here, :], _ = normalised(xg[here, :].astype(F32))
        return carry

    lax.fori_loop(0, 4, keep_hat, 0)
    quick2.step1()
    plane.step2()

    def own_keys(k):
        near[k].wait_recv()
        value = dkv[rows(4 * GROUP + start_of(k), BLOCK), :].astype(F32) + land[1, block(k)].astype(F32)
        value = value + jnp.where(even, cross[1, block(k)].astype(F32), 0.0)
        if k in order[:2]:
            far[k].wait_recv()
            value = value + fin[order.index(k)].astype(F32)
        dqkv[block(k), 256:768] = value.astype(BF)

    def grad_parts(first, second):
        grad = nt(jnp.concatenate([dqkv[block(first), :], dqkv[block(second), :]], axis=0), wqkv[...])
        return grad[0:BLOCK], grad[BLOCK:2 * BLOCK]

    def tally(k, grad):
        small_ref[0:1, :] += jnp.sum(grad * hats[block(k), :], axis=0, keepdims=True)
        small_ref[2:3, :] += jnp.sum(grad, axis=0, keepdims=True)

    own_keys(2)
    own_keys(1)
    across, above = grad_parts(2, 1)
    scatter.part[2] = across.astype(BF)
    scatter.send_far()
    scatter.part[0] = above.astype(BF)
    tally(2, across)
    tally(1, above)
    own_keys(3)
    own_keys(0)
    weight_grad(n1, dqkv.at[:, 256:768], late, 0)
    quick.start()
    below, here = grad_parts(3, 0)
    scatter.part[1] = below.astype(BF)
    own[...] = here
    tally(3, below)
    tally(0, here)
    spread_bias(10, jnp.sum(dqkv[:, 512:768].astype(F32), axis=0, keepdims=True))

    def lanes(x, width):
        return pl.ds(pl.multiple_of(x * width, 128), width)

    sends = []
    for i, dx in enumerate((1, -1, 2)):
        to = lax.rem(p.x + dx + 4, 4)
        sends.append(copies.put(small_ref.at[:, lanes(to, 256)], xsum.at[i], p.at(dx=dx)))
    scatter.send_above()
    scatter.send_below()
    quick2.step2()
    quick.step1()
    for copy in sends:
        copy.wait_recv()
    line[...] = small_ref[:, lanes(p.x, 256)] + xsum[0] + xsum[1] + xsum[2]
    sends = []
    for dy in (0, 1, -1, 2):
        for flip in (False, True):
            if dy or flip:
                to = lax.rem(p.y + dy + 4, 4) // 2
                sends.append(
                    copies.put(line.at[:, lanes(to, 128)], ysum.at[len(sends)], p.at(dy=dy, flip=flip))
                )
    plane.step3()
    quick.step2()
    hat, scale = normalised(x_ref[...].astype(F32))
    back, _, _ = norm_back(hat, scale, own[...] + scatter.received(), vec_ref[0:1, :])
    gin_ref[...] = gafter_ref[...] + back
    for copy in sends:
        copy.wait_recv()
    total = line[:, lanes(p.y // 2, 128)]
    for i in range(7):
        total = total + ysum[i]
    zsum[3] = total
    sends = [copies.put(zsum.at[3, 0:8], zsum.at[i, 0:8], p.at(dz=dz)) for i, dz in enumerate((1, -1, 2))]
    plane.step4()
    quick2.step3()
    quick.step3()
    plane.step5()
    for copy in sends:
        copy.wait_recv()
    sums_out[0:8] = zsum[3, 0:8] + zsum[0, 0:8] + zsum[1, 0:8] + zsum[2, 0:8]
    sums_out[8:16] = zsum[3, 8:16]
    quick2.step4(mid_ref)
    quick.step4(late_ref)
    plane.step6(early_ref)
    copies.finish()


N5_COPIES = 2 + 4 + 6 + 4 + 4 + 2 + 4 + 18 + 2 * 17 + 3 + 7 + 3


def call_last(*operands):
    shape = jax.ShapeDtypeStruct
    return pl.pallas_call(
        last_kernel,
        out_shape=(
            shape((BLOCK, D), F32),
            shape((BLOCK, D), F32),
            shape((32, 2048), F32),
            shape((32, 512), F32),
            shape((32, 512), F32),
            shape((16, 128), F32),
        ),
        in_specs=[pl.BlockSpec(memory_space=pltpu.SMEM)] + vm(12) + far_memory(4),
        out_specs=tuple(vm(6)),
        scratch_shapes=[
            pltpu.VMEM((GROUP, 256), BF),
            pltpu.VMEM((5 * GROUP, 512), BF),
            pltpu.VMEM((GROUP, D), BF),
            pltpu.VMEM((GROUP, D), BF),
            pltpu.VMEM((D, 768), BF),
            pltpu.VMEM((GROUP, D), BF),
            pltpu.VMEM((2, GROUP, 512), BF),
            pltpu.VMEM((2, GROUP, 512), BF),
            pltpu.VMEM((2, GROUP, 512), BF),
            pltpu.VMEM((2, BLOCK, 512), BF),
            pltpu.VMEM((2, BLOCK, 512), BF),
            pltpu.VMEM((GROUP, 768), BF),
            pltpu.VMEM((D, 2048), BF),
            pltpu.VMEM((D, 512), BF),
            pltpu.VMEM((D, 512), BF),
            pltpu.VMEM((BLOCK, D), F32),
            pltpu.VMEM((GROUP, D), F32),
            pltpu.VMEM((16, D), F32),
            pltpu.VMEM((3, 16, 256), F32),
            pltpu.VMEM((7, 16, 128), F32),
            pltpu.VMEM((4, 16, 128), F32),
            pltpu.VMEM((16, 256), F32),
            pltpu.SemaphoreType.DMA((4,)),
            pltpu.SemaphoreType.DMA((N5_COPIES,)),
            pltpu.SemaphoreType.DMA((N5_COPIES,)),
            *RingScatter.scratch(),
            *RingReturn.scratch(),
            *PlaneScatter.scratch(2048),
            *QuickScatter.scratch(512),
            *AttentionBack.scratch(),
            *QuickScatter.scratch(512),
        ],
        compiler_params=pltpu.CompilerParams(
            collective_id=3, has_side_effects=True, vmem_limit_bytes=VMEM_LIMIT
        ),
        name="project_back",
    )(*operands)


def finish_kernel(
    out_ref, gin_ref, early_ref, mid_ref, late_ref, small_ref,
    out, gin, wqkv, wout, wfc, wproj, bqv, bfc, gains, shifts,
):
    dp, z = lax.axis_index("dp"), lax.axis_index("tensor")
    out[...] = out_ref[...]
    gin[...] = gin_ref[...]
    wqkv[0] = mid_ref[:, 0:256]
    wqkv[1] = late_ref[:, 0:256]
    wqkv[2] = late_ref[:, 256:512]
    wout[...] = mid_ref[:, 256:512]
    wfc[...] = early_ref[:, 0:1024]
    wproj[...] = early_ref[:, 1024:2048]

    def pick(first, offset, width):
        row = lax.broadcasted_iota(jnp.int32, (128, 128), 0)
        lane = lax.broadcasted_iota(jnp.int32, (128, 128), 1)
        chosen = jnp.where(row == lane + lax.rem(offset, 128), 1.0, 0.0).astype(F32)
        return exact(small_ref[first:first + 8, :], chosen)[:, 0:width]

    eight = pick(0, (dp * 4 + z) * 8, 8)
    gains[...] = eight[0:2]
    shifts[...] = eight[2:6]
    bqv[...] = pick(8, dp * 8, 8)[1:3]
    bfc[...] = pick(8, dp * 32, 32)[0:1]


def call_finish(*operands):
    shape = jax.ShapeDtypeStruct
    return pl.pallas_call(
        finish_kernel,
        out_shape=(
            shape((BLOCK, D), F32),
            shape((BLOCK, D), F32),
            shape((3, 32, 256), F32),
            shape((32, 256), F32),
            shape((32, 1024), F32),
            shape((32, 1024), F32),
            shape((2, 8), F32),
            shape((1, 32), F32),
            shape((2, 8), F32),
            shape((4, 8), F32),
        ),
        in_specs=vm(6),
        out_specs=tuple(vm(10)),
        compiler_params=pltpu.CompilerParams(vmem_limit_bytes=VMEM_LIMIT),
        name="lay_out",
    )(*operands)


def on_device(inputs, lengths, w_qkv, w_out, w_fc, w_proj, b_qv, b_fc, gains, shifts, cotangent):
    q, kv, vec, ctx, lse, n1, xg, cotg, wqkv, wo, wfc = call_first(
        lengths, inputs, cotangent, w_qkv[0].transpose(1, 0, 2), w_out[0].T, w_fc[0],
        gains[0], shifts[0], b_qv[0], b_fc,
    )
    gafter, gaf, dctx, sums, res, outs, dw_mlp = call_middle(
        inputs, ctx, vec, w_proj[0].T, wo, wfc, cotg
    )
    gin, out, early, mid, late, small = call_last(
        lengths, q, kv, lse, dctx, inputs, vec, gafter, gaf, ctx, sums, res, outs, n1, xg, wqkv, dw_mlp
    )
    out, gin, g_qkv, g_out, g_fc, g_proj, g_bqv, g_bfc, g_gains, g_shifts = call_finish(
        out, gin, early, mid, late, small
    )
    return (
        out, gin, g_qkv.transpose(1, 0, 2)[None], g_out.T[None], g_fc[None], g_proj.T[None],
        g_bqv[None], g_bfc, g_gains[None], g_shifts[None],
    )


def solution(mesh):
    return jax.shard_map(
        on_device,
        mesh=mesh,
        in_specs=(
            P(("dp", "tensor"), None),
            P(),
            P(None, "dp", None, "tensor"),
            P(None, "tensor", "dp"),
            P(None, "dp", "tensor"),
            P(None, "tensor", "dp"),
            P(None, None, ("tensor", "dp")),
            P(None, ("tensor", "dp")),
            P(None, None, ("dp", "tensor")),
            P(None, None, ("dp", "tensor")),
            P(("dp", "tensor"), None),
        ),
        out_specs=(
            P(("dp", "tensor"), None),
            P(("dp", "tensor"), None),
            P(None, "dp", None, "tensor"),
            P(None, "tensor", "dp"),
            P(None, "dp", "tensor"),
            P(None, "tensor", "dp"),
            P(None, None, ("tensor", "dp")),
            P(None, ("tensor", "dp")),
            P(None, None, ("dp", "tensor")),
            P(None, None, ("dp", "tensor")),
        ),
        check_vma=False,
    )
```
